32 devices in a mesh: seq: 16 (over z, x, core), grp: 2 (over y).
Axes of the slice: x: 2, y: 2, z: 4, core: 2. Of those that a mesh axis runs over, the one named last changes fastest.
Arguments:
- tokens: bfloat16 [2, 8192, 768], P('grp', 'seq'), may hold values from -6 to 6
- w_qkv: bfloat16 [768, 2304], replicated, may hold values from -0.21875 to 0.21875
- w_out: bfloat16 [768, 768], replicated, may hold values from -2.5 to 2.5
- w_in: bfloat16 [768, 3072], replicated, may hold values from -0.21875 to 0.21875
- w_back: bfloat16 [3072, 768], replicated, may hold values from -0.109375 to 0.109375
- ln1_gain: float32 [768], replicated, may hold values from 0.25 to 1.75
- ln1_bias: float32 [768], replicated, may hold values from -3 to 3
- ln2_gain: float32 [768], replicated, may hold values from 0.25 to 1.75
- ln2_bias: float32 [768], replicated, may hold values from -3 to 3
- doc_units: int32 [2, 4], P('grp'), may hold values from 1 to 8, as said below
- tail_pad: int32 [2, 4], P('grp'), may hold values from 0 to 63
- global_ids: int32 [2, 4, 2], P('grp'), may hold values from 0 to 63, as said below
- rand_blocks: int32 [2, 128, 3], P('grp', 'seq'), may hold values from 0 to 127, as said below
- out_grad: bfloat16 [2, 8192, 768], P('grp', 'seq'), may hold values from -6 to 6
Outputs:
- output: bfloat16 [2, 8192, 768], P('grp', 'seq')
- tokens_grad: bfloat16 [2, 8192, 768], P('grp', 'seq')
- qkv_grad: float32 [768, 2304], P('seq')
- out_proj_grad: float32 [768, 768], P('seq')
- in_grad: float32 [768, 3072], P('seq')
- back_grad: float32 [3072, 768], P('seq')
- ln1_gain_grad: float32 [768], P('seq')
- ln1_bias_grad: float32 [768], P('seq')
- ln2_gain_grad: float32 [768], P('seq')
- ln2_bias_grad: float32 [768], P('seq')
The draws below stay inside these ranges and needn't reach their ends.
Inputs may be any that keep to these rules, and one draw needn't show every extreme that they name: `doc_units`: per group the lengths sum to 16; the sequences lie end to end from the group's first block. `tail_pad`: padding tokens of a sequence, all in its last block. `global_ids`: each offset is less than its sequence's number of blocks. `rand_blocks`: entry [g, b, r] is a block of group g in the same sequence as block b.
All inputs are finite; a program needn't handle non-finite values.
Results may differ from the reference program's by a relative error of at most 0.013.
Values may be sent and summed in bfloat16 or wider, within the bound.
No kernel may reach another device: no remote copies, remote signals or barrier semaphores. Data moves between devices by JAX's collectives and lax.ppermute only.
A program may use at most 640 MiB of HBM per device.

```python
import jax
import jax.numpy as jnp
from jax import lax

D = 768
HD = 64
FF = 3072
BLK = 64
NRAND = 3
UNITB = 8
MOSTU = 8
GROUPS = 2
NBLK = 128
GROUP_TOK = 8192
NDOC = 4


def doc_plan(key):
    doc_count = NDOC
    extra_units = NBLK // UNITB - doc_count
    slot_count = doc_count * (MOSTU - 1)

    def one_group(group_key):
        key_long, key_short, key_order = jax.random.split(group_key, 3)
        long_doc = jax.random.randint(key_long, (), 0, doc_count)
        short_doc = (long_doc + 1 + jax.random.randint(key_short, (), 0, doc_count - 1)) % doc_count
        slot_owner = jnp.arange(slot_count) // (MOSTU - 1)
        shuffled = jax.random.permutation(key_order, slot_count)
        tier = jnp.where(slot_owner == long_doc, 0, jnp.where(slot_owner == short_doc, 2, 1))
        priority = tier * slot_count + shuffled
        position = jnp.argsort(jnp.argsort(priority))
        granted = (position < extra_units).astype(jnp.int32).reshape(doc_count, MOSTU - 1).sum(1)
        return (1 + granted).astype(jnp.int32)
    group_keys = jax.vmap(lambda group_index: jax.random.fold_in(key, group_index))(jnp.arange(GROUPS))
    return jax.vmap(one_group)(group_keys)


def doc_bounds(doc_len):
    doc_end = (jnp.cumsum(doc_len) * UNITB).astype(jnp.int32)
    starts = (doc_end - doc_len * UNITB).astype(jnp.int32)
    blocks = jnp.arange(NBLK, dtype=jnp.int32)
    member = ((blocks[:, None] >= starts[None, :]) & (blocks[:, None] < doc_end[None, :])).astype(jnp.int32)
    return (jnp.sum(member * starts[None, :], 1).astype(jnp.int32), jnp.sum(member * doc_end[None, :], 1).astype(jnp.int32))


def draw_doc_units(key, part):
    return doc_plan(key)


def draw_rand_blocks(key, part):
    doc_len = doc_plan(key)
    key = jax.random.fold_in(key, 2)

    def one_group(group_key, lengths):
        seq_begin, finish = doc_bounds(lengths)
        picks = jax.random.randint(group_key, (NBLK, NRAND), seq_begin[:, None], finish[:, None]).astype(jnp.int32)
        picks = picks.at[0, 0].set(0)
        return picks.at[NBLK - 1, 0].set(NBLK - 1)
    group_keys = jax.vmap(lambda group_index: jax.random.fold_in(key, group_index))(jnp.arange(GROUPS))
    return jax.vmap(one_group)(group_keys, doc_len).astype(jnp.int32)


def draw_global_ids(key, part):
    doc_len = doc_plan(key)
    key = jax.random.fold_in(key, 3)

    def one_group(group_key, lengths):
        picks = jax.random.randint(group_key, (NDOC, 2), 0, (lengths * UNITB)[:, None]).astype(jnp.int32)
        longest = jnp.argmax(lengths)
        shortest = jnp.argmin(lengths)
        picks = picks.at[longest, 1].set((lengths[longest] * UNITB - 1).astype(jnp.int32))
        return picks.at[shortest, 0].set(0)
    group_keys = jax.vmap(lambda group_index: jax.random.fold_in(key, group_index))(jnp.arange(GROUPS))
    return jax.vmap(one_group)(group_keys, doc_len).astype(jnp.int32)


def with_ends(values, stream_key, low, top_value):
    extent = values.shape
    place = [jax.random.randint(jax.random.fold_in(stream_key, axis), (), 0, extent[axis]) for axis in range(len(extent))]
    values = values.at[tuple(place)].set(low)
    longest = extent.index(max(extent))
    place[longest] = (place[longest] + 1) % extent[longest]
    return values.at[tuple(place)].set(top_value)


def steps_of(own_key, shape, pieces, least, top_value):
    level, own = 1.0, jax.random.fold_in(own_key, 6)
    for dim, blocks in pieces:
        steps = jnp.exp(jax.random.uniform(jax.random.fold_in(own, dim), (blocks,), jnp.float32, least / len(pieces), top_value / len(pieces)))
        level = level * jnp.repeat(steps, shape[dim] // blocks).reshape([-1 if axis == dim else 1 for axis in range(len(shape))])
    return level


def bell_draw(key, shape, deviation, most, pieces=(), kind=jnp.bfloat16):
    array = jax.random.normal(key, shape, jnp.float32) * deviation
    if len(pieces) > 0:
        array = steps_of(key, shape, pieces, -0.22, 0.18) * array
    return jnp.clip(array, min=-most, max=most).astype(kind)


def setup_inputs(seed: int = 0) -> dict:
    keys = jax.random.split(jax.random.key(seed), 15)
    return {
        "tokens": bell_draw(keys[0], (GROUPS, GROUP_TOK, D), 1.0, 6.0, ((0, 2), (1, 16))),
        "w_qkv": bell_draw(keys[1], (D, 3 * D), D ** -0.5, 0.21875),
        "w_out": bell_draw(keys[2], (D, D), (D // 128) ** -0.5, 2.5),
        "w_in": bell_draw(keys[3], (D, FF), D ** -0.5, 0.21875),
        "w_back": bell_draw(keys[4], (FF, D), FF ** -0.5, 0.109375),
        "ln1_gain": jnp.clip(1.0 + 0.15 * jax.random.normal(keys[5], (D,), jnp.float32), 0.25, 1.75),
        "ln1_bias": bell_draw(keys[6], (D,), 0.3, 3.0, (), jnp.float32),
        "ln2_gain": jnp.clip(1.0 + 0.15 * jax.random.normal(keys[7], (D,), jnp.float32), 0.25, 1.75),
        "ln2_bias": bell_draw(keys[8], (D,), 0.3, 3.0, (), jnp.float32),
        "doc_units": draw_doc_units(jax.random.fold_in(keys[14], 71), 0),
        "tail_pad": with_ends(jax.random.randint(keys[10], (GROUPS, NDOC), 0, BLK), jax.random.fold_in(keys[10], 1), 0, BLK - 1).astype(jnp.int32),
        "global_ids": draw_global_ids(jax.random.fold_in(keys[14], 71), 0),
        "rand_blocks": draw_rand_blocks(jax.random.fold_in(keys[14], 71), 0),
        "out_grad": bell_draw(keys[13], (GROUPS, GROUP_TOK, D), 1.0, 6.0, ((0, 2), (1, 16))),
    }


@jax.custom_vjp
def low(v):
    return lax.optimization_barrier(v.astype(jnp.bfloat16)).astype(jnp.float32)

@jax.custom_vjp
def low_back(v):
    return v

def low_keep(v):
    return (low(v), None)

def low_pass(kept, grad):
    return (grad,)

def back_keep(v):
    return (v, None)

def back_low(kept, grad):
    return (low(grad),)
low.defvjp(low_keep, low_pass)
low_back.defvjp(back_keep, back_low)
ln_eps = 1e-12
highest = lax.Precision.HIGHEST

def layer_norm(values, gain, bias):
    center = values - lax.optimization_barrier(jnp.mean(values, -1, keepdims=True))
    variance = lax.optimization_barrier(jnp.mean(center * center, -1, keepdims=True))
    return center * lax.rsqrt(variance + ln_eps) * gain + bias

def gelu_exact(values):
    return jax.nn.gelu(values, approximate=False)

def block_plan(doc_len, tail_len, global_rel, rand_rows, total_blocks, first_row):
    per_dev = rand_rows.shape[0]
    doc_end = (jnp.cumsum(doc_len) * UNITB).astype(jnp.int32)
    starts = (doc_end - doc_len * UNITB).astype(jnp.int32)
    blocks = jnp.arange(total_blocks, dtype=jnp.int32)
    member = ((blocks[:, None] >= starts[None, :]) & (blocks[:, None] < doc_end[None, :])).astype(jnp.int32)

    def per_block(column):
        return lax.optimization_barrier(jnp.sum(member * column[None, :], 1)).astype(jnp.int32)
    seq_begin = per_block(starts)
    finish = per_block(doc_end)
    padding = per_block(tail_len.astype(jnp.int32))
    glob_one = per_block(global_rel[:, 0].astype(jnp.int32))
    glob_two = per_block(global_rel[:, 1].astype(jnp.int32))
    filled = jnp.where(blocks == finish - 1, BLK - padding, BLK).astype(jnp.int32)
    query_ids = (first_row + jnp.arange(per_dev, dtype=jnp.int32)).astype(jnp.int32)

    def own_rows(values):
        return lax.dynamic_slice_in_dim(values, first_row, per_dev)
    q_begin = own_rows(seq_begin)
    q_finish = own_rows(finish)
    before = jnp.where(query_ids - 1 >= q_begin, query_ids - 1, -1).astype(jnp.int32)
    follow = jnp.where(query_ids + 1 < q_finish, query_ids + 1, -1).astype(jnp.int32)
    fixed_part = jnp.stack([before, query_ids, follow, q_begin + own_rows(glob_one), q_begin + own_rows(glob_two)], 1)
    candidates = jnp.concatenate([fixed_part.astype(jnp.int32), rand_rows.astype(jnp.int32)], 1)
    cand_count = candidates.shape[1]
    equal_ids = candidates[:, :, None] == candidates[:, None, :]
    earlier = jnp.arange(cand_count)[:, None] > jnp.arange(cand_count)[None, :]
    repeat = jnp.any(equal_ids & earlier[None], 2)
    usable = (candidates >= 0) & jnp.logical_not(repeat)
    chosen = jnp.where(usable, candidates, query_ids[:, None]).astype(jnp.int32)
    key_live = (jnp.arange(BLK)[None, None, :] < filled[chosen][:, :, None]) & usable[:, :, None]
    return (chosen, key_live)

def layer_fwd(tok, params, chosen, key_live):
    w_qkv, w_out, w_in, w_back, gain_one, bias_one, gain_two, bias_two = params
    tok_rows, model_width = tok.shape
    head_count = model_width // HD
    total_blocks = tok_rows // BLK
    step_blocks = min(total_blocks, 4096 // BLK)
    laps_count = total_blocks // step_blocks
    cand_count = chosen.shape[1]
    score_scale = HD ** (-0.5)
    input_one = low(layer_norm(tok, gain_one, bias_one))
    projected = jnp.dot(input_one, w_qkv, precision=highest)
    query_rows = low(low_back(projected[:, :model_width]))
    keyval = low(low_back(projected[:, model_width:]))
    kv_blocks = keyval.reshape(total_blocks, BLK, 2, head_count, HD)

    def attend(inputs):
        query_blk, chosen_blk, live_blk = inputs
        gathered = kv_blocks[chosen_blk]
        key_rows = gathered[:, :, :, 0].reshape(step_blocks, cand_count * BLK, head_count, HD)
        val_rows = gathered[:, :, :, 1].reshape(step_blocks, cand_count * BLK, head_count, HD)
        raw_dots = jnp.einsum('bqhd,bkhd->bhqk', query_blk, key_rows, precision=highest)
        live_mask = live_blk.reshape(step_blocks, 1, 1, cand_count * BLK)
        scores = jnp.where(live_mask, low_back(raw_dots) * score_scale, -1e+30)
        row_max = lax.optimization_barrier(jnp.max(scores, -1, keepdims=True))
        expo_scores = jnp.exp(scores - row_max)
        probs = low(expo_scores / lax.optimization_barrier(jnp.sum(expo_scores, -1, keepdims=True)))
        return jnp.einsum('bhqk,bkhd->bqhd', probs, val_rows, precision=highest)
    context = lax.map(jax.checkpoint(attend), (query_rows.reshape(laps_count, step_blocks, BLK, head_count, HD), chosen.reshape(laps_count, step_blocks, cand_count), key_live.reshape(laps_count, step_blocks, cand_count, BLK)))
    context = low(low_back(context.reshape(tok_rows, model_width)))
    hidden = tok + low_back(jnp.dot(context, w_out, precision=highest))
    input_two = low(layer_norm(hidden, gain_two, bias_two))
    pre_act = low_back(jnp.dot(input_two, w_in, precision=highest))
    activ = low(gelu_exact(pre_act))
    return hidden + jnp.dot(activ, w_back, precision=highest)

def reference(tokens, w_qkv, w_out, w_in, w_back, ln1_gain, ln1_bias, ln2_gain, ln2_bias, doc_units, tail_pad, global_ids, rand_blocks, out_grad):
    params = (w_qkv.astype(jnp.float32), w_out.astype(jnp.float32), w_in.astype(jnp.float32), w_back.astype(jnp.float32), ln1_gain.astype(jnp.float32), ln1_bias.astype(jnp.float32), ln2_gain.astype(jnp.float32), ln2_bias.astype(jnp.float32))
    outputs = []
    input_grads = []
    totals = tuple((jnp.zeros(item.shape, jnp.float32) for item in params))
    for group_index in range(GROUPS):
        chosen, key_live = block_plan(doc_units[group_index], tail_pad[group_index], global_ids[group_index], rand_blocks[group_index], NBLK, 0)

        def run_layer(tok, *weights):
            return layer_fwd(tok, weights, chosen, key_live)
        result, pullback = jax.vjp(run_layer, tokens[group_index].astype(jnp.float32), *params)
        grads = pullback(out_grad[group_index].astype(jnp.float32))
        outputs.append(result.astype(jnp.bfloat16))
        input_grads.append(grads[0].astype(jnp.bfloat16))
        totals = tuple((left + right for left, right in zip(totals, grads[1:])))
    return (jnp.stack(outputs), jnp.stack(input_grads), totals[0], totals[1], totals[2], totals[3], totals[4], totals[5], totals[6], totals[7])
```

```python
import functools

import jax
import jax.numpy as jnp
from jax import lax
from jax.experimental import pallas as pl
from jax.experimental.pallas import tpu as pltpu
from jax.sharding import PartitionSpec as P

HD = 64
BLK = 64
UNITB = 8
QUAD = 4
QW = QUAD * HD
ln_eps = 1e-12
bf16 = jnp.bfloat16
f32 = jnp.float32
VMEM_LIMIT = 60 * 1024 * 1024
vmem = functools.partial(pl.BlockSpec, memory_space=pltpu.VMEM)
smem = functools.partial(pl.BlockSpec, memory_space=pltpu.SMEM)
anym = functools.partial(pl.BlockSpec, memory_space=pl.ANY)


def shape(dims, dtype):
    return jax.ShapeDtypeStruct(dims, dtype)


def dot(a, b):
    return lax.dot_general(a, b, (((1,), (0,)), ((), ())), preferred_element_type=f32)


def dot_nt(a, b):
    return lax.dot_general(a, b, (((1,), (1,)), ((), ())), preferred_element_type=f32)


def dot_tn(a, b):
    return lax.dot_general(a, b, (((0,), (0,)), ((), ())), preferred_element_type=f32)


def norm_stats(values):
    center = values - jnp.mean(values, -1, keepdims=True)
    inv_std = lax.rsqrt(jnp.mean(center * center, -1, keepdims=True) + ln_eps)
    return center * inv_std, inv_std


def block_plan(doc_len, tail_len, global_rel, rand_rows, first_row):
    per_dev = rand_rows.shape[0]
    doc_end = jnp.cumsum(doc_len) * UNITB
    starts = doc_end - doc_len * UNITB
    mine = ((first_row >= starts) & (first_row < doc_end)).astype(jnp.int32)
    begin = jnp.sum(mine * starts)
    finish = jnp.sum(mine * doc_end)
    padding = jnp.sum(mine * tail_len)
    glob_one = begin + jnp.sum(mine * global_rel[:, 0])
    glob_two = begin + jnp.sum(mine * global_rel[:, 1])
    rows = first_row + jnp.arange(per_dev, dtype=jnp.int32)
    before = jnp.where(rows - 1 >= begin, rows - 1, -1)
    follow = jnp.where(rows + 1 < finish, rows + 1, -1)
    whole = jnp.zeros_like(rows)
    candidates = jnp.concatenate(
        [jnp.stack([before, rows, follow, whole + glob_one, whole + glob_two], 1), rand_rows], 1
    )
    count = candidates.shape[1]
    equal = candidates[:, :, None] == candidates[:, None, :]
    earlier = jnp.arange(count)[:, None] > jnp.arange(count)[None, :]
    usable = (candidates >= 0) & jnp.logical_not(jnp.any(equal & earlier[None], 2))
    filled = jnp.where(candidates == finish - 1, BLK - padding, BLK)
    live = jnp.where(usable, filled, 0).astype(jnp.int32)
    halo = jnp.stack(
        [
            jnp.where(first_row - 1 >= begin, first_row - 1, first_row),
            jnp.where(first_row + per_dev < finish, first_row + per_dev, first_row),
            glob_one,
            glob_two,
        ]
    )
    slots = jnp.concatenate([halo, rand_rows.reshape(-1)]).astype(jnp.int32)
    return live.reshape(-1), slots


def head_masks(rows):
    lane = lax.broadcasted_iota(jnp.int32, (rows, QW), 1) // HD
    return [lane == h for h in range(QUAD)]


def spread(values, masks):
    zero = jnp.zeros_like(values)
    return jnp.concatenate([jnp.where(m, values, zero) for m in masks], 0)


def collect(values, masks):
    out = values[:BLK]
    for h in range(1, QUAD):
        out = jnp.where(masks[h], values[h * BLK : (h + 1) * BLK], out)
    return out


def key_rows(ext, slots, i, cols):
    return jnp.concatenate(
        [
            ext[pl.ds(pl.multiple_of(i * BLK, BLK), 3 * BLK), cols],
            slots[2 * BLK : 4 * BLK, cols],
            slots[pl.ds(pl.multiple_of((4 + 3 * i) * BLK, BLK), 3 * BLK), cols],
        ],
        0,
    )


def masked(scores, live, i, cand):
    row = lax.broadcasted_iota(jnp.int32, (BLK, QW), 0)
    return jnp.concatenate(
        [
            jnp.where(row < live[i * cand + c], scores[c * BLK : (c + 1) * BLK], -1e30)
            for c in range(cand)
        ],
        0,
    )


def fill_ext(ext, own, slots):
    rows = own.shape[0]
    ext[0:BLK, :] = slots[0:BLK, :]
    ext[BLK : BLK + rows, :] = own[...]
    ext[BLK + rows : 2 * BLK + rows, :] = slots[BLK : 2 * BLK, :]


def forward_kernel(
    slot_ids, live, window, query, own_kv, w_qkv, gain, bias,
    context, lse, slot_norm, slot_kv,
    slot_tok, ext, sems,
):
    count = slot_tok.shape[0]
    width = query.shape[1]
    nblk = query.shape[0] // BLK
    cand = live.shape[0] // nblk

    def fetch(s):
        return pltpu.make_async_copy(window.at[slot_ids[s]], slot_tok.at[s], sems.at[s])

    for s in range(count):
        fetch(s).start()
    group = 4

    def project(step, _):
        for k in range(group):
            fetch(step * group + k).wait()
        rows = pl.ds(pl.multiple_of(step * group * BLK, group * BLK), group * BLK)
        tok = slot_tok[pl.ds(step * group, group)].reshape(group * BLK, width).astype(f32)
        normed, _ = norm_stats(tok)
        low = (normed * gain[...] + bias[...]).astype(bf16)
        slot_norm[rows, :] = low
        slot_kv[rows, :] = dot(low, w_qkv[:, width:]).astype(bf16)
        return 0

    lax.fori_loop(0, count // group, project, 0)
    fill_ext(ext, own_kv, slot_kv)
    masks = head_masks(BLK)

    def attend(i, _):
        qrows = pl.ds(pl.multiple_of(i * BLK, BLK), BLK)
        for quad in range(width // QW):
            cols = pl.ds(quad * QW, QW)
            vcols = pl.ds(width + quad * QW, QW)
            keys = key_rows(ext, slot_kv, i, cols)
            vals = key_rows(ext, slot_kv, i, vcols)
            scores = masked(dot_nt(keys, spread(query[qrows, cols], masks)), live, i, cand)
            top = jnp.max(scores, 0, keepdims=True)
            expo = jnp.exp(scores - top)
            total = jnp.sum(expo, 0, keepdims=True)
            probs = (expo * (1.0 / total)).astype(bf16)
            lse[i, pl.ds(quad, 1), :] = top + jnp.log(total)
            context[qrows, cols] = collect(dot_tn(probs, vals), masks).astype(bf16)
        return 0

    lax.fori_loop(0, nblk, attend, 0)


def backward_kernel(
    live, query, own_kv, slot_kv, lse, d_context, own_norm, slot_norm, w_qkv,
    d_own_norm, d_slot_norm, qkv_part,
    ext, d_ext, d_glob, d_slot, d_query,
):
    rows_own, width = query.shape
    nblk = rows_own // BLK
    cand = live.shape[0] // nblk
    fill_ext(ext, own_kv, slot_kv)
    d_ext[...] = jnp.zeros_like(d_ext)
    d_glob[...] = jnp.zeros_like(d_glob)
    masks = head_masks(BLK)

    def attend(i, _):
        qrows = pl.ds(pl.multiple_of(i * BLK, BLK), BLK)
        near = pl.ds(pl.multiple_of(i * BLK, BLK), 3 * BLK)
        far = pl.ds(pl.multiple_of((4 + 3 * i) * BLK, BLK), 3 * BLK)
        for quad in range(width // QW):
            cols = pl.ds(quad * QW, QW)
            vcols = pl.ds(width + quad * QW, QW)
            keys = key_rows(ext, slot_kv, i, cols)
            vals = key_rows(ext, slot_kv, i, vcols)
            spread_q = spread(query[qrows, cols], masks)
            spread_d = spread(d_context[qrows, cols], masks)
            scores = masked(dot_nt(keys, spread_q), live, i, cand)
            probs = jnp.exp(scores - lse[i, pl.ds(quad, 1), :])
            d_probs = dot_nt(vals, spread_d)
            delta = jnp.sum(d_probs * probs, 0, keepdims=True)
            d_scores = (probs * (d_probs - delta)).astype(bf16)
            d_keys = dot(d_scores, spread_q)
            d_vals = dot(probs.astype(bf16), spread_d)
            d_query[qrows, cols] = (collect(dot_tn(d_scores, keys), masks) * HD**-0.5).astype(bf16)
            for grads, where in ((d_keys, cols), (d_vals, vcols)):
                d_ext[near, where] += grads[: 3 * BLK]
                d_glob[:, where] += grads[3 * BLK : 5 * BLK]
                d_slot[far, where] = grads[5 * BLK :].astype(bf16)
        return 0

    lax.fori_loop(0, nblk, attend, 0)
    d_slot[0:BLK, :] = d_ext[0:BLK, :].astype(bf16)
    d_slot[BLK : 2 * BLK, :] = d_ext[BLK + rows_own :, :].astype(bf16)
    d_slot[2 * BLK : 4 * BLK, :] = d_glob[...].astype(bf16)
    ext[0:rows_own, :] = d_ext[BLK : BLK + rows_own, :].astype(bf16)
    d_own = ext[0:rows_own, :]
    d_own_norm[...] = dot_nt(d_query[...], w_qkv[:, :width]) + dot_nt(d_own, w_qkv[:, width:])
    step_rows = 4 * BLK

    def back(step, _):
        rows = pl.ds(pl.multiple_of(step * step_rows, step_rows), step_rows)
        d_slot_norm[rows, :] = dot_nt(d_slot[rows, :], w_qkv[:, width:])
        return 0

    lax.fori_loop(0, d_slot.shape[0] // step_rows, back, 0)
    dests, parts, share, _ = qkv_part.shape
    qkv_part[:, 0] = dot_tn(own_norm[...], d_query[...]).astype(bf16).reshape(dests, share, width)
    for part in range(1, parts):
        cols = pl.ds((part - 1) * width, width)
        grads = dot_tn(own_norm[...], d_own[:, (part - 1) * width : part * width])
        grads += dot_tn(slot_norm[...], d_slot[:, cols])
        qkv_part[:, part] = grads.astype(bf16).reshape(dests, share, width)


def gelu_both(x):
    half_erf = 0.5 * lax.erf(x * 0.7071067811865476)
    cdf = 0.5 + half_erf
    density = jnp.exp(-0.5 * x * x) * 0.3989422804014327
    return x * cdf, cdf + x * density


def middle_kernel(
    tokens, context, grad_out, w_out, gain, bias, w_in, w_back,
    output, d_hidden, d_context, in_part, back_part, out_part, gain_part, bias_part,
    hidden, norm_low, norm_t, out_sum, d_norm, act, slope,
):
    step, steps = pl.program_id(0), pl.num_programs(0)
    rows, width = hidden.shape
    tile = 128

    @pl.when(step == 0)
    def _():
        for r in range(0, rows, tile):
            t = slice(r, r + tile)
            value = tokens[t, :].astype(f32) + dot(context[t, :], w_out[...])
            hidden[t, :] = value
            normed, _ = norm_stats(value)
            norm_low[t, :] = (normed * gain[...] + bias[...]).astype(bf16)
        norm_t[...] = norm_low[...].T
        out_sum[...] = jnp.zeros_like(out_sum)
        d_norm[...] = jnp.zeros_like(d_norm)

    for r in range(0, rows, tile):
        t = slice(r, r + tile)
        value, grad = gelu_both(dot(norm_low[t, :], w_in[...]))
        low = value.astype(bf16)
        act[t, :] = low
        out_sum[t, :] += dot(low, w_back[...])
        d_low = (dot_nt(grad_out[t, :], w_back[...]) * grad).astype(bf16)
        slope[t, :] = d_low
        d_norm[t, :] += dot_nt(d_low, w_in[...])
    chunk = act.shape[1]
    back_part[...] = dot_tn(act[...], grad_out[...]).astype(bf16).reshape(back_part.shape)
    in_part[...] = dot(norm_t[...], slope[...]).astype(bf16).reshape(in_part.shape)

    @pl.when(step == steps - 1)
    def _():
        for r in range(0, rows, tile):
            t = slice(r, r + tile)
            value = hidden[t, :]
            output[t, :] = (value + out_sum[t, :]).astype(bf16)
            normed, inv = norm_stats(value)
            grad = d_norm[t, :]
            part_gain = jnp.sum(grad * normed, 0, keepdims=True)
            part_bias = jnp.sum(grad, 0, keepdims=True)
            if r == 0:
                gain_part[...] = part_gain
                bias_part[...] = part_bias
            else:
                gain_part[...] += part_gain
                bias_part[...] += part_bias
            hat = grad * gain[...]
            mean_hat = jnp.mean(hat, -1, keepdims=True)
            mean_dot = jnp.mean(hat * normed, -1, keepdims=True)
            total = grad_out[t, :].astype(f32) + inv * (hat - mean_hat - normed * mean_dot)
            d_hidden[t, :] = total
            low = total.astype(bf16)
            norm_low[t, :] = low
            d_context[t, :] = dot_nt(low, w_out[...]).astype(bf16)
        out_part[...] = dot_tn(context[...], norm_low[...]).astype(bf16)


def body(
    tokens, w_qkv, w_out, w_in, w_back, ln1_gain, ln1_bias, ln2_gain, ln2_bias,
    doc_units, tail_pad, global_ids, rand_blocks, out_grad,
):
    tok = tokens[0]
    grad_out = out_grad[0]
    rows, width = tok.shape
    ff = w_in.shape[1]
    per_dev = rows // BLK
    shards = lax.axis_size("seq")
    share = width // 16 if shards == 16 else width // shards
    first_row = lax.axis_index("seq") * per_dev
    live, slots = block_plan(doc_units[0], tail_pad[0], global_ids[0], rand_blocks[0], first_row)
    count = slots.shape[0]
    gain1, bias1 = ln1_gain[None], ln1_bias[None]
    gain2, bias2 = ln2_gain[None], ln2_bias[None]

    window = lax.all_gather(tok, "seq").reshape(shards * per_dev, BLK, width)

    normed_one, inv_one = norm_stats(tok.astype(f32))
    own_norm = (normed_one * ln1_gain + ln1_bias).astype(bf16)
    projected = jnp.dot(own_norm, w_qkv, preferred_element_type=f32)
    query = (projected[:, :width] * HD**-0.5).astype(bf16)
    own_kv = projected[:, width:].astype(bf16)

    params = pltpu.CompilerParams(vmem_limit_bytes=VMEM_LIMIT)
    quads = width // QW
    context, lse, slot_norm, slot_kv = pl.pallas_call(
        forward_kernel,
        out_shape=[
            shape((rows, width), bf16),
            shape((per_dev, quads, QW), f32),
            shape((count * BLK, width), bf16),
            shape((count * BLK, 2 * width), bf16),
        ],
        in_specs=[smem(), smem(), anym()] + [vmem()] * 5,
        out_specs=[vmem()] * 4,
        scratch_shapes=[
            pltpu.VMEM((count, BLK, width), bf16),
            pltpu.VMEM((rows + 2 * BLK, 2 * width), bf16),
            pltpu.SemaphoreType.DMA((count,)),
        ],
        compiler_params=params,
        name="attend_forward",
    )(slots, live, window, query, own_kv, w_qkv, gain1, bias1)

    chunk = width
    steps = ff // chunk
    per_share = ff // shards
    dests = chunk // per_share
    const = lambda *dims: pl.BlockSpec(dims, lambda s: (0,) * len(dims))
    output, d_hidden, d_context, in_part, back_part, out_part, gain_two, bias_two = pl.pallas_call(
        middle_kernel,
        grid=(steps,),
        in_specs=[
            const(rows, width), const(rows, width), const(rows, width), const(width, width),
            const(1, width), const(1, width),
            pl.BlockSpec((width, chunk), lambda s: (0, s)),
            pl.BlockSpec((chunk, width), lambda s: (s, 0)),
        ],
        out_specs=[
            const(rows, width), const(rows, width), const(rows, width),
            pl.BlockSpec((width, chunk), lambda s: (0, s)),
            pl.BlockSpec((chunk, width), lambda s: (s, 0)),
            const(width, width), const(1, width), const(1, width),
        ],
        out_shape=[
            shape((rows, width), bf16), shape((rows, width), f32), shape((rows, width), bf16),
            shape((width, ff), bf16), shape((ff, width), bf16), shape((width, width), bf16),
            shape((1, width), f32), shape((1, width), f32),
        ],
        scratch_shapes=[
            pltpu.VMEM((rows, width), f32), pltpu.VMEM((rows, width), bf16),
            pltpu.VMEM((width, rows), bf16), pltpu.VMEM((rows, width), f32),
            pltpu.VMEM((rows, width), f32), pltpu.VMEM((rows, chunk), bf16),
            pltpu.VMEM((rows, chunk), bf16),
        ],
        compiler_params=params,
        name="middle",
    )(tok, context, grad_out, w_out, gain2, bias2, w_in, w_back)

    parts = w_qkv.shape[1] // width
    d_own_norm, d_slot_norm, qkv_part = pl.pallas_call(
        backward_kernel,
        out_shape=[
            shape((rows, width), f32),
            shape((count * BLK, width), f32),
            shape((1, parts, width, width), bf16),
        ],
        in_specs=[smem()] + [vmem()] * 8,
        out_specs=[vmem()] * 3,
        scratch_shapes=[
            pltpu.VMEM((rows + 2 * BLK, 2 * width), bf16),
            pltpu.VMEM((rows + 2 * BLK, 2 * width), f32),
            pltpu.VMEM((2 * BLK, 2 * width), f32),
            pltpu.VMEM((count * BLK, 2 * width), bf16),
            pltpu.VMEM((rows, width), bf16),
        ],
        compiler_params=params,
        name="attend_backward",
    )(live, query, own_kv, slot_kv, lse, d_context, own_norm, slot_norm, w_qkv)

    spread_grads = jnp.zeros((shards * per_dev, BLK, width), f32)
    spread_grads = spread_grads.at[slots].add(d_slot_norm.reshape(count, BLK, width))
    others = lax.psum_scatter(
        spread_grads.astype(bf16).reshape(shards * rows, width), "seq", scatter_dimension=0, tiled=True
    )
    d_norm1 = d_own_norm + others.astype(f32)
    grad_hat = d_norm1 * ln1_gain
    d_first = inv_one * (
        grad_hat
        - jnp.mean(grad_hat, -1, keepdims=True)
        - normed_one * jnp.mean(grad_hat * normed_one, -1, keepdims=True)
    )
    tokens_grad = (d_hidden + d_first).astype(bf16)
    gain_one = jnp.sum(d_norm1 * normed_one, 0)
    bias_one = jnp.sum(d_norm1, 0)

    def reduce(part):
        mine = lax.psum_scatter(part, "seq", scatter_dimension=0, tiled=True)
        return lax.psum(mine, "grp").astype(f32)

    qkv_part = jnp.moveaxis(qkv_part[0], 0, 1).reshape(width, parts * width)
    vectors = jnp.stack([gain_one, bias_one, gain_two[0], bias_two[0]], 1)
    vectors = lax.psum(lax.psum_scatter(vectors, "seq", scatter_dimension=0, tiled=True), "grp")
    return (
        output[None],
        tokens_grad[None],
        reduce(qkv_part),
        reduce(out_part),
        reduce(in_part),
        reduce(back_part),
        vectors[:, 0],
        vectors[:, 1],
        vectors[:, 2],
        vectors[:, 3],
    )


def solution(mesh):
    in_specs = (
        P("grp", "seq", None),
        P(),
        P(),
        P(),
        P(),
        P(),
        P(),
        P(),
        P(),
        P("grp", None),
        P("grp", None),
        P("grp", None, None),
        P("grp", "seq", None),
        P("grp", "seq", None),
    )
    out_specs = (
        P("grp", "seq", None),
        P("grp", "seq", None),
        P("seq", None),
        P("seq", None),
        P("seq", None),
        P("seq", None),
        P("seq"),
        P("seq"),
        P("seq"),
        P("seq"),
    )
    return jax.shard_map(body, mesh=mesh, in_specs=in_specs, out_specs=out_specs, check_vma=False)
```

```python
import functools

import jax
import jax.numpy as jnp
from jax import lax
from jax.experimental import pallas as pl
from jax.experimental.pallas import tpu as pltpu
from jax.sharding import PartitionSpec as P

HD = 64
BLK = 64
UNITB = 8
QUAD = 4
QW = QUAD * HD
ln_eps = 1e-12
bf16 = jnp.bfloat16
f32 = jnp.float32
VMEM_LIMIT = 60 * 1024 * 1024
COST = pl.CostEstimate(flops=40_000_000_000, bytes_accessed=1, transcendentals=0)
vmem = functools.partial(pl.BlockSpec, memory_space=pltpu.VMEM)
smem = functools.partial(pl.BlockSpec, memory_space=pltpu.SMEM)
anym = functools.partial(pl.BlockSpec, memory_space=pl.ANY)


def shape(dims, dtype):
    return jax.ShapeDtypeStruct(dims, dtype)


def dot(a, b):
    return lax.dot_general(a, b, (((1,), (0,)), ((), ())), preferred_element_type=f32)


def dot_nt(a, b):
    return lax.dot_general(a, b, (((1,), (1,)), ((), ())), preferred_element_type=f32)


def dot_tn(a, b):
    return lax.dot_general(a, b, (((0,), (0,)), ((), ())), preferred_element_type=f32)


def norm_stats(values):
    center = values - jnp.mean(values, -1, keepdims=True)
    inv_std = lax.rsqrt(jnp.mean(center * center, -1, keepdims=True) + ln_eps)
    return center * inv_std, inv_std


def block_plan(doc_len, tail_len, global_rel, rand_rows, first_row):
    per_dev = rand_rows.shape[0]
    doc_end = jnp.cumsum(doc_len) * UNITB
    starts = doc_end - doc_len * UNITB
    mine = ((first_row >= starts) & (first_row < doc_end)).astype(jnp.int32)
    begin = jnp.sum(mine * starts)
    finish = jnp.sum(mine * doc_end)
    padding = jnp.sum(mine * tail_len)
    glob_one = begin + jnp.sum(mine * global_rel[:, 0])
    glob_two = begin + jnp.sum(mine * global_rel[:, 1])
    rows = first_row + jnp.arange(per_dev, dtype=jnp.int32)
    before = jnp.where(rows - 1 >= begin, rows - 1, -1)
    follow = jnp.where(rows + 1 < finish, rows + 1, -1)
    whole = jnp.zeros_like(rows)
    candidates = jnp.concatenate(
        [jnp.stack([before, rows, follow, whole + glob_one, whole + glob_two], 1), rand_rows], 1
    )
    count = candidates.shape[1]
    equal = candidates[:, :, None] == candidates[:, None, :]
    earlier = jnp.arange(count)[:, None] > jnp.arange(count)[None, :]
    usable = (candidates >= 0) & jnp.logical_not(jnp.any(equal & earlier[None], 2))
    filled = jnp.where(candidates == finish - 1, BLK - padding, BLK)
    live = jnp.where(usable, filled, 0).astype(jnp.int32)
    halo = jnp.stack(
        [
            jnp.where(first_row - 1 >= begin, first_row - 1, first_row),
            jnp.where(first_row + per_dev < finish, first_row + per_dev, first_row),
            glob_one,
            glob_two,
        ]
    )
    slots = jnp.concatenate([halo, rand_rows.reshape(-1)]).astype(jnp.int32)
    return live.reshape(-1), slots


def head_masks(rows):
    lane = lax.broadcasted_iota(jnp.int32, (rows, QW), 1) // HD
    return [lane == h for h in range(QUAD)]


def spread(values, masks):
    zero = jnp.zeros_like(values)
    return jnp.concatenate([jnp.where(m, values, zero) for m in masks], 0)


def collect(values, masks):
    out = values[:BLK]
    for h in range(1, QUAD):
        out = jnp.where(masks[h], values[h * BLK : (h + 1) * BLK], out)
    return out


def key_rows(ext, slots, i, cols):
    return jnp.concatenate(
        [
            ext[pl.ds(pl.multiple_of(i * BLK, BLK), 3 * BLK), cols],
            slots[2 * BLK : 4 * BLK, cols],
            slots[pl.ds(pl.multiple_of((4 + 3 * i) * BLK, BLK), 3 * BLK), cols],
        ],
        0,
    )


def masked(scores, live, i, cand):
    row = lax.broadcasted_iota(jnp.int32, (BLK, QW), 0)
    return jnp.concatenate(
        [
            jnp.where(row < live[i * cand + c], scores[c * BLK : (c + 1) * BLK], -1e30)
            for c in range(cand)
        ],
        0,
    )


def fill_ext(ext, own, slots):
    rows = own.shape[0]
    ext[0:BLK, :] = slots[0:BLK, :]
    ext[BLK : BLK + rows, :] = own[...]
    ext[BLK + rows : 2 * BLK + rows, :] = slots[BLK : 2 * BLK, :]


def forward_kernel(num_pieces, codes, live, *refs):
    pieces, refs = refs[:num_pieces], refs[num_pieces:]
    query, own_kv, w_qkv, gain, bias = refs[:5]
    context, lse, slot_norm, slot_hat, slot_kv, slot_tok, ext, sems = refs[5:]
    count = slot_tok.shape[0]
    per_piece = pieces[0].shape[0]
    width = query.shape[1]
    nblk = query.shape[0] // BLK
    cand = live.shape[0] // nblk

    def fetch(s, piece, block):
        return pltpu.make_async_copy(piece.at[block], slot_tok.at[s], sems.at[s])

    def start(s, _):
        which, block = codes[s] // per_piece, codes[s] % per_piece
        for k, piece in enumerate(pieces):

            @pl.when(which == k)
            def _():
                fetch(s, piece, block).start()

        return 0

    lax.fori_loop(0, count, start, 0)
    group = 4

    def project(step, _):
        for k in range(group):
            fetch(step * group + k, pieces[0], 0).wait()
        rows = pl.ds(pl.multiple_of(step * group * BLK, group * BLK), group * BLK)
        tok = slot_tok[pl.ds(step * group, group)].reshape(group * BLK, width).astype(f32)
        normed, _ = norm_stats(tok)
        slot_hat[rows, :] = normed.astype(bf16)
        low = (normed * gain[...] + bias[...]).astype(bf16)
        slot_norm[rows, :] = low
        slot_kv[rows, :] = dot(low, w_qkv[:, width:]).astype(bf16)
        return 0

    lax.fori_loop(0, count // group, project, 0)
    fill_ext(ext, own_kv, slot_kv)
    masks = head_masks(BLK)

    def attend(i, _):
        qrows = pl.ds(pl.multiple_of(i * BLK, BLK), BLK)
        for quad in range(width // QW):
            cols = pl.ds(quad * QW, QW)
            vcols = pl.ds(width + quad * QW, QW)
            keys = key_rows(ext, slot_kv, i, cols)
            vals = key_rows(ext, slot_kv, i, vcols)
            scores = masked(dot_nt(keys, spread(query[qrows, cols], masks)), live, i, cand)
            top = jnp.max(scores, 0, keepdims=True)
            expo = jnp.exp(scores - top)
            total = jnp.sum(expo, 0, keepdims=True)
            probs = (expo * (1.0 / total)).astype(bf16)
            lse[i, pl.ds(quad, 1), :] = top + jnp.log(total)
            context[qrows, cols] = collect(dot_tn(probs, vals), masks).astype(bf16)
        return 0

    lax.fori_loop(0, nblk, attend, 0)


def backward_kernel(parts, live, lse, *refs):
    ins, refs = refs[: 6 * len(parts)], refs[6 * len(parts) :]
    outs, (ext, d_ext, d_glob) = refs[: 3 * len(parts)], refs[3 * len(parts) :]
    rows_own = ins[0].shape[0]
    nblk = rows_own // BLK
    cand = live.shape[0] // nblk
    d_ext[...] = jnp.zeros_like(d_ext)
    d_glob[...] = jnp.zeros_like(d_glob)
    masks = head_masks(BLK)
    for n in range(len(parts)):
        for kv in range(2):
            own, slots = ins[6 * n + 2 + kv], ins[6 * n + 4 + kv]
            fill_ext(ext.at[2 * n + kv], own, slots)

    def attend(i, _):
        qrows = pl.ds(pl.multiple_of(i * BLK, BLK), BLK)
        near = pl.ds(pl.multiple_of(i * BLK, BLK), 3 * BLK)
        far = pl.ds(pl.multiple_of((4 + 3 * i) * BLK, BLK), 3 * BLK)
        every = pl.ds(0, QW)
        for n, part in enumerate(parts):
            query, d_context, _, _, slot_k, slot_v = ins[6 * n : 6 * n + 6]
            d_query, _, d_slot = outs[3 * n : 3 * n + 3]
            keys = key_rows(ext.at[2 * n], slot_k, i, every)
            vals = key_rows(ext.at[2 * n + 1], slot_v, i, every)
            spread_q = spread(query[qrows, :], masks)
            spread_d = spread(d_context[qrows, :], masks)
            scores = masked(dot_nt(keys, spread_q), live, i, cand)
            probs = jnp.exp(scores - lse[i, pl.ds(part, 1), :])
            d_probs = dot_nt(vals, spread_d)
            delta = jnp.sum(d_probs * probs, 0, keepdims=True)
            d_scores = (probs * (d_probs - delta)).astype(bf16)
            d_keys = dot(d_scores, spread_q)
            d_vals = dot(probs.astype(bf16), spread_d)
            d_query[qrows, :] = (collect(dot_tn(d_scores, keys), masks) * HD**-0.5).astype(bf16)
            for kv, grads in enumerate((d_keys, d_vals)):
                d_ext[2 * n + kv, near, :] += grads[: 3 * BLK]
                d_glob[2 * n + kv] += grads[3 * BLK : 5 * BLK]
                d_slot[far, kv * QW : (kv + 1) * QW] = grads[5 * BLK :].astype(bf16)
        return 0

    lax.fori_loop(0, nblk, attend, 0)
    for n in range(len(parts)):
        _, d_own, d_slot = outs[3 * n : 3 * n + 3]
        for kv in range(2):
            cols = slice(kv * QW, (kv + 1) * QW)
            d_slot[0:BLK, cols] = d_ext[2 * n + kv, 0:BLK, :].astype(bf16)
            d_slot[BLK : 2 * BLK, cols] = d_ext[2 * n + kv, BLK + rows_own :, :].astype(bf16)
            d_slot[2 * BLK : 4 * BLK, cols] = d_glob[2 * n + kv].astype(bf16)
            d_own[:, cols] = d_ext[2 * n + kv, BLK : BLK + rows_own, :].astype(bf16)


def joined(refs, rows):
    return jnp.concatenate(
        [r[rows, kv * QW : (kv + 1) * QW] for kv in range(2) for r in refs], 1
    )


def project_back_kernel(quads, w_qkv, own_hat, slot_hat, *refs):
    ins, (d_own_norm, d_slot_norm, gain_part, bias_part) = refs[:-4], refs[-4:]
    d_query, d_own, d_slot = ins[0::3], ins[1::3], ins[2::3]
    rows_own, width = d_own_norm.shape
    step_rows = 4 * BLK

    def add(grads, hat, first):
        gain = jnp.sum(grads * hat.astype(f32), 0, keepdims=True)
        bias = jnp.sum(grads, 0, keepdims=True)
        if first:
            gain_part[...], bias_part[...] = gain, bias
        else:
            gain_part[...] += gain
            bias_part[...] += bias

    for r in range(0, rows_own, step_rows):
        rows = slice(r, r + step_rows)
        grads = dot_nt(jnp.concatenate([d[rows, :] for d in d_query], 1), w_qkv[:, :width])
        grads += dot_nt(joined(d_own, rows), w_qkv[:, width:])
        d_own_norm[rows, :] = grads
        add(grads, own_hat[rows, :], r == 0)

    def back(step, _):
        rows = pl.ds(pl.multiple_of(step * step_rows, step_rows), step_rows)
        grads = dot_nt(joined(d_slot, rows), w_qkv[:, width:])
        d_slot_norm[rows, :] = grads.astype(bf16)
        add(grads, slot_hat[rows, :], False)
        return 0

    lax.fori_loop(0, d_slot_norm.shape[0] // step_rows, back, 0)


def halves_to_dests(coords, grads, half, keep, send, slot, side):
    share = grads.shape[0] // 16
    for zr in range(4):
        for xr in range(2):
            for cr, target in ((0, keep), (1, send)):
                dest = (zr ^ coords[0]) * 4 + (xr ^ coords[1]) * 2 + (cr ^ coords[2])
                rows = pl.ds(pl.multiple_of(dest * share, 16), share)
                target[side, xr, zr, slot * share : (slot + 1) * share, :] = grads[
                    rows, half * 384 : (half + 1) * 384
                ]


def qkv_grad_kernel(num_out, coords, gain1, bias1, gain2, bias2, own_norm, slot_norm, *refs):
    ins, outs, tmp = refs[: -1 - num_out], refs[-1 - num_out : -1], refs[-1]
    d_query, d_own, d_slot = ins[0::3], ins[1::3], ins[2::3]
    width = own_norm.shape[1]
    whole = slice(None)
    for part in range(3):
        if part == 0:
            grads = dot_tn(own_norm[...], jnp.concatenate([d[...] for d in d_query], 1))
        else:
            cols = slice((part - 1) * QW, part * QW)
            grads = dot_tn(own_norm[...], jnp.concatenate([d[:, cols] for d in d_own], 1))
            grads += dot_tn(slot_norm[...], jnp.concatenate([d[:, cols] for d in d_slot], 1))
        if num_out == 1:
            outs[0][:, part * width : (part + 1) * width] = grads.astype(bf16)
        else:
            tmp[...] = grads.astype(bf16)
            for half in range(2):
                piece = part * 2 + half
                side = (piece // 3) ^ coords[3]
                halves_to_dests(coords, tmp, half, outs[0], outs[1], piece % 3, side)
    if num_out == 2:
        half = width // 2
        lines = [v[:, h * half : (h + 1) * half] for v in (gain1, bias1, gain2, bias2) for h in (0, 1)]
        block = jnp.concatenate(lines + [jnp.zeros((8, half), f32)], 0).astype(bf16)
        rows = slice(outs[0].shape[3] - 16, outs[0].shape[3])
        for out in outs:
            for side in range(2):
                for xr in range(2):
                    for zr in range(4):
                        out[side, xr, zr, rows, :] = block


def gelu_both(x):
    half_erf = 0.5 * lax.erf(x * 0.7071067811865476)
    cdf = 0.5 + half_erf
    density = jnp.exp(-0.5 * x * x) * 0.3989422804014327
    return x * cdf, cdf + x * density


def middle_kernel(
    num_grads, coords, tokens, context, grad_out, w_out, gain, bias, w_in, w_back,
    output, d_hidden, d_context, gain_part, bias_part, *refs,
):
    grad_refs, refs = refs[:num_grads], refs[num_grads:]
    hidden, norm_low, norm_t, out_sum, d_norm, act, slope, tmp = refs
    step, steps = pl.program_id(0), pl.num_programs(0)
    rows, width = hidden.shape
    tile = 128

    @pl.when(step == 0)
    def _():
        for r in range(0, rows, tile):
            t = slice(r, r + tile)
            value = tokens[t, :].astype(f32) + dot(context[t, :], w_out[...])
            hidden[t, :] = value
            normed, _ = norm_stats(value)
            norm_low[t, :] = (normed * gain[...] + bias[...]).astype(bf16)
        norm_t[...] = norm_low[...].T
        out_sum[...] = jnp.zeros_like(out_sum)
        d_norm[...] = jnp.zeros_like(d_norm)

    for r in range(0, rows, tile):
        t = slice(r, r + tile)
        value, grad = gelu_both(dot(norm_low[t, :], w_in[...]))
        low = value.astype(bf16)
        act[t, :] = low
        out_sum[t, :] += dot(low, w_back[...])
        d_low = (dot_nt(grad_out[t, :], w_back[...]) * grad).astype(bf16)
        slope[t, :] = d_low
        d_norm[t, :] += dot_nt(d_low, w_in[...])
    back_grads = dot_tn(act[...], grad_out[...]).astype(bf16)
    in_grads = dot(norm_t[...], slope[...]).astype(bf16)
    if num_grads == 3:
        grad_refs[0][...] = back_grads
        grad_refs[1][...] = in_grads
    else:
        tmp[...] = back_grads
        share = tmp.shape[0] // 8
        for yr in range(2):
            for xr in range(2):
                for cr in range(2):
                    place = (xr ^ coords[1]) * 4 + (cr ^ coords[2]) * 2 + (yr ^ coords[3])
                    rows_from = pl.ds(pl.multiple_of(place * share, 16), share)
                    for half in range(2):
                        grad_refs[cr][yr, xr, 0, half * share : (half + 1) * share, :] = tmp[
                            rows_from, half * width // 2 : (half + 1) * width // 2
                        ]
        tmp[...] = in_grads
        side = (step // 2) ^ coords[3]
        for odd in range(2):

            @pl.when(step % 2 == odd)
            def _():
                for half in range(2):
                    halves_to_dests(
                        coords, tmp, half, grad_refs[2], grad_refs[3], odd * 2 + half, side
                    )

    @pl.when(step == steps - 1)
    def _():
        for r in range(0, rows, tile):
            t = slice(r, r + tile)
            value = hidden[t, :]
            output[t, :] = (value + out_sum[t, :]).astype(bf16)
            normed, inv = norm_stats(value)
            grad = d_norm[t, :]
            part_gain = jnp.sum(grad * normed, 0, keepdims=True)
            part_bias = jnp.sum(grad, 0, keepdims=True)
            if r == 0:
                gain_part[...] = part_gain
                bias_part[...] = part_bias
            else:
                gain_part[...] += part_gain
                bias_part[...] += part_bias
            hat = grad * gain[...]
            mean_hat = jnp.mean(hat, -1, keepdims=True)
            mean_dot = jnp.mean(hat * normed, -1, keepdims=True)
            total = grad_out[t, :].astype(f32) + inv * (hat - mean_hat - normed * mean_dot)
            d_hidden[t, :] = total
            low = total.astype(bf16)
            norm_low[t, :] = low
            d_context[t, :] = dot_nt(low, w_out[...]).astype(bf16)
        out_grads = dot_tn(context[...], norm_low[...]).astype(bf16)
        if num_grads == 3:
            grad_refs[2][...] = out_grads
        else:
            tmp[...] = out_grads
            for half in range(2):
                halves_to_dests(
                    coords, tmp, half, grad_refs[2], grad_refs[3], 4, half ^ coords[3]
                )


def hop(values, route):
    return lax.ppermute(values, "seq", route)


def swap(bit):
    return [(i, i ^ bit) for i in range(16)]


CORE, ACROSS = swap(1), swap(2)
NEAR, FAR = swap(4), swap(8)
UP = [(i, i + 4) for i in range(12)]
DOWN = [(i + 4, i) for i in range(12)]
UP_LATE = UP[4:]
DOWN_LATE = DOWN[:8]
LOW, HIGH = ACROSS[:8], ACROSS[8:]


def tie(*values):
    return lax.optimization_barrier(values)


def gather_pieces(tok):
    below, above, beside = hop(tok, UP), hop(tok, DOWN), hop(tok, ACROSS)
    sib = {"own": hop(tok, CORE)}
    below, above, beside = tie(below, above, beside)
    below2, above2 = hop(below, UP_LATE), hop(above, DOWN_LATE)
    sib["below"], sib["above"], sib["beside"] = [hop(v, CORE) for v in (below, above, beside)]
    below_x, above_x = hop(beside, UP), hop(beside, DOWN)
    below2, above2 = tie(below2, above2)
    below2_x, above2_x = hop(below2, HIGH), hop(above2, LOW)
    pieces = []
    for plain, crossed in (
        (below2, below2_x), (below, below_x), (tok, beside), (above, above_x), (above2, above2_x),
    ):
        for piece in (plain, crossed):
            if piece is tok:
                other = sib["own"]
            elif piece is below:
                other = sib["below"]
            elif piece is above:
                other = sib["above"]
            elif piece is beside:
                other = sib["beside"]
            else:
                other = hop(piece, CORE)
            pieces += [piece, other]
    return pieces


def slot_codes(slots, per_dev, coords):
    owner, block = slots // per_dev, slots % per_dev
    z, x, core = owner // 4, (owner // 2) % 2, owner % 2
    piece = (z - coords[0] + 2) * 4 + (x ^ coords[1]) * 2 + (core ^ coords[2])
    return (piece * per_dev + block).astype(jnp.int32)


def scatter_kernel(codes, sib_codes, own, sib, *refs):
    outs, acc = refs[:-1], refs[-1]
    per_dev = outs[0].shape[0]
    acc[...] = jnp.zeros_like(acc)

    def add(s, _):
        for which, source, cls in ((codes, own, 0), (sib_codes, sib, 1)):
            piece, block = which[s] // per_dev, which[s] % per_dev

            @pl.when(piece % 2 == cls)
            def _():
                acc[(piece // 2) * per_dev + block] += source[s].astype(f32)

        return 0

    lax.fori_loop(0, own.shape[0], add, 0)
    for k, out in enumerate(outs):

        def store(b, _):
            out[b] = acc[k * per_dev + b].astype(bf16)
            return 0

        lax.fori_loop(0, per_dev, store, 0)


def plus(*values):
    total = values[0].astype(f32)
    for value in values[1:]:
        total = total + value.astype(f32)
    return total.astype(bf16)


def over_y(values):
    return lax.ppermute(values, "grp", [(0, 1), (1, 0)])


def split(keep, got, axis=0):
    pick = lambda v, n: v[n] if axis == 0 else v[:, n]
    return plus(pick(keep, 1), pick(got, 1)), plus(pick(keep, 0), pick(got, 0))


def by_pairs(values):
    return values.reshape((2, 2) + values.shape[1:])


def both_halves(mine):
    other = over_y(mine)
    first = lax.axis_index("grp") == 0
    return jnp.stack([jnp.where(first, mine, other), jnp.where(first, other, mine)]).astype(f32)


def call(kernel, out_shape, in_specs, scratch, name):
    return pl.pallas_call(
        kernel,
        out_shape=out_shape,
        in_specs=in_specs,
        out_specs=[vmem()] * len(out_shape),
        scratch_shapes=scratch,
        compiler_params=pltpu.CompilerParams(vmem_limit_bytes=VMEM_LIMIT),
        cost_estimate=COST,
        name=name,
    )


def body(
    tokens, w_qkv, w_out, w_in, w_back, ln1_gain, ln1_bias, ln2_gain, ln2_bias,
    doc_units, tail_pad, global_ids, rand_blocks, out_grad,
):
    tok = tokens[0]
    grad_out = out_grad[0]
    rows, width = tok.shape
    ff = w_in.shape[1]
    per_dev = rows // BLK
    shards = lax.axis_size("seq")
    placed = shards == 16 and lax.axis_size("grp") == 2
    me = lax.axis_index("seq")
    first_row = me * per_dev
    coords = jnp.stack([me // 4, (me // 2) % 2, me % 2, lax.axis_index("grp")]).astype(jnp.int32)
    live, slots = block_plan(doc_units[0], tail_pad[0], global_ids[0], rand_blocks[0], first_row)
    count = slots.shape[0]
    gain1, bias1 = ln1_gain[None], ln1_bias[None]
    gain2, bias2 = ln2_gain[None], ln2_bias[None]

    if placed:
        pieces = gather_pieces(tok)
        pieces = [p.reshape(per_dev, BLK, width) for p in pieces]
        codes = slot_codes(slots, per_dev, coords)
    else:
        pieces = [lax.all_gather(tok, "seq").reshape(shards * per_dev, BLK, width)]
        codes = slots

    normed_one, inv_one = norm_stats(tok.astype(f32))
    own_norm = (normed_one * ln1_gain + ln1_bias).astype(bf16)
    projected = jnp.dot(own_norm, w_qkv, preferred_element_type=f32)
    query = (projected[:, :width] * HD**-0.5).astype(bf16)
    own_kv = projected[:, width:].astype(bf16)

    quads = width // QW
    context, lse, slot_norm, slot_hat, slot_kv = call(
        functools.partial(forward_kernel, len(pieces)),
        [
            shape((rows, width), bf16),
            shape((per_dev, quads, QW), f32),
            shape((count * BLK, width), bf16),
            shape((count * BLK, width), bf16),
            shape((count * BLK, 2 * width), bf16),
        ],
        [smem(), smem()] + [anym()] * len(pieces) + [vmem()] * 5,
        [
            pltpu.VMEM((count, BLK, width), bf16),
            pltpu.VMEM((rows + 2 * BLK, 2 * width), bf16),
            pltpu.SemaphoreType.DMA((count,)),
        ],
        "attend_forward",
    )(codes, live, *pieces, query, own_kv, w_qkv, gain1, bias1)

    chunk = width
    steps = ff // chunk
    const = lambda *dims: pl.BlockSpec(dims, lambda s, c: (0,) * len(dims))
    if placed:
        back_half = (2, 2, 4, ff // 16, width // 2)
        rest_half = (2, 2, 4, 5 * (width // 16), width // 2)
        back_spec = pl.BlockSpec((2, 2, 1, ff // 16, width // 2), lambda s, c: (0, 0, s ^ c[0], 0, 0))
        grad_specs = [back_spec, back_spec, const(*rest_half), const(*rest_half)]
        grad_shapes = [shape(back_half, bf16)] * 2 + [shape(rest_half, bf16)] * 2
    else:
        grad_specs = [
            pl.BlockSpec((chunk, width), lambda s, c: (s, 0)),
            pl.BlockSpec((width, chunk), lambda s, c: (0, s)),
            const(width, width),
        ]
        grad_shapes = [
            shape((ff, width), bf16), shape((width, ff), bf16), shape((width, width), bf16),
        ]
    output, d_hidden, d_context, gain_two, bias_two, *grads = pl.pallas_call(
        functools.partial(middle_kernel, len(grad_specs)),
        grid_spec=pltpu.PrefetchScalarGridSpec(
            num_scalar_prefetch=1,
            grid=(steps,),
            in_specs=[
                const(rows, width), const(rows, width), const(rows, width), const(width, width),
                const(1, width), const(1, width),
                pl.BlockSpec((width, chunk), lambda s, c: (0, s)),
                pl.BlockSpec((chunk, width), lambda s, c: (s, 0)),
            ],
            out_specs=[
                const(rows, width), const(rows, width), const(rows, width),
                const(1, width), const(1, width), *grad_specs,
            ],
            scratch_shapes=[
                pltpu.VMEM((rows, width), f32), pltpu.VMEM((rows, width), bf16),
                pltpu.VMEM((width, rows), bf16), pltpu.VMEM((rows, width), f32),
                pltpu.VMEM((rows, width), f32), pltpu.VMEM((rows, chunk), bf16),
                pltpu.VMEM((rows, chunk), bf16), pltpu.VMEM((chunk, width), bf16),
            ],
        ),
        out_shape=[
            shape((rows, width), bf16), shape((rows, width), f32), shape((rows, width), bf16),
            shape((1, width), f32), shape((1, width), f32), *grad_shapes,
        ],
        compiler_params=pltpu.CompilerParams(vmem_limit_bytes=VMEM_LIMIT),
        cost_estimate=COST,
        name="middle",
    )(coords, tok, context, grad_out, w_out, gain2, bias2, w_in, w_back)

    share = width // shards
    parts_in = (query, d_context, own_kv, own_kv, slot_kv, slot_kv)

    def attend_back(parts, ins):
        live, lse, *arrays = ins
        column = lambda n, j: pl.BlockSpec((n, QW), lambda i: (0, j))
        specs, operands, outs = [], [], []
        for part in parts:
            specs += [column(rows, part), column(rows, part)]
            specs += [column(rows, part), column(rows, part + quads)]
            specs += [column(count * BLK, part), column(count * BLK, part + quads)]
            operands += arrays
            outs += [
                shape((rows, QW), bf16), shape((rows, 2 * QW), bf16),
                shape((count * BLK, 2 * QW), bf16),
            ]
        whole = lambda s: pl.BlockSpec(s.shape, lambda i: (0,) * len(s.shape))
        return list(pl.pallas_call(
            functools.partial(backward_kernel, parts),
            grid=(1,),
            out_shape=outs,
            in_specs=[smem(), whole(lse)] + specs,
            out_specs=[whole(o) for o in outs],
            scratch_shapes=[
                pltpu.VMEM((2 * len(parts), rows + 2 * BLK, QW), bf16),
                pltpu.VMEM((2 * len(parts), rows + 2 * BLK, QW), f32),
                pltpu.VMEM((2 * len(parts), 2 * BLK, QW), f32),
            ],
            compiler_params=pltpu.CompilerParams(vmem_limit_bytes=VMEM_LIMIT),
            cost_estimate=COST,
            name="attend_backward",
        )(live, lse, *operands))

    if placed:
        keep_a, send_a, keep_b, send_b = grads
        got_a, got_b = hop(send_a, CORE), hop(send_b, CORE)
        first = attend_back((0,), (live, lse) + parts_in)
        got_a, got_b, *first = tie(got_a, got_b, *first)
        out_a, mine_a = split(keep_a, got_a)
        out_b, mine_b = split(keep_b, got_b, 1)
        out_a, mine_a, out_b, mine_b, live_late, *first = tie(
            out_a, mine_a, out_b, mine_b, live, *first
        )
        got_a, got_b = over_y(out_a), hop(out_b, ACROSS)
        d_parts = first + attend_back((1, 2), (live_late, lse) + parts_in)
    else:
        d_parts = attend_back((0, 1, 2), (live, lse) + parts_in)

    hat = normed_one.astype(bf16)
    d_own_norm, d_slot_norm, gain_one, bias_one = call(
        functools.partial(project_back_kernel, quads),
        [
            shape((rows, width), f32), shape((count * BLK, width), bf16),
            shape((1, width), f32), shape((1, width), f32),
        ],
        [vmem()] * (3 + 3 * quads),
        [],
        "project_back",
    )(w_qkv, hat, slot_hat, *d_parts)

    def qkv_grads(d_parts):
        if placed:
            shapes = [shape((2, 2, 4, 3 * share + 16, width // 2), bf16)] * 2
        else:
            shapes = [shape((width, 3 * width), bf16)]
        return call(
            functools.partial(qkv_grad_kernel, len(shapes)),
            shapes,
            [smem()] + [vmem()] * (6 + 3 * quads),
            [pltpu.VMEM((width, width), bf16)],
            "qkv_grads",
        )(coords, gain_one, bias_one, gain_two, bias_two, own_norm, slot_norm, *d_parts)

    def token_grads(d_norm1):
        grad_hat = d_norm1 * ln1_gain
        d_first = inv_one * (
            grad_hat
            - jnp.mean(grad_hat, -1, keepdims=True)
            - normed_one * jnp.mean(grad_hat * normed_one, -1, keepdims=True)
        )
        return (d_hidden + d_first).astype(bf16)

    if placed:
        d_slot_norm = d_slot_norm.reshape(count, BLK, width)
        sib_codes = hop(codes, CORE)
        sib_norm = hop(d_slot_norm, CORE)
        got_a, got_b, *d_parts = tie(got_a, got_b, *d_parts, d_slot_norm)[:-1]
        out_a, mine_a = split(mine_a, got_a)
        out_b, mine_b = split(mine_b, got_b)
        out_a, mine_a, out_b, mine_b, *d_parts = tie(out_a, mine_a, out_b, mine_b, *d_parts)
        got_a, got_b = hop(out_a, ACROSS), over_y(out_b)
        keep_c, send_c = qkv_grads(d_parts)
        keep_c, send_c, sib_norm = tie(keep_c, send_c, sib_norm)
        got_c = hop(send_c, CORE)
        piece_shape = shape((per_dev, BLK, width), bf16)
        sums = call(
            scatter_kernel,
            [piece_shape] * 10,
            [smem(), smem(), vmem(), vmem()],
            [pltpu.VMEM((10 * per_dev, BLK, width), f32)],
            "scatter_slots",
        )(codes, sib_codes, d_slot_norm, sib_norm)
        below2, below2_x, below, below_x, own, beside, above, above_x, above2, above2_x = [
            p.reshape(rows, width) for p in sums
        ]
        in_below2, in_above2 = hop(below2_x, HIGH), hop(above2_x, LOW)
        from_above_x, from_below_x = hop(below_x, DOWN), hop(above_x, UP)
        got_a, got_b, got_c, own = tie(got_a, got_b, got_c, own)
        out_c, mine_c = split(keep_c, got_c)
        mine_ab = [plus(m, g) for m, g in ((mine_a, got_a), (mine_b, got_b))]
        mine_ab = by_pairs(jnp.concatenate(mine_ab, 1))
        out_c, mine_c, mine_ab, in_below2, in_above2, from_above_x, from_below_x = tie(
            out_c, mine_c, mine_ab, in_below2, in_above2, from_above_x, from_below_x
        )
        got_c = over_y(out_c)
        got_ab = hop(mine_ab[:, 1], NEAR)
        below2, above2 = plus(below2, in_below2), plus(above2, in_above2)
        beside = plus(beside, from_above_x, from_below_x)
        from_above2, from_below2 = hop(below2, DOWN[4:]), hop(above2, UP[:8])
        from_beside = hop(beside, ACROSS)
        got_c, got_ab, below2, above2, beside = tie(got_c, got_ab, below2, above2, beside)
        out_c, mine_c = split(mine_c, got_c)
        mine_ab = plus(mine_ab[:, 0], got_ab)
        out_c, mine_c, mine_ab, from_above2, from_below2, from_beside = tie(
            out_c, mine_c, mine_ab, from_above2, from_below2, from_beside
        )
        got_c = hop(out_c, ACROSS)
        got_ab = hop(mine_ab[1], FAR)
        below, above = plus(below, from_above2), plus(above, from_below2)
        from_above, from_below = hop(below, DOWN), hop(above, UP)
        got_c, got_ab, below, above = tie(got_c, got_ab, below, above)
        mine_c = by_pairs(plus(mine_c, got_c))
        mine_ab = plus(mine_ab[0], got_ab)
        mine_c, mine_ab, from_above, from_below = tie(mine_c, mine_ab, from_above, from_below)
        got_c = hop(mine_c[:, 1], NEAR)
        halves_ab = both_halves(mine_ab)
        d_norm1 = d_own_norm
        for part in (own, from_beside, from_above, from_below):
            d_norm1 = d_norm1 + part.astype(f32)
        tokens_grad = token_grads(d_norm1)
        got_c, tokens_grad = tie(got_c, tokens_grad)
        mine_c = plus(mine_c[:, 0], got_c)
        got_c = hop(mine_c[1], FAR)
        halves_c = both_halves(plus(mine_c[0], got_c))

        half = width // 2
        back_rows = ff // 16
        back_grad = halves_ab[:, :back_rows].reshape(2, 2, back_rows // 2, half)
        back_grad = back_grad.transpose(0, 2, 1, 3).reshape(back_rows, width)
        rest = halves_ab[:, back_rows:].reshape(2, 5, share, half)
        in_grad = rest[:, :4].reshape(8, share, half).transpose(1, 0, 2).reshape(share, ff)
        out_proj_grad = rest[:, 4].transpose(1, 0, 2).reshape(share, width)
        qkv_grad = halves_c[:, : 3 * share].reshape(6, share, half).transpose(1, 0, 2)
        qkv_grad = qkv_grad.reshape(share, 3 * width)
        vectors = halves_c[0, 3 * share : 3 * share + 8].reshape(4, width)
        vectors = lax.dynamic_slice_in_dim(vectors, me * share, share, 1)
    else:
        spread_grads = jnp.zeros((shards * per_dev, BLK, width), f32)
        spread_grads = spread_grads.at[slots].add(
            d_slot_norm.reshape(count, BLK, width).astype(f32)
        )
        others = lax.psum_scatter(
            spread_grads.astype(bf16).reshape(shards * rows, width),
            "seq", scatter_dimension=0, tiled=True,
        )
        tokens_grad = token_grads(d_own_norm + others.astype(f32))

        def reduce(part):
            mine = lax.psum_scatter(part, "seq", scatter_dimension=0, tiled=True)
            return lax.psum(mine, "grp").astype(f32)

        back_grad, in_grad, out_proj_grad = [reduce(g) for g in grads]
        qkv_grad = reduce(qkv_grads(d_parts)[0])
        vectors = jnp.concatenate([gain_one, bias_one, gain_two, bias_two])
        vectors = lax.psum(vectors, ("seq", "grp"))
        vectors = lax.dynamic_slice_in_dim(vectors, me * share, share, 1)
    return (
        output[None],
        tokens_grad[None],
        qkv_grad,
        out_proj_grad,
        in_grad,
        back_grad,
        vectors[0],
        vectors[1],
        vectors[2],
        vectors[3],
    )


def solution(mesh):
    in_specs = (
        P("grp", "seq", None),
        P(),
        P(),
        P(),
        P(),
        P(),
        P(),
        P(),
        P(),
        P("grp", None),
        P("grp", None),
        P("grp", None, None),
        P("grp", "seq", None),
        P("grp", "seq", None),
    )
    out_specs = (
        P("grp", "seq", None),
        P("grp", "seq", None),
        P("seq", None),
        P("seq", None),
        P("seq", None),
        P("seq", None),
        P("seq"),
        P("seq"),
        P("seq"),
        P("seq"),
    )
    return jax.shard_map(body, mesh=mesh, in_specs=in_specs, out_specs=out_specs, check_vma=False)
```

```python
import functools

import jax
import jax.numpy as jnp
from jax import lax
from jax.experimental import pallas as pl
from jax.experimental.pallas import tpu as pltpu
from jax.sharding import PartitionSpec as P

HD = 64
BLK = 64
UNITB = 8
QUAD = 4
QW = QUAD * HD
ln_eps = 1e-12
bf16 = jnp.bfloat16
f32 = jnp.float32
ROOM = (12, 26, 40, 14, 36, 22, 24)
BRIEF = pl.CostEstimate(flops=1_000_000, bytes_accessed=1, transcendentals=0)
COST = pl.CostEstimate(flops=40_000_000_000, bytes_accessed=1, transcendentals=0)
vmem = functools.partial(pl.BlockSpec, memory_space=pltpu.VMEM)
smem = functools.partial(pl.BlockSpec, memory_space=pltpu.SMEM)
anym = functools.partial(pl.BlockSpec, memory_space=pl.ANY)
hbm = functools.partial(pl.BlockSpec, memory_space=pltpu.HBM)


def shape(dims, dtype):
    return jax.ShapeDtypeStruct(dims, dtype)


def dot(a, b):
    return lax.dot_general(a, b, (((1,), (0,)), ((), ())), preferred_element_type=f32)


def dot_nt(a, b):
    return lax.dot_general(a, b, (((1,), (1,)), ((), ())), preferred_element_type=f32)


def dot_tn(a, b):
    return lax.dot_general(a, b, (((0,), (0,)), ((), ())), preferred_element_type=f32)


def norm_stats(values):
    center = values - jnp.mean(values, -1, keepdims=True)
    inv_std = lax.rsqrt(jnp.mean(center * center, -1, keepdims=True) + ln_eps)
    return center * inv_std, inv_std


def block_plan(doc_len, tail_len, global_rel, rand_rows, first_row):
    per_dev = rand_rows.shape[0]
    doc_end = jnp.cumsum(doc_len) * UNITB
    starts = doc_end - doc_len * UNITB
    mine = ((first_row >= starts) & (first_row < doc_end)).astype(jnp.int32)
    begin = jnp.sum(mine * starts)
    finish = jnp.sum(mine * doc_end)
    padding = jnp.sum(mine * tail_len)
    glob_one = begin + jnp.sum(mine * global_rel[:, 0])
    glob_two = begin + jnp.sum(mine * global_rel[:, 1])
    rows = first_row + jnp.arange(per_dev, dtype=jnp.int32)
    before = jnp.where(rows - 1 >= begin, rows - 1, -1)
    follow = jnp.where(rows + 1 < finish, rows + 1, -1)
    whole = jnp.zeros_like(rows)
    candidates = jnp.concatenate(
        [jnp.stack([before, rows, follow, whole + glob_one, whole + glob_two], 1), rand_rows], 1
    )
    count = candidates.shape[1]
    equal = candidates[:, :, None] == candidates[:, None, :]
    earlier = jnp.arange(count)[:, None] > jnp.arange(count)[None, :]
    usable = (candidates >= 0) & jnp.logical_not(jnp.any(equal & earlier[None], 2))
    filled = jnp.where(candidates == finish - 1, BLK - padding, BLK)
    live = jnp.where(usable, filled, 0).astype(jnp.int32)
    halo = jnp.stack(
        [
            jnp.where(first_row - 1 >= begin, first_row - 1, first_row),
            jnp.where(first_row + per_dev < finish, first_row + per_dev, first_row),
            glob_one,
            glob_two,
        ]
    )
    slots = jnp.concatenate([halo, rand_rows.reshape(-1)]).astype(jnp.int32)
    return live.reshape(-1), slots


def head_masks(rows):
    lane = lax.broadcasted_iota(jnp.int32, (rows, QW), 1) // HD
    return [lane == h for h in range(QUAD)]


def spread(values, masks):
    zero = jnp.zeros_like(values)
    return jnp.concatenate([jnp.where(m, values, zero) for m in masks], 0)


def collect(values, masks):
    out = values[:BLK]
    for h in range(1, QUAD):
        out = jnp.where(masks[h], values[h * BLK : (h + 1) * BLK], out)
    return out


def key_rows(ext, slots, i, cols):
    return jnp.concatenate(
        [
            ext[pl.ds(pl.multiple_of(i * BLK, BLK), 3 * BLK), cols],
            slots[2 * BLK : 4 * BLK, cols],
            slots[pl.ds(pl.multiple_of((4 + 3 * i) * BLK, BLK), 3 * BLK), cols],
        ],
        0,
    )


def masked(scores, live, i, cand):
    row = lax.broadcasted_iota(jnp.int32, (BLK, QW), 0)
    return jnp.concatenate(
        [
            jnp.where(row < live[i * cand + c], scores[c * BLK : (c + 1) * BLK], -1e30)
            for c in range(cand)
        ],
        0,
    )


def fill_ext(ext, own, slots):
    rows = own.shape[0]
    ext[0:BLK, :] = slots[0:BLK, :]
    ext[BLK : BLK + rows, :] = own[...]
    ext[BLK + rows : 2 * BLK + rows, :] = slots[BLK : 2 * BLK, :]


def own_kernel(tokens, w_qkv, gain, bias, query, own_kv, own_norm, own_hat):
    rows, width = tokens.shape
    tile = 128
    for r in range(0, rows, tile):
        t = slice(r, r + tile)
        normed, _ = norm_stats(tokens[t, :].astype(f32))
        own_hat[t, :] = normed.astype(bf16)
        low = (normed * gain[...] + bias[...]).astype(bf16)
        own_norm[t, :] = low
        query[t, :] = (dot(low, w_qkv[:, :width]) * HD**-0.5).astype(bf16)
        own_kv[t, :] = dot(low, w_qkv[:, width:]).astype(bf16)


def forward_kernel(num_pieces, codes, live, *refs):
    pieces, refs = refs[:num_pieces], refs[num_pieces:]
    query, own_kv, w_qkv, gain, bias = refs[:5]
    context, lse, slot_norm, slot_hat, slot_kv, slot_tok, ext, sems = refs[5:]
    count = slot_tok.shape[0]
    per_piece = pieces[0].shape[0]
    width = query.shape[1]
    nblk = query.shape[0] // BLK
    cand = live.shape[0] // nblk

    def fetch(s, piece, block):
        return pltpu.make_async_copy(piece.at[block], slot_tok.at[s], sems.at[s])

    def start(s, _):
        which, block = codes[s] // per_piece, codes[s] % per_piece
        for k, piece in enumerate(pieces):

            @pl.when(which == k)
            def _():
                fetch(s, piece, block).start()

        return 0

    lax.fori_loop(0, count, start, 0)
    group = 4

    def project(step, _):
        for k in range(group):
            fetch(step * group + k, pieces[0], 0).wait()
        rows = pl.ds(pl.multiple_of(step * group * BLK, group * BLK), group * BLK)
        tok = slot_tok[pl.ds(step * group, group)].reshape(group * BLK, width).astype(f32)
        normed, _ = norm_stats(tok)
        slot_hat[rows, :] = normed.astype(bf16)
        low = (normed * gain[...] + bias[...]).astype(bf16)
        slot_norm[rows, :] = low
        slot_kv[rows, :] = dot(low, w_qkv[:, width:]).astype(bf16)
        return 0

    lax.fori_loop(0, count // group, project, 0)
    fill_ext(ext, own_kv, slot_kv)
    masks = head_masks(BLK)

    def attend(i, _):
        qrows = pl.ds(pl.multiple_of(i * BLK, BLK), BLK)
        for quad in range(width // QW):
            cols = pl.ds(quad * QW, QW)
            vcols = pl.ds(width + quad * QW, QW)
            keys = key_rows(ext, slot_kv, i, cols)
            vals = key_rows(ext, slot_kv, i, vcols)
            scores = masked(dot_nt(keys, spread(query[qrows, cols], masks)), live, i, cand)
            top = jnp.max(scores, 0, keepdims=True)
            expo = jnp.exp(scores - top)
            total = jnp.sum(expo, 0, keepdims=True)
            probs = (expo * (1.0 / total)).astype(bf16)
            lse[i, pl.ds(quad, 1), :] = top + jnp.log(total)
            context[qrows, cols] = collect(dot_tn(probs, vals), masks).astype(bf16)
        return 0

    lax.fori_loop(0, nblk, attend, 0)


def attend_back_parts(parts, live, lse, ins, outs, ext, d_ext, d_glob):
    rows_own = ins[0].shape[0]
    nblk = rows_own // BLK
    cand = live.shape[0] // nblk
    d_ext[...] = jnp.zeros_like(d_ext)
    d_glob[...] = jnp.zeros_like(d_glob)
    masks = head_masks(BLK)
    for n in range(len(parts)):
        for kv in range(2):
            own, slots = ins[6 * n + 2 + kv], ins[6 * n + 4 + kv]
            fill_ext(ext.at[2 * n + kv], own, slots)

    def attend(i, _):
        qrows = pl.ds(pl.multiple_of(i * BLK, BLK), BLK)
        near = pl.ds(pl.multiple_of(i * BLK, BLK), 3 * BLK)
        far = pl.ds(pl.multiple_of((4 + 3 * i) * BLK, BLK), 3 * BLK)
        every = pl.ds(0, QW)
        for n, part in enumerate(parts):
            query, d_context, _, _, slot_k, slot_v = ins[6 * n : 6 * n + 6]
            d_query, _, d_slot = outs[3 * n : 3 * n + 3]
            keys = key_rows(ext.at[2 * n], slot_k, i, every)
            vals = key_rows(ext.at[2 * n + 1], slot_v, i, every)
            spread_q = spread(query[qrows, :], masks)
            spread_d = spread(d_context[qrows, :], masks)
            scores = masked(dot_nt(keys, spread_q), live, i, cand)
            probs = jnp.exp(scores - lse[i, pl.ds(part, 1), :])
            d_probs = dot_nt(vals, spread_d)
            delta = jnp.sum(d_probs * probs, 0, keepdims=True)
            d_scores = (probs * (d_probs - delta)).astype(bf16)
            d_keys = dot(d_scores, spread_q)
            d_vals = dot(probs.astype(bf16), spread_d)
            d_query[qrows, :] = (collect(dot_tn(d_scores, keys), masks) * HD**-0.5).astype(bf16)
            for kv, grads in enumerate((d_keys, d_vals)):
                d_ext[2 * n + kv, near, :] += grads[: 3 * BLK]
                d_glob[2 * n + kv] += grads[3 * BLK : 5 * BLK]
                d_slot[far, kv * QW : (kv + 1) * QW] = grads[5 * BLK :].astype(bf16)
        return 0

    lax.fori_loop(0, nblk, attend, 0)
    for n in range(len(parts)):
        _, d_own, d_slot = outs[3 * n : 3 * n + 3]
        for kv in range(2):
            cols = slice(kv * QW, (kv + 1) * QW)
            d_slot[0:BLK, cols] = d_ext[2 * n + kv, 0:BLK, :].astype(bf16)
            d_slot[BLK : 2 * BLK, cols] = d_ext[2 * n + kv, BLK + rows_own :, :].astype(bf16)
            d_slot[2 * BLK : 4 * BLK, cols] = d_glob[2 * n + kv].astype(bf16)
            d_own[:, cols] = d_ext[2 * n + kv, BLK : BLK + rows_own, :].astype(bf16)


def first_backward_kernel(parts, live, lse, *refs):
    count = len(parts)
    ins, outs, scratch = refs[: 6 * count], refs[6 * count : 9 * count], refs[9 * count :]
    attend_back_parts(parts, live, lse, ins, outs, *scratch)


def joined(refs, rows):
    return jnp.concatenate(
        [r[rows, kv * QW : (kv + 1) * QW] for kv in range(2) for r in refs], 1
    )


def last_backward_kernel(parts, early, live, lse, *refs):
    count = len(parts)
    late = 3 + 3 * early
    held_hbm, refs = refs[:late], refs[late:]
    ins, outs, refs = refs[: 6 * count], refs[6 * count : 9 * count], refs[9 * count :]
    (d_own_norm, d_slot_norm, gain_part, bias_part), refs = refs[:4], refs[4:]
    scratch, held, sems = refs[:3], refs[3:-1], refs[-1]
    copies = [
        pltpu.make_async_copy(src, dst, sems.at[n])
        for n, (src, dst) in enumerate(zip(held_hbm, held))
    ]
    for copy in copies:
        copy.start()
    attend_back_parts(parts, live, lse, ins, outs, *scratch)
    for copy in copies:
        copy.wait()
    w_qkv, own_hat, slot_hat = held[:3]
    grads_in = held[3:] + outs
    d_query, d_own, d_slot = grads_in[0::3], grads_in[1::3], grads_in[2::3]
    rows_own, width = d_own_norm.shape
    step_rows = 4 * BLK

    def add(grads, hat, first):
        gain = jnp.sum(grads * hat.astype(f32), 0, keepdims=True)
        bias = jnp.sum(grads, 0, keepdims=True)
        if first:
            gain_part[...], bias_part[...] = gain, bias
        else:
            gain_part[...] += gain
            bias_part[...] += bias

    for r in range(0, rows_own, step_rows):
        rows = slice(r, r + step_rows)
        grads = dot_nt(jnp.concatenate([d[rows, :] for d in d_query], 1), w_qkv[:, :width])
        grads += dot_nt(joined(d_own, rows), w_qkv[:, width:])
        d_own_norm[rows, :] = grads
        add(grads, own_hat[rows, :], r == 0)

    def back(step, _):
        rows = pl.ds(pl.multiple_of(step * step_rows, step_rows), step_rows)
        grads = dot_nt(joined(d_slot, rows), w_qkv[:, width:])
        d_slot_norm[rows, :] = grads.astype(bf16)
        add(grads, slot_hat[rows, :], False)
        return 0

    lax.fori_loop(0, d_slot_norm.shape[0] // step_rows, back, 0)


def halves_to_dests(coords, grads, half, keep, send, slot, side):
    share = grads.shape[0] // 16
    for zr in range(4):
        for xr in range(2):
            for cr, target in ((0, keep), (1, send)):
                dest = (zr ^ coords[0]) * 4 + (xr ^ coords[1]) * 2 + (cr ^ coords[2])
                rows = pl.ds(pl.multiple_of(dest * share, 16), share)
                target[side, xr, zr, slot * share : (slot + 1) * share, :] = grads[
                    rows, half * 384 : (half + 1) * 384
                ]


def qkv_grad_kernel(num_out, coords, gain1, bias1, gain2, bias2, own_norm, slot_norm, *refs):
    ins, outs, tmp = refs[: -1 - num_out], refs[-1 - num_out : -1], refs[-1]
    d_query, d_own, d_slot = ins[0::3], ins[1::3], ins[2::3]
    width = own_norm.shape[1]
    whole = slice(None)
    for part in range(3):
        if part == 0:
            grads = dot_tn(own_norm[...], jnp.concatenate([d[...] for d in d_query], 1))
        else:
            cols = slice((part - 1) * QW, part * QW)
            grads = dot_tn(own_norm[...], jnp.concatenate([d[:, cols] for d in d_own], 1))
            grads += dot_tn(slot_norm[...], jnp.concatenate([d[:, cols] for d in d_slot], 1))
        if num_out == 1:
            outs[0][:, part * width : (part + 1) * width] = grads.astype(bf16)
        else:
            tmp[...] = grads.astype(bf16)
            for half in range(2):
                piece = part * 2 + half
                side = (piece // 3) ^ coords[3]
                halves_to_dests(coords, tmp, half, outs[0], outs[1], piece % 3, side)
    if num_out == 2:
        half = width // 2
        lines = [v[:, h * half : (h + 1) * half] for v in (gain1, bias1, gain2, bias2) for h in (0, 1)]
        block = jnp.concatenate(lines + [jnp.zeros((8, half), f32)], 0).astype(bf16)
        rows = slice(outs[0].shape[3] - 16, outs[0].shape[3])
        for out in outs:
            for side in range(2):
                for xr in range(2):
                    for zr in range(4):
                        out[side, xr, zr, rows, :] = block


def gelu_both(x):
    half_erf = 0.5 * lax.erf(x * 0.7071067811865476)
    cdf = 0.5 + half_erf
    density = jnp.exp(-0.5 * x * x) * 0.3989422804014327
    return x * cdf, cdf + x * density


def middle_kernel(
    num_grads, coords, tokens, context, grad_out, w_out, gain, bias, w_in, w_back,
    output, d_hidden, d_context, gain_part, bias_part, *refs,
):
    grad_refs, refs = refs[:num_grads], refs[num_grads:]
    hidden, norm_low, norm_t, out_sum, d_norm, act, slope, tmp = refs
    step, steps = pl.program_id(0), pl.num_programs(0)
    rows, width = hidden.shape
    tile = 128

    @pl.when(step == 0)
    def _():
        for r in range(0, rows, tile):
            t = slice(r, r + tile)
            value = tokens[t, :].astype(f32) + dot(context[t, :], w_out[...])
            hidden[t, :] = value
            normed, _ = norm_stats(value)
            norm_low[t, :] = (normed * gain[...] + bias[...]).astype(bf16)
        norm_t[...] = norm_low[...].T
        out_sum[...] = jnp.zeros_like(out_sum)
        d_norm[...] = jnp.zeros_like(d_norm)

    for r in range(0, rows, tile):
        t = slice(r, r + tile)
        value, grad = gelu_both(dot(norm_low[t, :], w_in[...]))
        low = value.astype(bf16)
        act[t, :] = low
        out_sum[t, :] += dot(low, w_back[...])
        d_low = (dot_nt(grad_out[t, :], w_back[...]) * grad).astype(bf16)
        slope[t, :] = d_low
        d_norm[t, :] += dot_nt(d_low, w_in[...])
    back_grads = dot_tn(act[...], grad_out[...]).astype(bf16)
    in_grads = dot(norm_t[...], slope[...]).astype(bf16)
    if num_grads == 3:
        grad_refs[0][...] = back_grads
        grad_refs[1][...] = in_grads
    else:
        tmp[...] = back_grads
        share = tmp.shape[0] // 8
        for yr in range(2):
            for xr in range(2):
                for cr in range(2):
                    place = (xr ^ coords[1]) * 4 + (cr ^ coords[2]) * 2 + (yr ^ coords[3])
                    rows_from = pl.ds(pl.multiple_of(place * share, 16), share)
                    for half in range(2):
                        grad_refs[cr][yr, xr, 0, half * share : (half + 1) * share, :] = tmp[
                            rows_from, half * width // 2 : (half + 1) * width // 2
                        ]
        tmp[...] = in_grads
        side = (step // 2) ^ coords[3]
        for odd in range(2):

            @pl.when(step % 2 == odd)
            def _():
                for half in range(2):
                    halves_to_dests(
                        coords, tmp, half, grad_refs[2], grad_refs[3], odd * 2 + half, side
                    )

    @pl.when(step == steps - 1)
    def _():
        for r in range(0, rows, tile):
            t = slice(r, r + tile)
            value = hidden[t, :]
            output[t, :] = (value + out_sum[t, :]).astype(bf16)
            normed, inv = norm_stats(value)
            grad = d_norm[t, :]
            part_gain = jnp.sum(grad * normed, 0, keepdims=True)
            part_bias = jnp.sum(grad, 0, keepdims=True)
            if r == 0:
                gain_part[...] = part_gain
                bias_part[...] = part_bias
            else:
                gain_part[...] += part_gain
                bias_part[...] += part_bias
            hat = grad * gain[...]
            mean_hat = jnp.mean(hat, -1, keepdims=True)
            mean_dot = jnp.mean(hat * normed, -1, keepdims=True)
            total = grad_out[t, :].astype(f32) + inv * (hat - mean_hat - normed * mean_dot)
            d_hidden[t, :] = total
            low = total.astype(bf16)
            norm_low[t, :] = low
            d_context[t, :] = dot_nt(low, w_out[...]).astype(bf16)
        out_grads = dot_tn(context[...], norm_low[...]).astype(bf16)
        if num_grads == 3:
            grad_refs[2][...] = out_grads
        else:
            tmp[...] = out_grads
            for half in range(2):
                halves_to_dests(
                    coords, tmp, half, grad_refs[2], grad_refs[3], 4, half ^ coords[3]
                )


def hop(values, route):
    return lax.ppermute(values, "seq", route)


def swap(bit):
    return [(i, i ^ bit) for i in range(16)]


CORE, ACROSS = swap(1), swap(2)
NEAR, FAR = swap(4), swap(8)
UP = [(i, i + 4) for i in range(12)]
DOWN = [(i + 4, i) for i in range(12)]
UP_LATE = [(i, i + 4) for i in range(4, 12) if i % 4 != 0]
DOWN_LATE = [(i + 4, i) for i in range(8) if i % 4 != 3]
UP_EARLY = [(i, i + 4) for i in range(8) if i % 4 != 3]
DOWN_EARLY = [(i + 4, i) for i in range(4, 12) if i % 4 != 0]
FAR_IN = [(i, i ^ 2) for i in range(16) if (i >= 8) == bool(i & 2)]
FAR_OUT = [(i, i ^ 2) for i in range(16) if (i >= 8) != bool(i & 2)]


def tie(*values):
    return lax.optimization_barrier(values)


def after(mark, *values):
    return tie(mark, *values)[1:]


def gather_pieces(tok, coords, meanwhile):
    beside, below, above = hop(tok, ACROSS), hop(tok, UP), hop(tok, DOWN)
    s_tok = hop(tok, CORE)
    beside, below, above, s_tok, *done = tie(beside, below, above, s_tok, *meanwhile())
    below2, above2 = hop(below, UP_LATE), hop(above, DOWN_LATE)
    s_beside, s_below, s_above = [hop(v, CORE) for v in (beside, below, above)]
    below2, above2, s_beside, s_below, s_above, beside = tie(
        below2, above2, s_beside, s_below, s_above, beside
    )
    far = jnp.where(coords[0] >= 2, below2, above2)
    below_x, above_x, far_x = hop(beside, UP), hop(beside, DOWN), hop(far, FAR_IN)
    s_far = hop(far, CORE)
    below_x, above_x, far_x, s_far = tie(below_x, above_x, far_x, s_far)
    s_below_x, s_above_x, s_far_x = [hop(v, CORE) for v in (below_x, above_x, far_x)]
    pieces = [
        below, s_below, below_x, s_below_x, tok, s_tok, beside, s_beside,
        above, s_above, above_x, s_above_x, far, s_far, far_x, s_far_x,
    ]
    return pieces, done


def slot_codes(slots, per_dev, coords):
    owner, block = slots // per_dev, slots % per_dev
    z, x, core = owner // 4, (owner // 2) % 2, owner % 2
    level = jnp.where(jnp.abs(z - coords[0]) == 2, 3, z - coords[0] + 1)
    piece = level * 4 + (x ^ coords[1]) * 2 + (core ^ coords[2])
    return (piece * per_dev + block).astype(jnp.int32)


def scatter_kernel(codes, sib_codes, own, sib, *refs):
    outs, acc = refs[:-1], refs[-1]
    per_dev = outs[0].shape[0]
    acc[...] = jnp.zeros_like(acc)

    def add(s, _):
        for which, source, cls in ((codes, own, 0), (sib_codes, sib, 1)):
            piece, block = which[s] // per_dev, which[s] % per_dev

            @pl.when(piece % 2 == cls)
            def _():
                acc[(piece // 2) * per_dev + block] += source[s].astype(f32)

        return 0

    lax.fori_loop(0, own.shape[0], add, 0)
    for k, out in enumerate(outs):

        def store(b, _):
            out[b] = acc[k * per_dev + b].astype(bf16)
            return 0

        lax.fori_loop(0, per_dev, store, 0)


def plus(*values):
    total = values[0].astype(f32)
    for value in values[1:]:
        total = total + value.astype(f32)
    return total.astype(bf16)


def over_y(values):
    return lax.ppermute(values, "grp", [(0, 1), (1, 0)])


def split(keep, got, axis=0):
    pick = lambda v, n: v[n] if axis == 0 else v[:, n]
    return plus(pick(keep, 1), pick(got, 1)), plus(pick(keep, 0), pick(got, 0))


def by_pairs(values):
    return values.reshape((2, 2) + values.shape[1:])


def both_halves(mine, other):
    first = lax.axis_index("grp") == 0
    return jnp.stack([jnp.where(first, mine, other), jnp.where(first, other, mine)]).astype(f32)


def call(kernel, out_shape, in_specs, scratch, name, cost=COST, room=32):
    return pl.pallas_call(
        kernel,
        out_shape=out_shape,
        in_specs=in_specs,
        out_specs=[vmem()] * len(out_shape),
        scratch_shapes=scratch,
        compiler_params=pltpu.CompilerParams(vmem_limit_bytes=room * 1024 * 1024),
        cost_estimate=cost,
        name=name,
    )


def body(
    tokens, w_qkv, w_out, w_in, w_back, ln1_gain, ln1_bias, ln2_gain, ln2_bias,
    doc_units, tail_pad, global_ids, rand_blocks, out_grad,
):
    tok = tokens[0]
    grad_out = out_grad[0]
    rows, width = tok.shape
    ff = w_in.shape[1]
    per_dev = rows // BLK
    shards = lax.axis_size("seq")
    placed = shards == 16 and lax.axis_size("grp") == 2
    me = lax.axis_index("seq")
    first_row = me * per_dev
    coords = jnp.stack([me // 4, (me // 2) % 2, me % 2, lax.axis_index("grp")]).astype(jnp.int32)
    live, slots = block_plan(doc_units[0], tail_pad[0], global_ids[0], rand_blocks[0], first_row)
    count = slots.shape[0]
    gain1, bias1 = ln1_gain[None], ln1_bias[None]
    gain2, bias2 = ln2_gain[None], ln2_bias[None]

    def own_rows(codes, live):
        operands = tie(tok, codes, live)
        outs = call(
            own_kernel,
            [
                shape((rows, width), bf16), shape((rows, 2 * width), bf16),
                shape((rows, width), bf16), shape((rows, width), bf16),
            ],
            [vmem()] * 4,
            [],
            "own_rows", room=ROOM[0],
        )(operands[0], w_qkv, gain1, bias1)
        return list(outs) + list(operands[1:])

    if placed:
        codes = slot_codes(slots, per_dev, coords)
        pieces, done = gather_pieces(tok, coords, lambda: own_rows(codes, live))
        pieces = [p.reshape(per_dev, BLK, width) for p in pieces]
    else:
        pieces = [lax.all_gather(tok, "seq").reshape(shards * per_dev, BLK, width)]
        done = own_rows(slots, live)
    query, own_kv, own_norm, own_hat, codes, live = done

    quads = width // QW
    context, lse, slot_norm, slot_hat, slot_kv = call(
        functools.partial(forward_kernel, len(pieces)),
        [
            shape((rows, width), bf16),
            shape((per_dev, quads, QW), f32),
            shape((count * BLK, width), bf16),
            shape((count * BLK, width), bf16),
            shape((count * BLK, 2 * width), bf16),
        ],
        [smem(), smem()] + [hbm()] * len(pieces) + [vmem()] * 5,
        [
            pltpu.VMEM((count, BLK, width), bf16),
            pltpu.VMEM((rows + 2 * BLK, 2 * width), bf16),
            pltpu.SemaphoreType.DMA((count,)),
        ],
        "attend_forward",
        room=ROOM[1],
    )(codes, live, *pieces, query, own_kv, w_qkv, gain1, bias1)

    chunk = width
    steps = ff // chunk
    const = lambda *dims: pl.BlockSpec(dims, lambda s, c: (0,) * len(dims))
    if placed:
        back_half = (2, 2, 4, ff // 16, width // 2)
        rest_half = (2, 2, 4, 5 * (width // 16), width // 2)
        back_spec = pl.BlockSpec((2, 2, 1, ff // 16, width // 2), lambda s, c: (0, 0, s ^ c[0], 0, 0))
        grad_specs = [back_spec, back_spec, const(*rest_half), const(*rest_half)]
        grad_shapes = [shape(back_half, bf16)] * 2 + [shape(rest_half, bf16)] * 2
    else:
        grad_specs = [
            pl.BlockSpec((chunk, width), lambda s, c: (s, 0)),
            pl.BlockSpec((width, chunk), lambda s, c: (0, s)),
            const(width, width),
        ]
        grad_shapes = [
            shape((ff, width), bf16), shape((width, ff), bf16), shape((width, width), bf16),
        ]
    output, d_hidden, d_context, gain_two, bias_two, *grads = pl.pallas_call(
        functools.partial(middle_kernel, len(grad_specs)),
        grid_spec=pltpu.PrefetchScalarGridSpec(
            num_scalar_prefetch=1,
            grid=(steps,),
            in_specs=[
                const(rows, width), const(rows, width), const(rows, width), const(width, width),
                const(1, width), const(1, width),
                pl.BlockSpec((width, chunk), lambda s, c: (0, s)),
                pl.BlockSpec((chunk, width), lambda s, c: (s, 0)),
            ],
            out_specs=[
                const(rows, width), const(rows, width), const(rows, width),
                const(1, width), const(1, width), *grad_specs,
            ],
            scratch_shapes=[
                pltpu.VMEM((rows, width), f32), pltpu.VMEM((rows, width), bf16),
                pltpu.VMEM((width, rows), bf16), pltpu.VMEM((rows, width), f32),
                pltpu.VMEM((rows, width), f32), pltpu.VMEM((rows, chunk), bf16),
                pltpu.VMEM((rows, chunk), bf16), pltpu.VMEM((chunk, width), bf16),
            ],
        ),
        out_shape=[
            shape((rows, width), bf16), shape((rows, width), f32), shape((rows, width), bf16),
            shape((1, width), f32), shape((1, width), f32), *grad_shapes,
        ],
        compiler_params=pltpu.CompilerParams(vmem_limit_bytes=ROOM[2] * 1024 * 1024),
        cost_estimate=COST,
        name="middle",
    )(coords, tok, context, grad_out, w_out, gain2, bias2, w_in, w_back)

    share = width // shards
    parts_in = (query, d_context, own_kv, own_kv, slot_kv, slot_kv)

    def attend_back(parts, live, early):
        column = lambda n, j: pl.BlockSpec((n, QW), lambda i: (0, j))
        whole = lambda s: pl.BlockSpec(s.shape, lambda i: (0,) * len(s.shape))
        specs, operands, outs, held = [], [], [], []
        for part in parts:
            specs += [column(rows, part), column(rows, part)]
            specs += [column(rows, part), column(rows, part + quads)]
            specs += [column(count * BLK, part), column(count * BLK, part + quads)]
            operands += [query, d_context, own_kv, own_kv, slot_kv, slot_kv]
            outs += [
                shape((rows, QW), bf16), shape((rows, 2 * QW), bf16),
                shape((count * BLK, 2 * QW), bf16),
            ]
        scratch = [
            pltpu.VMEM((2 * len(parts), rows + 2 * BLK, QW), bf16),
            pltpu.VMEM((2 * len(parts), rows + 2 * BLK, QW), f32),
            pltpu.VMEM((2 * len(parts), 2 * BLK, QW), f32),
        ]
        kernel = functools.partial(first_backward_kernel, parts)
        if early is not None:
            held = [w_qkv, own_hat, slot_hat, *early]
            kernel = functools.partial(last_backward_kernel, parts, len(early) // 3)
            outs += [
                shape((rows, width), f32), shape((count * BLK, width), bf16),
                shape((1, width), f32), shape((1, width), f32),
            ]
            scratch += [pltpu.VMEM(v.shape, v.dtype) for v in held]
            scratch += [pltpu.SemaphoreType.DMA((len(held),))]
        return list(
            pl.pallas_call(
                kernel,
                grid=(1,),
                out_shape=outs,
                in_specs=[smem(), whole(lse)] + [anym()] * len(held) + specs,
                out_specs=[whole(o) for o in outs],
                scratch_shapes=scratch,
                compiler_params=pltpu.CompilerParams(
                    vmem_limit_bytes=ROOM[3 if early is None else 4] * 1024 * 1024
                ),
                cost_estimate=COST,
                name="attend_backward",
            )(live, lse, *held, *operands)
        )

    first = attend_back((0,), live, None)
    if placed:
        keep_a, send_a, keep_b, send_b = grads
        got_a, got_b = hop(send_a, CORE), hop(send_b, CORE)
        got_a, got_b, *first = tie(got_a, got_b, *first)
        out_a, mine_a = split(keep_a, got_a)
        sum_b = plus(keep_b, got_b)
        sum_b = sum_b.reshape((2, 2, 2, 2) + sum_b.shape[3:])
        out_b, mine_b = sum_b[:, :, :, 1], sum_b[:, :, :, 0]
        out_a, mine_a, out_b, mine_b, live, *first = tie(
            out_a, mine_a, out_b, mine_b, live, *first
        )
        got_a, got_b = over_y(out_a), hop(out_b, NEAR)
    rest = attend_back((1, 2), live, first)
    d_parts = first + rest[:6]
    d_own_norm, d_slot_norm, gain_one, bias_one = rest[6:]

    def qkv_grads(d_parts):
        if placed:
            shapes = [shape((2, 2, 4, 3 * share + 16, width // 2), bf16)] * 2
        else:
            shapes = [shape((width, 3 * width), bf16)]
        return call(
            functools.partial(qkv_grad_kernel, len(shapes)),
            shapes,
            [smem()] + [vmem()] * (6 + 3 * quads),
            [pltpu.VMEM((width, width), bf16)],
            "qkv_grads",
            room=ROOM[5],
        )(coords, gain_one, bias_one, gain_two, bias_two, own_norm, slot_norm, *d_parts)

    def token_grads(d_norm1):
        normed_one, inv_one = norm_stats(tok.astype(f32))
        grad_hat = d_norm1 * ln1_gain
        d_first = inv_one * (
            grad_hat
            - jnp.mean(grad_hat, -1, keepdims=True)
            - normed_one * jnp.mean(grad_hat * normed_one, -1, keepdims=True)
        )
        return (d_hidden + d_first).astype(bf16)

    if placed:
        d_slot_norm = d_slot_norm.reshape(count, BLK, width)
        sib_codes = hop(codes, CORE)
        sib_norm = hop(d_slot_norm, CORE)
        got_a, got_b, d_slot_norm, *d_parts = tie(got_a, got_b, d_slot_norm, *d_parts)
        sum_a = plus(mine_a, got_a)
        sum_a = sum_a.reshape((2, 2, 2) + sum_a.shape[2:])
        out_a, mine_a = sum_a[:, :, 1], sum_a[:, :, 0]
        out_b, mine_b = split(mine_b, got_b, 1)
        out_a, mine_a, out_b, mine_b, *d_parts = tie(out_a, mine_a, out_b, mine_b, *d_parts)
        got_a, got_b = hop(out_a, NEAR), hop(out_b, ACROSS)
        keep_c, send_c = qkv_grads(d_parts)
        keep_c, send_c, sib_norm = tie(keep_c, send_c, sib_norm)
        got_c = hop(send_c, CORE)
        piece_shape = shape((per_dev, BLK, width), bf16)
        sums = call(
            scatter_kernel,
            [piece_shape] * 8,
            [smem(), smem(), vmem(), vmem()],
            [pltpu.VMEM((8 * per_dev, BLK, width), f32)],
            "scatter_slots",
            room=ROOM[6],
        )(codes, sib_codes, d_slot_norm, sib_norm)
        below, below_x, own, beside, above, above_x, far, far_x = [
            p.reshape(rows, width) for p in sums
        ]
        from_above_x, from_below_x = hop(below_x, DOWN), hop(above_x, UP)
        in_far = hop(far_x, FAR_OUT)
        mine_a, got_a, mine_b, got_b = after(own, mine_a, got_a, mine_b, got_b)
        out_a, mine_a = split(mine_a, got_a)
        out_b, mine_b = split(mine_b, got_b)
        got_a, got_b = hop(out_a, ACROSS), over_y(out_b)
        keep_c, got_c = after(mine_b, keep_c, got_c)
        out_c, mine_c = split(keep_c, got_c)
        got_c = over_y(out_c)
        mine_a, got_a, mine_b, got_b = after(mine_c, mine_a, got_a, mine_b, got_b)
        sum_ab = jnp.concatenate([plus(mine_a, got_a), plus(mine_b, got_b)], 1)
        out_ab, mine_ab = sum_ab[1], sum_ab[0]
        in_far, from_above_x, from_below_x = after(mine_ab, in_far, from_above_x, from_below_x)
        far = plus(far, in_far)
        beside = plus(beside, from_above_x, from_below_x)
        from_above2, from_below2 = hop(far, DOWN_EARLY), hop(far, UP_EARLY)
        from_beside = hop(beside, ACROSS)
        got_ab = hop(*after(beside, out_ab), FAR)
        mine_c, got_c = after(beside, mine_c, got_c)
        out_c, mine_c = split(mine_c, got_c)
        got_c = hop(out_c, ACROSS)
        mine_ab, got_ab = after(mine_c, mine_ab, got_ab)
        mine_ab = plus(mine_ab, got_ab)
        other_ab = over_y(mine_ab)
        from_above2, from_below2 = after(mine_ab, from_above2, from_below2)
        below, above = plus(below, from_above2), plus(above, from_below2)
        from_above, from_below = hop(below, DOWN), hop(above, UP)
        mine_c, got_c = after(above, mine_c, got_c)
        sum_c = by_pairs(plus(mine_c, got_c))
        out_c, mine_c = sum_c[:, 1], sum_c[:, 0]
        got_c = hop(out_c, NEAR)
        half = width // 2
        back_rows = ff // 16
        halves_ab = both_halves(*after(mine_c, mine_ab, other_ab))
        back_grad = halves_ab[:, :back_rows].reshape(2, 2, back_rows // 2, half)
        back_grad = back_grad.transpose(0, 2, 1, 3).reshape(back_rows, width)
        rest = halves_ab[:, back_rows:].reshape(2, 5, share, half)
        in_grad = rest[:, :4].reshape(8, share, half).transpose(1, 0, 2).reshape(share, ff)
        out_proj_grad = rest[:, 4].transpose(1, 0, 2).reshape(share, width)
        mine_c, got_c = after(back_grad, mine_c, got_c)
        mine_c = plus(mine_c, got_c)
        got_c = hop(mine_c[1], FAR)
        parts = after(mine_c, own, from_beside, from_above, from_below)
        d_norm1 = d_own_norm
        for part in parts:
            d_norm1 = d_norm1 + part.astype(f32)
        tokens_grad = token_grads(d_norm1)
        mine_c, got_c = after(tokens_grad, mine_c, got_c)
        mine_c = plus(mine_c[0], got_c)
        halves_c = both_halves(mine_c, over_y(mine_c))
        qkv_grad = halves_c[:, : 3 * share].reshape(6, share, half).transpose(1, 0, 2)
        qkv_grad = qkv_grad.reshape(share, 3 * width)
        vectors = halves_c[0, 3 * share : 3 * share + 8].reshape(4, width)
        vectors = lax.dynamic_slice_in_dim(vectors, me * share, share, 1)
    else:
        spread_grads = jnp.zeros((shards * per_dev, BLK, width), f32)
        spread_grads = spread_grads.at[slots].add(
            d_slot_norm.reshape(count, BLK, width).astype(f32)
        )
        others = lax.psum_scatter(
            spread_grads.astype(bf16).reshape(shards * rows, width),
            "seq", scatter_dimension=0, tiled=True,
        )
        tokens_grad = token_grads(d_own_norm + others.astype(f32))

        def reduce(part):
            mine = lax.psum_scatter(part, "seq", scatter_dimension=0, tiled=True)
            return lax.psum(mine, "grp").astype(f32)

        back_grad, in_grad, out_proj_grad = [reduce(g) for g in grads]
        qkv_grad = reduce(qkv_grads(d_parts)[0])
        vectors = jnp.concatenate([gain_one, bias_one, gain_two, bias_two])
        vectors = lax.psum(vectors, ("seq", "grp"))
        vectors = lax.dynamic_slice_in_dim(vectors, me * share, share, 1)
    return (
        output[None],
        tokens_grad[None],
        qkv_grad,
        out_proj_grad,
        in_grad,
        back_grad,
        vectors[0],
        vectors[1],
        vectors[2],
        vectors[3],
    )


def solution(mesh):
    in_specs = (
        P("grp", "seq", None),
        P(),
        P(),
        P(),
        P(),
        P(),
        P(),
        P(),
        P(),
        P("grp", None),
        P("grp", None),
        P("grp", None, None),
        P("grp", "seq", None),
        P("grp", "seq", None),
    )
    out_specs = (
        P("grp", "seq", None),
        P("grp", "seq", None),
        P("seq", None),
        P("seq", None),
        P("seq", None),
        P("seq", None),
        P("seq"),
        P("seq"),
        P("seq"),
        P("seq"),
    )
    return jax.shard_map(body, mesh=mesh, in_specs=in_specs, out_specs=out_specs, check_vma=False)
```

```python
import functools

import jax
import jax.numpy as jnp
from jax import lax
from jax.experimental import pallas as pl
from jax.experimental.pallas import tpu as pltpu
from jax.sharding import PartitionSpec as P

HD = 64
BLK = 64
UNITB = 8
QUAD = 4
QW = QUAD * HD
ln_eps = 1e-12
bf16 = jnp.bfloat16
f32 = jnp.float32
ROOM = (12, 56, 40, 14, 36, 22, 24)
BRIEF = pl.CostEstimate(flops=1_000_000, bytes_accessed=1, transcendentals=0)
COST = pl.CostEstimate(flops=40_000_000_000, bytes_accessed=1, transcendentals=0)
vmem = functools.partial(pl.BlockSpec, memory_space=pltpu.VMEM)
smem = functools.partial(pl.BlockSpec, memory_space=pltpu.SMEM)
anym = functools.partial(pl.BlockSpec, memory_space=pl.ANY)
hbm = functools.partial(pl.BlockSpec, memory_space=pltpu.HBM)


def shape(dims, dtype):
    return jax.ShapeDtypeStruct(dims, dtype)


def dot(a, b):
    return lax.dot_general(a, b, (((1,), (0,)), ((), ())), preferred_element_type=f32)


def dot_nt(a, b):
    return lax.dot_general(a, b, (((1,), (1,)), ((), ())), preferred_element_type=f32)


def dot_tn(a, b):
    return lax.dot_general(a, b, (((0,), (0,)), ((), ())), preferred_element_type=f32)


def norm_stats(values):
    center = values - jnp.mean(values, -1, keepdims=True)
    inv_std = lax.rsqrt(jnp.mean(center * center, -1, keepdims=True) + ln_eps)
    return center * inv_std, inv_std


def block_plan(doc_len, tail_len, global_rel, rand_rows, first_row):
    per_dev = rand_rows.shape[0]
    doc_end = jnp.cumsum(doc_len) * UNITB
    starts = doc_end - doc_len * UNITB
    mine = ((first_row >= starts) & (first_row < doc_end)).astype(jnp.int32)
    begin = jnp.sum(mine * starts)
    finish = jnp.sum(mine * doc_end)
    padding = jnp.sum(mine * tail_len)
    glob_one = begin + jnp.sum(mine * global_rel[:, 0])
    glob_two = begin + jnp.sum(mine * global_rel[:, 1])
    rows = first_row + jnp.arange(per_dev, dtype=jnp.int32)
    before = jnp.where(rows - 1 >= begin, rows - 1, -1)
    follow = jnp.where(rows + 1 < finish, rows + 1, -1)
    whole = jnp.zeros_like(rows)
    candidates = jnp.concatenate(
        [jnp.stack([before, rows, follow, whole + glob_one, whole + glob_two], 1), rand_rows], 1
    )
    count = candidates.shape[1]
    equal = candidates[:, :, None] == candidates[:, None, :]
    earlier = jnp.arange(count)[:, None] > jnp.arange(count)[None, :]
    usable = (candidates >= 0) & jnp.logical_not(jnp.any(equal & earlier[None], 2))
    filled = jnp.where(candidates == finish - 1, BLK - padding, BLK)
    live = jnp.where(usable, filled, 0).astype(jnp.int32)
    halo = jnp.stack(
        [
            jnp.where(first_row - 1 >= begin, first_row - 1, first_row),
            jnp.where(first_row + per_dev < finish, first_row + per_dev, first_row),
            glob_one,
            glob_two,
        ]
    )
    slots = jnp.concatenate([halo, rand_rows.reshape(-1)]).astype(jnp.int32)
    return live.reshape(-1), slots


def head_masks(rows):
    lane = lax.broadcasted_iota(jnp.int32, (rows, QW), 1) // HD
    return [lane == h for h in range(QUAD)]


def spread(values, masks):
    zero = jnp.zeros_like(values)
    return jnp.concatenate([jnp.where(m, values, zero) for m in masks], 0)


def collect(values, masks):
    out = values[:BLK]
    for h in range(1, QUAD):
        out = jnp.where(masks[h], values[h * BLK : (h + 1) * BLK], out)
    return out


def key_rows(ext, slots, i, cols):
    return jnp.concatenate(
        [
            ext[pl.ds(pl.multiple_of(i * BLK, BLK), 3 * BLK), cols],
            slots[2 * BLK : 4 * BLK, cols],
            slots[pl.ds(pl.multiple_of((4 + 3 * i) * BLK, BLK), 3 * BLK), cols],
        ],
        0,
    )


def masked(scores, live, i, cand):
    row = lax.broadcasted_iota(jnp.int32, (BLK, QW), 0)
    return jnp.concatenate(
        [
            jnp.where(row < live[i * cand + c], scores[c * BLK : (c + 1) * BLK], -1e30)
            for c in range(cand)
        ],
        0,
    )


def fill_ext(ext, own, slots):
    rows = own.shape[0]
    ext[0:BLK, :] = slots[0:BLK, :]
    ext[BLK : BLK + rows, :] = own[...]
    ext[BLK + rows : 2 * BLK + rows, :] = slots[BLK : 2 * BLK, :]


def own_kernel(tokens, w_qkv, gain, bias, query, own_kv, own_norm, own_hat):
    rows, width = tokens.shape
    tile = 128
    for r in range(0, rows, tile):
        t = slice(r, r + tile)
        normed, _ = norm_stats(tokens[t, :].astype(f32))
        own_hat[t, :] = normed.astype(bf16)
        low = (normed * gain[...] + bias[...]).astype(bf16)
        own_norm[t, :] = low
        query[t, :] = (dot(low, w_qkv[:, :width]) * HD**-0.5).astype(bf16)
        own_kv[t, :] = dot(low, w_qkv[:, width:]).astype(bf16)


def forward_kernel(num_pieces, codes, live, gain, bias, *refs):
    pieces, refs = refs[:num_pieces], refs[num_pieces:]
    query_hbm, own_hbm, w_hbm, context, lse, hat_hbm, kv_hbm = refs[:7]
    slot_tok, ext, query, w_kv, slot_hat, slot_kv, sems, in_sems, out_sems = refs[7:]
    count = slot_tok.shape[0]
    per_piece = pieces[0].shape[0]
    rows_own, width = query.shape
    nblk = rows_own // BLK
    cand = live.shape[0] // nblk
    group = 4

    def fetch(s, piece, block):
        return pltpu.make_async_copy(piece.at[block], slot_tok.at[s], sems.at[s])

    def start(s, _):
        which, block = codes[s] // per_piece, codes[s] % per_piece
        for k, piece in enumerate(pieces):

            @pl.when(which == k)
            def _():
                fetch(s, piece, block).start()

        return 0

    ins = [
        pltpu.make_async_copy(w_hbm.at[:, pl.ds(width, 2 * width)], w_kv, in_sems.at[0]),
        pltpu.make_async_copy(own_hbm, ext.at[pl.ds(BLK, rows_own)], in_sems.at[1]),
        pltpu.make_async_copy(query_hbm, query, in_sems.at[2]),
    ]

    def outs(step):
        rows = pl.ds(pl.multiple_of(step * group * BLK, group * BLK), group * BLK)
        return rows, [
            pltpu.make_async_copy(slot_hat.at[rows], hat_hbm.at[rows], out_sems.at[step, 0]),
            pltpu.make_async_copy(slot_kv.at[rows], kv_hbm.at[rows], out_sems.at[step, 1]),
        ]

    ins[0].start()
    lax.fori_loop(0, count, start, 0)
    ins[1].start()
    ins[2].start()
    ins[0].wait()

    def project(step, _):
        for k in range(group):
            fetch(step * group + k, pieces[0], 0).wait()
        rows, copies = outs(step)
        tok = slot_tok[pl.ds(step * group, group)].reshape(group * BLK, width).astype(f32)
        normed, _ = norm_stats(tok)
        slot_hat[rows, :] = normed.astype(bf16)
        low = (normed * gain[...] + bias[...]).astype(bf16)
        slot_kv[rows, :] = dot(low, w_kv[...]).astype(bf16)
        for copy in copies:
            copy.start()
        return 0

    lax.fori_loop(0, count // group, project, 0)
    ins[1].wait()
    ins[2].wait()
    ext[0:BLK, :] = slot_kv[0:BLK, :]
    ext[BLK + rows_own :, :] = slot_kv[BLK : 2 * BLK, :]
    masks = head_masks(BLK)

    def attend(i, _):
        qrows = pl.ds(pl.multiple_of(i * BLK, BLK), BLK)
        for quad in range(width // QW):
            cols = pl.ds(quad * QW, QW)
            vcols = pl.ds(width + quad * QW, QW)
            keys = key_rows(ext, slot_kv, i, cols)
            vals = key_rows(ext, slot_kv, i, vcols)
            scores = masked(dot_nt(keys, spread(query[qrows, cols], masks)), live, i, cand)
            top = jnp.max(scores, 0, keepdims=True)
            expo = jnp.exp(scores - top)
            total = jnp.sum(expo, 0, keepdims=True)
            probs = (expo * (1.0 / total)).astype(bf16)
            lse[i, pl.ds(quad, 1), :] = top + jnp.log(total)
            context[qrows, cols] = collect(dot_tn(probs, vals), masks).astype(bf16)
        return 0

    lax.fori_loop(0, nblk, attend, 0, unroll=True)

    def finish(step, _):
        for copy in outs(step)[1]:
            copy.wait()
        return 0

    lax.fori_loop(0, count // group, finish, 0)


def attend_back_parts(parts, live, lse, ins, outs, ext, d_ext, d_glob):
    rows_own = ins[0].shape[0]
    nblk = rows_own // BLK
    cand = live.shape[0] // nblk
    d_ext[...] = jnp.zeros_like(d_ext)
    d_glob[...] = jnp.zeros_like(d_glob)
    masks = head_masks(BLK)
    for n in range(len(parts)):
        for kv in range(2):
            own, slots = ins[6 * n + 2 + kv], ins[6 * n + 4 + kv]
            fill_ext(ext.at[2 * n + kv], own, slots)

    def attend(i, _):
        qrows = pl.ds(pl.multiple_of(i * BLK, BLK), BLK)
        near = pl.ds(pl.multiple_of(i * BLK, BLK), 3 * BLK)
        far = pl.ds(pl.multiple_of((4 + 3 * i) * BLK, BLK), 3 * BLK)
        every = pl.ds(0, QW)
        for n, part in enumerate(parts):
            query, d_context, _, _, slot_k, slot_v = ins[6 * n : 6 * n + 6]
            d_query, _, d_slot = outs[3 * n : 3 * n + 3]
            keys = key_rows(ext.at[2 * n], slot_k, i, every)
            vals = key_rows(ext.at[2 * n + 1], slot_v, i, every)
            spread_q = spread(query[qrows, :], masks)
            spread_d = spread(d_context[qrows, :], masks)
            scores = masked(dot_nt(keys, spread_q), live, i, cand)
            probs = jnp.exp(scores - lse[i, pl.ds(part, 1), :])
            d_probs = dot_nt(vals, spread_d)
            delta = jnp.sum(d_probs * probs, 0, keepdims=True)
            d_scores = (probs * (d_probs - delta)).astype(bf16)
            d_keys = dot(d_scores, spread_q)
            d_vals = dot(probs.astype(bf16), spread_d)
            d_query[qrows, :] = (collect(dot_tn(d_scores, keys), masks) * HD**-0.5).astype(bf16)
            for kv, grads in enumerate((d_keys, d_vals)):
                d_ext[2 * n + kv, near, :] += grads[: 3 * BLK]
                d_glob[2 * n + kv] += grads[3 * BLK : 5 * BLK]
                d_slot[far, kv * QW : (kv + 1) * QW] = grads[5 * BLK :].astype(bf16)
        return 0

    lax.fori_loop(0, nblk, attend, 0, unroll=4 // len(parts))
    for n in range(len(parts)):
        _, d_own, d_slot = outs[3 * n : 3 * n + 3]
        for kv in range(2):
            cols = slice(kv * QW, (kv + 1) * QW)
            d_slot[0:BLK, cols] = d_ext[2 * n + kv, 0:BLK, :].astype(bf16)
            d_slot[BLK : 2 * BLK, cols] = d_ext[2 * n + kv, BLK + rows_own :, :].astype(bf16)
            d_slot[2 * BLK : 4 * BLK, cols] = d_glob[2 * n + kv].astype(bf16)
            d_own[:, cols] = d_ext[2 * n + kv, BLK : BLK + rows_own, :].astype(bf16)


def first_backward_kernel(parts, live, lse, *refs):
    count = len(parts)
    ins, outs, scratch = refs[: 6 * count], refs[6 * count : 9 * count], refs[9 * count :]
    attend_back_parts(parts, live, lse, ins, outs, *scratch)


def joined(refs, rows):
    return jnp.concatenate(
        [r[rows, kv * QW : (kv + 1) * QW] for kv in range(2) for r in refs], 1
    )


def last_backward_kernel(parts, early, live, lse, *refs):
    count = len(parts)
    late = 3 + 3 * early
    held_hbm, refs = refs[:late], refs[late:]
    ins, outs, refs = refs[: 6 * count], refs[6 * count : 9 * count], refs[9 * count :]
    (d_own_norm, d_slot_norm, gain_part, bias_part), refs = refs[:4], refs[4:]
    scratch, held, sems = refs[:3], refs[3:-1], refs[-1]
    copies = [
        pltpu.make_async_copy(src, dst, sems.at[n])
        for n, (src, dst) in enumerate(zip(held_hbm, held))
    ]
    for copy in copies:
        copy.start()
    attend_back_parts(parts, live, lse, ins, outs, *scratch)
    for copy in copies:
        copy.wait()
    w_qkv, own_hat, slot_hat = held[:3]
    grads_in = held[3:] + outs
    d_query, d_own, d_slot = grads_in[0::3], grads_in[1::3], grads_in[2::3]
    rows_own, width = d_own_norm.shape
    step_rows = 4 * BLK

    def add(grads, hat, first):
        gain = jnp.sum(grads * hat.astype(f32), 0, keepdims=True)
        bias = jnp.sum(grads, 0, keepdims=True)
        if first:
            gain_part[...], bias_part[...] = gain, bias
        else:
            gain_part[...] += gain
            bias_part[...] += bias

    for r in range(0, rows_own, step_rows):
        rows = slice(r, r + step_rows)
        grads = dot_nt(jnp.concatenate([d[rows, :] for d in d_query], 1), w_qkv[:, :width])
        grads += dot_nt(joined(d_own, rows), w_qkv[:, width:])
        d_own_norm[rows, :] = grads
        add(grads, own_hat[rows, :], r == 0)

    half_rows = d_slot_norm.shape[0] // 2

    def back(step, _):
        rows = pl.ds(pl.multiple_of(step * half_rows, BLK), half_rows)
        grads = dot_nt(joined(d_slot, rows), w_qkv[:, width:])
        d_slot_norm[rows, :] = grads.astype(bf16)
        add(grads, slot_hat[rows, :], False)
        return 0

    lax.fori_loop(0, 2, back, 0)


def halves_to_dests(coords, grads, half, keep, send, slot, side):
    share = grads.shape[0] // 16
    for zr in range(4):
        for xr in range(2):
            for cr, target in ((0, keep), (1, send)):
                dest = (zr ^ coords[0]) * 4 + (xr ^ coords[1]) * 2 + (cr ^ coords[2])
                rows = pl.ds(pl.multiple_of(dest * share, 16), share)
                target[side, xr, zr, slot * share : (slot + 1) * share, :] = grads[
                    rows, half * 384 : (half + 1) * 384
                ]


def qkv_grad_kernel(
    num_out, coords, gain1, bias1, gain2, bias2, gain, bias, own_norm, slot_hat, *refs
):
    ins, outs, tmp, slot_norm = refs[: -2 - num_out], refs[-2 - num_out : -2], refs[-2], refs[-1]
    for r in range(0, slot_norm.shape[0], 2 * BLK):
        rows = slice(r, r + 2 * BLK)
        normed = slot_hat[rows, :].astype(f32)
        slot_norm[rows, :] = (normed * gain[...] + bias[...]).astype(bf16)
    d_query, d_own, d_slot = ins[0::3], ins[1::3], ins[2::3]
    width = own_norm.shape[1]
    whole = slice(None)
    for part in range(3):
        if part == 0:
            grads = dot_tn(own_norm[...], jnp.concatenate([d[...] for d in d_query], 1))
        else:
            cols = slice((part - 1) * QW, part * QW)
            grads = dot_tn(own_norm[...], jnp.concatenate([d[:, cols] for d in d_own], 1))
            grads += dot_tn(slot_norm[...], jnp.concatenate([d[:, cols] for d in d_slot], 1))
        if num_out == 1:
            outs[0][:, part * width : (part + 1) * width] = grads.astype(bf16)
        else:
            tmp[...] = grads.astype(bf16)
            for half in range(2):
                piece = part * 2 + half
                side = (piece // 3) ^ coords[3]
                halves_to_dests(coords, tmp, half, outs[0], outs[1], piece % 3, side)
    if num_out == 2:
        half = width // 2
        lines = [v[:, h * half : (h + 1) * half] for v in (gain1, bias1, gain2, bias2) for h in (0, 1)]
        block = jnp.concatenate(lines + [jnp.zeros((8, half), f32)], 0).astype(bf16)
        rows = slice(outs[0].shape[3] - 16, outs[0].shape[3])
        for out in outs:
            for side in range(2):
                for xr in range(2):
                    for zr in range(4):
                        out[side, xr, zr, rows, :] = block


def gelu_both(x):
    half_erf = 0.5 * lax.erf(x * 0.7071067811865476)
    cdf = 0.5 + half_erf
    density = jnp.exp(-0.5 * x * x) * 0.3989422804014327
    return x * cdf, cdf + x * density


def middle_kernel(
    num_grads, coords, tokens, context, grad_out, w_out, gain, bias, w_in, w_back,
    output, d_hidden, d_context, gain_part, bias_part, *refs,
):
    grad_refs, refs = refs[:num_grads], refs[num_grads:]
    hidden, norm_low, norm_t, out_sum, d_norm, act, slope, tmp = refs
    step, steps = pl.program_id(0), pl.num_programs(0)
    rows, width = hidden.shape
    tile = 256

    @pl.when(step == 0)
    def _():
        for r in range(0, rows, tile):
            t = slice(r, r + tile)
            value = tokens[t, :].astype(f32) + dot(context[t, :], w_out[...])
            hidden[t, :] = value
            normed, _ = norm_stats(value)
            norm_low[t, :] = (normed * gain[...] + bias[...]).astype(bf16)
        norm_t[...] = norm_low[...].T
        out_sum[...] = jnp.zeros_like(out_sum)
        d_norm[...] = jnp.zeros_like(d_norm)

    for r in range(0, rows, tile):
        t = slice(r, r + tile)
        value, grad = gelu_both(dot(norm_low[t, :], w_in[...]))
        low = value.astype(bf16)
        act[t, :] = low
        out_sum[t, :] += dot(low, w_back[...])
        d_low = (dot_nt(grad_out[t, :], w_back[...]) * grad).astype(bf16)
        slope[t, :] = d_low
        d_norm[t, :] += dot_nt(d_low, w_in[...])
    back_grads = dot_tn(act[...], grad_out[...]).astype(bf16)
    in_grads = dot(norm_t[...], slope[...]).astype(bf16)
    if num_grads == 3:
        grad_refs[0][...] = back_grads
        grad_refs[1][...] = in_grads
    else:
        tmp[...] = back_grads
        share = tmp.shape[0] // 8
        for yr in range(2):
            for xr in range(2):
                for cr in range(2):
                    place = (xr ^ coords[1]) * 4 + (cr ^ coords[2]) * 2 + (yr ^ coords[3])
                    rows_from = pl.ds(pl.multiple_of(place * share, 16), share)
                    for half in range(2):
                        grad_refs[cr][yr, xr, 0, half * share : (half + 1) * share, :] = tmp[
                            rows_from, half * width // 2 : (half + 1) * width // 2
                        ]
        tmp[...] = in_grads
        side = (step // 2) ^ coords[3]
        for odd in range(2):

            @pl.when(step % 2 == odd)
            def _():
                for half in range(2):
                    halves_to_dests(
                        coords, tmp, half, grad_refs[2], grad_refs[3], odd * 2 + half, side
                    )

    @pl.when(step == steps - 1)
    def _():
        for r in range(0, rows, tile):
            t = slice(r, r + tile)
            value = hidden[t, :]
            output[t, :] = (value + out_sum[t, :]).astype(bf16)
            normed, inv = norm_stats(value)
            grad = d_norm[t, :]
            part_gain = jnp.sum(grad * normed, 0, keepdims=True)
            part_bias = jnp.sum(grad, 0, keepdims=True)
            if r == 0:
                gain_part[...] = part_gain
                bias_part[...] = part_bias
            else:
                gain_part[...] += part_gain
                bias_part[...] += part_bias
            hat = grad * gain[...]
            mean_hat = jnp.mean(hat, -1, keepdims=True)
            mean_dot = jnp.mean(hat * normed, -1, keepdims=True)
            total = grad_out[t, :].astype(f32) + inv * (hat - mean_hat - normed * mean_dot)
            d_hidden[t, :] = total
            low = total.astype(bf16)
            norm_low[t, :] = low
            d_context[t, :] = dot_nt(low, w_out[...]).astype(bf16)
        out_grads = dot_tn(context[...], norm_low[...]).astype(bf16)
        if num_grads == 3:
            grad_refs[2][...] = out_grads
        else:
            tmp[...] = out_grads
            for half in range(2):
                halves_to_dests(
                    coords, tmp, half, grad_refs[2], grad_refs[3], 4, half ^ coords[3]
                )


def hop(values, route):
    return lax.ppermute(values, "seq", route)


def swap(bit):
    return [(i, i ^ bit) for i in range(16)]


CORE, ACROSS = swap(1), swap(2)
NEAR, FAR = swap(4), swap(8)
UP = [(i, i + 4) for i in range(12)]
DOWN = [(i + 4, i) for i in range(12)]
UP_LATE = [(i, i + 4) for i in range(4, 12) if i % 4 != 0]
DOWN_LATE = [(i + 4, i) for i in range(8) if i % 4 != 3]
UP_EARLY = [(i, i + 4) for i in range(8) if i % 4 != 3]
DOWN_EARLY = [(i + 4, i) for i in range(4, 12) if i % 4 != 0]
FAR_IN = [(i, i ^ 2) for i in range(16) if (i >= 8) == bool(i & 2)]
FAR_OUT = [(i, i ^ 2) for i in range(16) if (i >= 8) != bool(i & 2)]


def tie(*values):
    return lax.optimization_barrier(values)


def after(mark, *values):
    return tie(mark, *values)[1:]


def gather_pieces(tok, coords, meanwhile):
    beside, below, above = hop(tok, ACROSS), hop(tok, UP), hop(tok, DOWN)
    s_tok = hop(tok, CORE)
    beside, below, above, s_tok, *done = tie(beside, below, above, s_tok, *meanwhile())
    below2, above2 = hop(below, UP_LATE), hop(above, DOWN_LATE)
    s_beside, s_below, s_above = [hop(v, CORE) for v in (beside, below, above)]
    below2, above2, s_beside, s_below, s_above, beside = tie(
        below2, above2, s_beside, s_below, s_above, beside
    )
    far = jnp.where(coords[0] >= 2, below2, above2)
    below_x, above_x, far_x = hop(beside, UP), hop(beside, DOWN), hop(far, FAR_IN)
    s_far = hop(far, CORE)
    below_x, above_x, far_x, s_far = tie(below_x, above_x, far_x, s_far)
    s_below_x, s_above_x, s_far_x = [hop(v, CORE) for v in (below_x, above_x, far_x)]
    pieces = [
        below, s_below, below_x, s_below_x, tok, s_tok, beside, s_beside,
        above, s_above, above_x, s_above_x, far, s_far, far_x, s_far_x,
    ]
    return pieces, done


def slot_codes(slots, per_dev, coords):
    owner, block = slots // per_dev, slots % per_dev
    z, x, core = owner // 4, (owner // 2) % 2, owner % 2
    level = jnp.where(jnp.abs(z - coords[0]) == 2, 3, z - coords[0] + 1)
    piece = level * 4 + (x ^ coords[1]) * 2 + (core ^ coords[2])
    return (piece * per_dev + block).astype(jnp.int32)


def scatter_kernel(codes, sib_codes, own, sib, *refs):
    outs, acc = refs[:-1], refs[-1]
    per_dev = outs[0].shape[0]
    acc[...] = jnp.zeros_like(acc)

    def add(s, _):
        for which, source, cls in ((codes, own, 0), (sib_codes, sib, 1)):
            piece, block = which[s] // per_dev, which[s] % per_dev

            @pl.when(piece % 2 == cls)
            def _():
                acc[(piece // 2) * per_dev + block] += source[s].astype(f32)

        return 0

    lax.fori_loop(0, own.shape[0], add, 0)
    for k, out in enumerate(outs):

        def store(b, _):
            out[b] = acc[k * per_dev + b].astype(bf16)
            return 0

        lax.fori_loop(0, per_dev, store, 0)


def plus(*values):
    total = values[0].astype(f32)
    for value in values[1:]:
        total = total + value.astype(f32)
    return total.astype(bf16)


def over_y(values):
    return lax.ppermute(values, "grp", [(0, 1), (1, 0)])


def split(keep, got, axis=0):
    pick = lambda v, n: v[n] if axis == 0 else v[:, n]
    return plus(pick(keep, 1), pick(got, 1)), plus(pick(keep, 0), pick(got, 0))


def by_pairs(values):
    return values.reshape((2, 2) + values.shape[1:])


def both_halves(mine, other):
    first = lax.axis_index("grp") == 0
    return jnp.stack([jnp.where(first, mine, other), jnp.where(first, other, mine)]).astype(f32)


def call(kernel, out_shape, in_specs, scratch, name, cost=COST, room=32, out_specs=None):
    return pl.pallas_call(
        kernel,
        out_shape=out_shape,
        in_specs=in_specs,
        out_specs=out_specs or [vmem()] * len(out_shape),
        scratch_shapes=scratch,
        compiler_params=pltpu.CompilerParams(vmem_limit_bytes=room * 1024 * 1024),
        cost_estimate=cost,
        name=name,
    )


def body(
    tokens, w_qkv, w_out, w_in, w_back, ln1_gain, ln1_bias, ln2_gain, ln2_bias,
    doc_units, tail_pad, global_ids, rand_blocks, out_grad,
):
    tok = tokens[0]
    grad_out = out_grad[0]
    rows, width = tok.shape
    ff = w_in.shape[1]
    per_dev = rows // BLK
    shards = lax.axis_size("seq")
    placed = shards == 16 and lax.axis_size("grp") == 2
    me = lax.axis_index("seq")
    first_row = me * per_dev
    coords = jnp.stack([me // 4, (me // 2) % 2, me % 2, lax.axis_index("grp")]).astype(jnp.int32)
    live, slots = block_plan(doc_units[0], tail_pad[0], global_ids[0], rand_blocks[0], first_row)
    count = slots.shape[0]
    gain1, bias1 = ln1_gain[None], ln1_bias[None]
    gain2, bias2 = ln2_gain[None], ln2_bias[None]

    def own_rows(codes, live):
        operands = tie(tok, codes, live)
        outs = call(
            own_kernel,
            [
                shape((rows, width), bf16), shape((rows, 2 * width), bf16),
                shape((rows, width), bf16), shape((rows, width), bf16),
            ],
            [vmem()] * 4,
            [],
            "own_rows", room=ROOM[0],
        )(operands[0], w_qkv, gain1, bias1)
        return list(outs) + list(operands[1:])

    if placed:
        codes = slot_codes(slots, per_dev, coords)
        pieces, done = gather_pieces(tok, coords, lambda: own_rows(codes, live))
        pieces = [p.reshape(per_dev, BLK, width) for p in pieces]
    else:
        pieces = [lax.all_gather(tok, "seq").reshape(shards * per_dev, BLK, width)]
        done = own_rows(slots, live)
    query, own_kv, own_norm, own_hat, codes, live = done

    quads = width // QW
    context, lse, slot_hat, slot_kv = call(
        functools.partial(forward_kernel, len(pieces)),
        [
            shape((rows, width), bf16),
            shape((per_dev, quads, QW), f32),
            shape((count * BLK, width), bf16),
            shape((count * BLK, 2 * width), bf16),
        ],
        [smem(), smem(), vmem(), vmem()] + [hbm()] * (len(pieces) + 3),
        [
            pltpu.VMEM((count, BLK, width), bf16),
            pltpu.VMEM((rows + 2 * BLK, 2 * width), bf16),
            pltpu.VMEM((rows, width), bf16),
            pltpu.VMEM((width, 2 * width), bf16),
            pltpu.VMEM((count * BLK, width), bf16),
            pltpu.VMEM((count * BLK, 2 * width), bf16),
            pltpu.SemaphoreType.DMA((count,)),
            pltpu.SemaphoreType.DMA((3,)),
            pltpu.SemaphoreType.DMA((count // 4, 2)),
        ],
        "attend_forward",
        room=ROOM[1],
        out_specs=[vmem(), vmem(), hbm(), hbm()],
    )(codes, live, gain1, bias1, *pieces, query, own_kv, w_qkv)

    chunk = width
    steps = ff // chunk
    const = lambda *dims: pl.BlockSpec(dims, lambda s, c: (0,) * len(dims))
    if placed:
        back_half = (2, 2, 4, ff // 16, width // 2)
        rest_half = (2, 2, 4, 5 * (width // 16), width // 2)
        back_spec = pl.BlockSpec((2, 2, 1, ff // 16, width // 2), lambda s, c: (0, 0, s ^ c[0], 0, 0))
        grad_specs = [back_spec, back_spec, const(*rest_half), const(*rest_half)]
        grad_shapes = [shape(back_half, bf16)] * 2 + [shape(rest_half, bf16)] * 2
    else:
        grad_specs = [
            pl.BlockSpec((chunk, width), lambda s, c: (s, 0)),
            pl.BlockSpec((width, chunk), lambda s, c: (0, s)),
            const(width, width),
        ]
        grad_shapes = [
            shape((ff, width), bf16), shape((width, ff), bf16), shape((width, width), bf16),
        ]
    output, d_hidden, d_context, gain_two, bias_two, *grads = pl.pallas_call(
        functools.partial(middle_kernel, len(grad_specs)),
        grid_spec=pltpu.PrefetchScalarGridSpec(
            num_scalar_prefetch=1,
            grid=(steps,),
            in_specs=[
                const(rows, width), const(rows, width), const(rows, width), const(width, width),
                const(1, width), const(1, width),
                pl.BlockSpec((width, chunk), lambda s, c: (0, s)),
                pl.BlockSpec((chunk, width), lambda s, c: (s, 0)),
            ],
            out_specs=[
                const(rows, width), const(rows, width), const(rows, width),
                const(1, width), const(1, width), *grad_specs,
            ],
            scratch_shapes=[
                pltpu.VMEM((rows, width), f32), pltpu.VMEM((rows, width), bf16),
                pltpu.VMEM((width, rows), bf16), pltpu.VMEM((rows, width), f32),
                pltpu.VMEM((rows, width), f32), pltpu.VMEM((rows, chunk), bf16),
                pltpu.VMEM((rows, chunk), bf16), pltpu.VMEM((chunk, width), bf16),
            ],
        ),
        out_shape=[
            shape((rows, width), bf16), shape((rows, width), f32), shape((rows, width), bf16),
            shape((1, width), f32), shape((1, width), f32), *grad_shapes,
        ],
        compiler_params=pltpu.CompilerParams(vmem_limit_bytes=ROOM[2] * 1024 * 1024),
        cost_estimate=COST,
        name="middle",
    )(coords, tok, context, grad_out, w_out, gain2, bias2, w_in, w_back)

    share = width // shards
    parts_in = (query, d_context, own_kv, own_kv, slot_kv, slot_kv)

    def attend_back(parts, live, early):
        column = lambda n, j: pl.BlockSpec((n, QW), lambda i: (0, j))
        whole = lambda s: pl.BlockSpec(s.shape, lambda i: (0,) * len(s.shape))
        specs, operands, outs, held = [], [], [], []
        for part in parts:
            specs += [column(rows, part), column(rows, part)]
            specs += [column(rows, part), column(rows, part + quads)]
            specs += [column(count * BLK, part), column(count * BLK, part + quads)]
            operands += [query, d_context, own_kv, own_kv, slot_kv, slot_kv]
            outs += [
                shape((rows, QW), bf16), shape((rows, 2 * QW), bf16),
                shape((count * BLK, 2 * QW), bf16),
            ]
        scratch = [
            pltpu.VMEM((2 * len(parts), rows + 2 * BLK, QW), bf16),
            pltpu.VMEM((2 * len(parts), rows + 2 * BLK, QW), f32),
            pltpu.VMEM((2 * len(parts), 2 * BLK, QW), f32),
        ]
        kernel = functools.partial(first_backward_kernel, parts)
        if early is not None:
            held = [w_qkv, own_hat, slot_hat, *early]
            kernel = functools.partial(last_backward_kernel, parts, len(early) // 3)
            outs += [
                shape((rows, width), f32), shape((count * BLK, width), bf16),
                shape((1, width), f32), shape((1, width), f32),
            ]
            scratch += [pltpu.VMEM(v.shape, v.dtype) for v in held]
            scratch += [pltpu.SemaphoreType.DMA((len(held),))]
        return list(
            pl.pallas_call(
                kernel,
                grid=(1,),
                out_shape=outs,
                in_specs=[smem(), whole(lse)] + [anym()] * len(held) + specs,
                out_specs=[whole(o) for o in outs],
                scratch_shapes=scratch,
                compiler_params=pltpu.CompilerParams(
                    vmem_limit_bytes=ROOM[3 if early is None else 4] * 1024 * 1024
                ),
                cost_estimate=COST,
                name="attend_backward",
            )(live, lse, *held, *operands)
        )

    first = attend_back((0,), live, None)
    if placed:
        keep_a, send_a, keep_b, send_b = grads
        got_a, got_b = hop(send_a, CORE), hop(send_b, CORE)
        got_a, got_b, *first = tie(got_a, got_b, *first)
        third = 3 * share
        pick = lambda v, low, high: v[:, :, :, low:high]
        total = lambda keep, got, low, high: plus(pick(keep, low, high), pick(got, low, high))
        in_z = lambda v: v.reshape(v.shape[:-3] + (2, 2) + v.shape[-2:])
        sum_y = in_z(total(keep_a, got_a, 0, third))
        sum_z = in_z(total(keep_b, got_b, 0, third))
        sum_x = in_z(
            jnp.concatenate(
                [
                    total(keep_a, got_a, third, 4 * share),
                    total(keep_b, got_b, third, 5 * share),
                ],
                3,
            )
        )
        out_y, mine_y = sum_y[1], sum_y[0]
        out_z, mine_z = sum_z[:, :, :, 1], sum_z[:, :, :, 0]
        out_x, mine_x = sum_x[:, 1], sum_x[:, 0]
        out_y, mine_y, out_z, mine_z, out_x, mine_x, live, *first = tie(
            out_y, mine_y, out_z, mine_z, out_x, mine_x, live, *first
        )
        got_y, got_z, got_x = over_y(out_y), hop(out_z, NEAR), hop(out_x, ACROSS)
    rest = attend_back((1, 2), live, first)
    d_parts = first + rest[:6]
    d_own_norm, d_slot_norm, gain_one, bias_one = rest[6:]

    def qkv_grads(d_parts):
        if placed:
            shapes = [shape((2, 2, 4, 3 * share + 16, width // 2), bf16)] * 2
        else:
            shapes = [shape((width, 3 * width), bf16)]
        return call(
            functools.partial(qkv_grad_kernel, len(shapes)),
            shapes,
            [smem()] + [vmem()] * (8 + 3 * quads),
            [pltpu.VMEM((width, width), bf16), pltpu.VMEM((count * BLK, width), bf16)],
            "qkv_grads",
            room=ROOM[5],
        )(
            coords, gain_one, bias_one, gain_two, bias_two, gain1, bias1, own_norm, slot_hat, *d_parts
        )

    def token_grads(d_norm1):
        normed_one, inv_one = norm_stats(tok.astype(f32))
        grad_hat = d_norm1 * ln1_gain
        d_first = inv_one * (
            grad_hat
            - jnp.mean(grad_hat, -1, keepdims=True)
            - normed_one * jnp.mean(grad_hat * normed_one, -1, keepdims=True)
        )
        return (d_hidden + d_first).astype(bf16)

    if placed:
        d_slot_norm = d_slot_norm.reshape(count, BLK, width)
        sib_codes = hop(codes, CORE)
        sib_norm = hop(d_slot_norm, CORE)
        got_y, got_z, got_x, d_slot_norm, *d_parts = tie(got_y, got_z, got_x, d_slot_norm, *d_parts)
        sum_y, sum_z, sum_x = plus(mine_y, got_y), plus(mine_z, got_z), plus(mine_x, got_x)
        out_y, mine_y = sum_y[:, :, 1], sum_y[:, :, 0]
        out_z, mine_z = sum_z[:, 1], sum_z[:, 0]
        out_x, mine_x = sum_x[1], sum_x[0]
        out_y, mine_y, out_z, mine_z, out_x, mine_x, *d_parts = tie(
            out_y, mine_y, out_z, mine_z, out_x, mine_x, *d_parts
        )
        got_y, got_z, got_x = hop(out_y, NEAR), hop(out_z, ACROSS), over_y(out_x)
        keep_c, send_c = qkv_grads(d_parts)
        keep_c, send_c, sib_norm, got_y, got_z, got_x = tie(
            keep_c, send_c, sib_norm, got_y, got_z, got_x
        )
        sum_y, sum_z, sum_x = plus(mine_y, got_y), plus(mine_z, got_z), plus(mine_x, got_x)
        out_y, mine_y = sum_y[1], sum_y[0]
        out_z, mine_z = sum_z[1], sum_z[0]
        out_x, mine_x = sum_x[:, 1], sum_x[:, 0]
        got_y, got_z, got_x = hop(out_y, ACROSS), over_y(out_z), hop(out_x, NEAR)
        mine_y, mine_z, mine_x, sib_norm = tie(mine_y, mine_z, mine_x, sib_norm)
        got_c = hop(send_c, CORE)
        piece_shape = shape((per_dev, BLK, width), bf16)
        sums = call(
            scatter_kernel,
            [piece_shape] * 8,
            [smem(), smem(), vmem(), vmem()],
            [pltpu.VMEM((8 * per_dev, BLK, width), f32)],
            "scatter_slots",
            room=ROOM[6],
        )(codes, sib_codes, d_slot_norm, sib_norm)
        below, below_x, own, beside, above, above_x, far, far_x = [
            p.reshape(rows, width) for p in sums
        ]
        from_above_x, from_below_x = hop(below_x, DOWN), hop(above_x, UP)
        in_far = hop(far_x, FAR_OUT)
        mine_y, mine_z, mine_x, got_y, got_z, got_x = after(
            own, mine_y, mine_z, mine_x, got_y, got_z, got_x
        )
        sum_y, sum_z, sum_x = plus(mine_y, got_y), plus(mine_z, got_z), plus(mine_x, got_x)
        sum_ab = jnp.concatenate([sum_y, sum_x[:, :share], sum_z, sum_x[:, share:]], 1)
        out_ab, mine_ab = sum_ab[1], sum_ab[0]
        keep_c, got_c = after(mine_ab, keep_c, got_c)
        out_c, mine_c = split(keep_c, got_c)
        got_c = over_y(out_c)
        mine_ab, _ = tie(mine_ab, mine_c)
        in_far, from_above_x, from_below_x = after(mine_ab, in_far, from_above_x, from_below_x)
        far = plus(far, in_far)
        beside = plus(beside, from_above_x, from_below_x)
        from_above2, from_below2 = hop(far, DOWN_EARLY), hop(far, UP_EARLY)
        from_beside = hop(beside, ACROSS)
        got_ab = hop(*after(beside, out_ab), FAR)
        mine_c, got_c = after(beside, mine_c, got_c)
        out_c, mine_c = split(mine_c, got_c)
        got_c = hop(out_c, ACROSS)
        mine_ab, got_ab = after(mine_c, mine_ab, got_ab)
        mine_ab = plus(mine_ab, got_ab)
        other_ab = over_y(mine_ab)
        from_above2, from_below2 = after(mine_ab, from_above2, from_below2)
        below, above = plus(below, from_above2), plus(above, from_below2)
        from_above, from_below = hop(below, DOWN), hop(above, UP)
        mine_c, got_c = after(above, mine_c, got_c)
        sum_c = by_pairs(plus(mine_c, got_c))
        out_c, mine_c = sum_c[:, 1], sum_c[:, 0]
        got_c = hop(out_c, NEAR)
        half = width // 2
        back_rows = ff // 16
        halves_ab = both_halves(*after(mine_c, mine_ab, other_ab))
        back_grad = halves_ab[:, :back_rows].reshape(2, 2, back_rows // 2, half)
        back_grad = back_grad.transpose(0, 2, 1, 3).reshape(back_rows, width)
        rest = halves_ab[:, back_rows:].reshape(2, 5, share, half)
        in_grad = rest[:, :4].reshape(8, share, half).transpose(1, 0, 2).reshape(share, ff)
        out_proj_grad = rest[:, 4].transpose(1, 0, 2).reshape(share, width)
        mine_c, got_c = after(back_grad, mine_c, got_c)
        mine_c = plus(mine_c, got_c)
        got_c = hop(mine_c[1], FAR)
        parts = after(mine_c, own, from_beside, from_above, from_below)
        d_norm1 = d_own_norm
        for part in parts:
            d_norm1 = d_norm1 + part.astype(f32)
        tokens_grad = token_grads(d_norm1)
        mine_c, got_c = after(tokens_grad, mine_c, got_c)
        mine_c = plus(mine_c[0], got_c)
        halves_c = both_halves(mine_c, over_y(mine_c))
        qkv_grad = halves_c[:, : 3 * share].reshape(6, share, half).transpose(1, 0, 2)
        qkv_grad = qkv_grad.reshape(share, 3 * width)
        vectors = halves_c[0, 3 * share : 3 * share + 8].reshape(4, width)
        vectors = lax.dynamic_slice_in_dim(vectors, me * share, share, 1)
    else:
        spread_grads = jnp.zeros((shards * per_dev, BLK, width), f32)
        spread_grads = spread_grads.at[slots].add(
            d_slot_norm.reshape(count, BLK, width).astype(f32)
        )
        others = lax.psum_scatter(
            spread_grads.astype(bf16).reshape(shards * rows, width),
            "seq", scatter_dimension=0, tiled=True,
        )
        tokens_grad = token_grads(d_own_norm + others.astype(f32))

        def reduce(part):
            mine = lax.psum_scatter(part, "seq", scatter_dimension=0, tiled=True)
            return lax.psum(mine, "grp").astype(f32)

        back_grad, in_grad, out_proj_grad = [reduce(g) for g in grads]
        qkv_grad = reduce(qkv_grads(d_parts)[0])
        vectors = jnp.concatenate([gain_one, bias_one, gain_two, bias_two])
        vectors = lax.psum(vectors, ("seq", "grp"))
        vectors = lax.dynamic_slice_in_dim(vectors, me * share, share, 1)
    return (
        output[None],
        tokens_grad[None],
        qkv_grad,
        out_proj_grad,
        in_grad,
        back_grad,
        vectors[0],
        vectors[1],
        vectors[2],
        vectors[3],
    )


def solution(mesh):
    in_specs = (
        P("grp", "seq", None),
        P(),
        P(),
        P(),
        P(),
        P(),
        P(),
        P(),
        P(),
        P("grp", None),
        P("grp", None),
        P("grp", None, None),
        P("grp", "seq", None),
        P("grp", "seq", None),
    )
    out_specs = (
        P("grp", "seq", None),
        P("grp", "seq", None),
        P("seq", None),
        P("seq", None),
        P("seq", None),
        P("seq", None),
        P("seq"),
        P("seq"),
        P("seq"),
        P("seq"),
    )
    return jax.shard_map(body, mesh=mesh, in_specs=in_specs, out_specs=out_specs, check_vma=False)
```

```python
import functools

import jax
import jax.numpy as jnp
from jax import lax
from jax.experimental import pallas as pl
from jax.experimental.pallas import tpu as pltpu
from jax.sharding import PartitionSpec as P

HD = 64
BLK = 64
UNITB = 8
QUAD = 4
QW = QUAD * HD
ln_eps = 1e-12
bf16 = jnp.bfloat16
f32 = jnp.float32
ROOM = (12, 56, 40, 14, 30, 18, 20)
BRIEF = pl.CostEstimate(flops=1_000_000, bytes_accessed=1, transcendentals=0)
COST = pl.CostEstimate(flops=40_000_000_000, bytes_accessed=1, transcendentals=0)
vmem = functools.partial(pl.BlockSpec, memory_space=pltpu.VMEM)
smem = functools.partial(pl.BlockSpec, memory_space=pltpu.SMEM)
anym = functools.partial(pl.BlockSpec, memory_space=pl.ANY)
hbm = functools.partial(pl.BlockSpec, memory_space=pltpu.HBM)


def shape(dims, dtype):
    return jax.ShapeDtypeStruct(dims, dtype)


def dot(a, b):
    return lax.dot_general(a, b, (((1,), (0,)), ((), ())), preferred_element_type=f32)


def dot_nt(a, b):
    return lax.dot_general(a, b, (((1,), (1,)), ((), ())), preferred_element_type=f32)


def dot_tn(a, b):
    return lax.dot_general(a, b, (((0,), (0,)), ((), ())), preferred_element_type=f32)


def norm_stats(values):
    center = values - jnp.mean(values, -1, keepdims=True)
    inv_std = lax.rsqrt(jnp.mean(center * center, -1, keepdims=True) + ln_eps)
    return center * inv_std, inv_std


def block_plan(doc_len, tail_len, global_rel, rand_rows, first_row):
    per_dev = rand_rows.shape[0]
    doc_end = jnp.cumsum(doc_len) * UNITB
    starts = doc_end - doc_len * UNITB
    mine = ((first_row >= starts) & (first_row < doc_end)).astype(jnp.int32)
    begin = jnp.sum(mine * starts)
    finish = jnp.sum(mine * doc_end)
    padding = jnp.sum(mine * tail_len)
    glob_one = begin + jnp.sum(mine * global_rel[:, 0])
    glob_two = begin + jnp.sum(mine * global_rel[:, 1])
    rows = first_row + jnp.arange(per_dev, dtype=jnp.int32)
    before = jnp.where(rows - 1 >= begin, rows - 1, -1)
    follow = jnp.where(rows + 1 < finish, rows + 1, -1)
    whole = jnp.zeros_like(rows)
    candidates = jnp.concatenate(
        [jnp.stack([before, rows, follow, whole + glob_one, whole + glob_two], 1), rand_rows], 1
    )
    count = candidates.shape[1]
    equal = candidates[:, :, None] == candidates[:, None, :]
    earlier = jnp.arange(count)[:, None] > jnp.arange(count)[None, :]
    usable = (candidates >= 0) & jnp.logical_not(jnp.any(equal & earlier[None], 2))
    filled = jnp.where(candidates == finish - 1, BLK - padding, BLK)
    live = jnp.where(usable, filled, 0).astype(jnp.int32)
    halo = jnp.stack(
        [
            jnp.where(first_row - 1 >= begin, first_row - 1, first_row),
            jnp.where(first_row + per_dev < finish, first_row + per_dev, first_row),
            glob_one,
            glob_two,
        ]
    )
    slots = jnp.concatenate([halo, rand_rows.reshape(-1)]).astype(jnp.int32)
    return live.reshape(-1), slots


def head_masks(rows):
    lane = lax.broadcasted_iota(jnp.int32, (rows, QW), 1) // HD
    return [lane == h for h in range(QUAD)]


def spread(values, masks):
    zero = jnp.zeros_like(values)
    return jnp.concatenate([jnp.where(m, values, zero) for m in masks], 0)


def collect(values, masks):
    out = values[:BLK]
    for h in range(1, QUAD):
        out = jnp.where(masks[h], values[h * BLK : (h + 1) * BLK], out)
    return out


def key_rows(ext, slots, i, cols):
    return jnp.concatenate(
        [
            ext[pl.ds(pl.multiple_of(i * BLK, BLK), 3 * BLK), cols],
            slots[2 * BLK : 4 * BLK, cols],
            slots[pl.ds(pl.multiple_of((4 + 3 * i) * BLK, BLK), 3 * BLK), cols],
        ],
        0,
    )


def masked(scores, live, i, cand):
    row = lax.broadcasted_iota(jnp.int32, (BLK, QW), 0)
    return jnp.concatenate(
        [
            jnp.where(row < live[i * cand + c], scores[c * BLK : (c + 1) * BLK], -1e30)
            for c in range(cand)
        ],
        0,
    )


def fill_ext(ext, own, slots):
    rows = own.shape[0]
    ext[0:BLK, :] = slots[0:BLK, :]
    ext[BLK : BLK + rows, :] = own[...]
    ext[BLK + rows : 2 * BLK + rows, :] = slots[BLK : 2 * BLK, :]


def own_kernel(tokens, w_qkv, gain, bias, query, own_kv, own_norm, own_hat):
    rows, width = tokens.shape
    tile = 128
    for r in range(0, rows, tile):
        t = slice(r, r + tile)
        normed, _ = norm_stats(tokens[t, :].astype(f32))
        own_hat[t, :] = normed.astype(bf16)
        low = (normed * gain[...] + bias[...]).astype(bf16)
        own_norm[t, :] = low
        query[t, :] = (dot(low, w_qkv[:, :width]) * HD**-0.5).astype(bf16)
        own_kv[t, :] = dot(low, w_qkv[:, width:]).astype(bf16)


def forward_kernel(num_pieces, codes, live, gain, bias, *refs):
    pieces, refs = refs[:num_pieces], refs[num_pieces:]
    query_hbm, own_hbm, w_hbm, context, lse, hat_hbm, kv_hbm = refs[:7]
    slot_tok, ext, query, w_kv, slot_hat, slot_kv, sems, in_sems, out_sems = refs[7:]
    count = slot_tok.shape[0]
    per_piece = pieces[0].shape[0]
    rows_own, width = query.shape
    nblk = rows_own // BLK
    cand = live.shape[0] // nblk
    group = 4

    def fetch(s, piece, block):
        return pltpu.make_async_copy(piece.at[block], slot_tok.at[s], sems.at[s])

    def start(s, _):
        which, block = codes[s] // per_piece, codes[s] % per_piece
        for k, piece in enumerate(pieces):

            @pl.when(which == k)
            def _():
                fetch(s, piece, block).start()

        return 0

    ins = [
        pltpu.make_async_copy(w_hbm.at[:, pl.ds(width, 2 * width)], w_kv, in_sems.at[0]),
        pltpu.make_async_copy(own_hbm, ext.at[pl.ds(BLK, rows_own)], in_sems.at[1]),
        pltpu.make_async_copy(query_hbm, query, in_sems.at[2]),
    ]

    def outs(step):
        rows = pl.ds(pl.multiple_of(step * group * BLK, group * BLK), group * BLK)
        return rows, [
            pltpu.make_async_copy(slot_hat.at[rows], hat_hbm.at[rows], out_sems.at[step, 0]),
            pltpu.make_async_copy(slot_kv.at[rows], kv_hbm.at[rows], out_sems.at[step, 1]),
        ]

    ins[0].start()
    lax.fori_loop(0, count, start, 0)
    ins[1].start()
    ins[2].start()
    ins[0].wait()

    def project(step, _):
        for k in range(group):
            fetch(step * group + k, pieces[0], 0).wait()
        rows, copies = outs(step)
        tok = slot_tok[pl.ds(step * group, group)].reshape(group * BLK, width).astype(f32)
        normed, _ = norm_stats(tok)
        slot_hat[rows, :] = normed.astype(bf16)
        low = (normed * gain[...] + bias[...]).astype(bf16)
        slot_kv[rows, :] = dot(low, w_kv[...]).astype(bf16)
        for copy in copies:
            copy.start()
        return 0

    lax.fori_loop(0, count // group, project, 0)
    ins[1].wait()
    ins[2].wait()
    ext[0:BLK, :] = slot_kv[0:BLK, :]
    ext[BLK + rows_own :, :] = slot_kv[BLK : 2 * BLK, :]
    masks = head_masks(BLK)

    def attend(i, _):
        qrows = pl.ds(pl.multiple_of(i * BLK, BLK), BLK)
        for quad in range(width // QW):
            cols = pl.ds(quad * QW, QW)
            vcols = pl.ds(width + quad * QW, QW)
            keys = key_rows(ext, slot_kv, i, cols)
            vals = key_rows(ext, slot_kv, i, vcols)
            scores = masked(dot_nt(keys, spread(query[qrows, cols], masks)), live, i, cand)
            top = jnp.max(scores, 0, keepdims=True)
            expo = jnp.exp(scores - top)
            total = jnp.sum(expo, 0, keepdims=True)
            probs = (expo * (1.0 / total)).astype(bf16)
            lse[i, pl.ds(quad, 1), :] = top + jnp.log(total)
            context[qrows, cols] = collect(dot_tn(probs, vals), masks).astype(bf16)
        return 0

    lax.fori_loop(0, nblk, attend, 0, unroll=True)

    def finish(step, _):
        for copy in outs(step)[1]:
            copy.wait()
        return 0

    lax.fori_loop(0, count // group, finish, 0)


def attend_back_parts(parts, live, lse, ins, outs, ext, d_ext, d_glob):
    rows_own = ins[0].shape[0]
    nblk = rows_own // BLK
    cand = live.shape[0] // nblk
    d_ext[...] = jnp.zeros_like(d_ext)
    d_glob[...] = jnp.zeros_like(d_glob)
    masks = head_masks(BLK)
    for n in range(len(parts)):
        for kv in range(2):
            own, slots = ins[6 * n + 2 + kv], ins[6 * n + 4 + kv]
            fill_ext(ext.at[2 * n + kv], own, slots)

    def attend(i, _):
        qrows = pl.ds(pl.multiple_of(i * BLK, BLK), BLK)
        near = pl.ds(pl.multiple_of(i * BLK, BLK), 3 * BLK)
        far = pl.ds(pl.multiple_of((4 + 3 * i) * BLK, BLK), 3 * BLK)
        every = pl.ds(0, QW)
        for n, part in enumerate(parts):
            query, d_context, _, _, slot_k, slot_v = ins[6 * n : 6 * n + 6]
            d_query, _, d_slot = outs[3 * n : 3 * n + 3]
            keys = key_rows(ext.at[2 * n], slot_k, i, every)
            vals = key_rows(ext.at[2 * n + 1], slot_v, i, every)
            spread_q = spread(query[qrows, :], masks)
            spread_d = spread(d_context[qrows, :], masks)
            scores = masked(dot_nt(keys, spread_q), live, i, cand)
            probs = jnp.exp(scores - lse[i, pl.ds(part, 1), :])
            d_probs = dot_nt(vals, spread_d)
            delta = jnp.sum(d_probs * probs, 0, keepdims=True)
            d_scores = (probs * (d_probs - delta)).astype(bf16)
            d_keys = dot(d_scores, spread_q)
            d_vals = dot(probs.astype(bf16), spread_d)
            d_query[qrows, :] = (collect(dot_tn(d_scores, keys), masks) * HD**-0.5).astype(bf16)
            for kv, grads in enumerate((d_keys, d_vals)):
                d_ext[2 * n + kv, near, :] += grads[: 3 * BLK]
                d_glob[2 * n + kv] += grads[3 * BLK : 5 * BLK]
                d_slot[far, kv * QW : (kv + 1) * QW] = grads[5 * BLK :].astype(bf16)
        return 0

    lax.fori_loop(0, nblk, attend, 0, unroll=4 // len(parts))
    for n in range(len(parts)):
        _, d_own, d_slot = outs[3 * n : 3 * n + 3]
        for kv in range(2):
            cols = slice(kv * QW, (kv + 1) * QW)
            d_slot[0:BLK, cols] = d_ext[2 * n + kv, 0:BLK, :].astype(bf16)
            d_slot[BLK : 2 * BLK, cols] = d_ext[2 * n + kv, BLK + rows_own :, :].astype(bf16)
            d_slot[2 * BLK : 4 * BLK, cols] = d_glob[2 * n + kv].astype(bf16)
            d_own[:, cols] = d_ext[2 * n + kv, BLK : BLK + rows_own, :].astype(bf16)


def first_backward_kernel(parts, live, lse, *refs):
    count = len(parts)
    ins, outs, scratch = refs[: 6 * count], refs[6 * count : 9 * count], refs[9 * count :]
    attend_back_parts(parts, live, lse, ins, outs, *scratch)


def joined(refs, rows):
    return jnp.concatenate(
        [r[rows, kv * QW : (kv + 1) * QW] for kv in range(2) for r in refs], 1
    )


def last_backward_kernel(parts, early, live, lse, *refs):
    count = len(parts)
    late = 3 + 3 * early
    held_hbm, refs = refs[:late], refs[late:]
    ins, outs, refs = refs[: 6 * count], refs[6 * count : 9 * count], refs[9 * count :]
    (d_own_norm, d_slot_norm, gain_part, bias_part), refs = refs[:4], refs[4:]
    scratch, held, sems = refs[:3], refs[3:-1], refs[-1]
    copies = [
        pltpu.make_async_copy(src, dst, sems.at[n])
        for n, (src, dst) in enumerate(zip(held_hbm, held))
    ]
    for copy in copies:
        copy.start()
    attend_back_parts(parts, live, lse, ins, outs, *scratch)
    for copy in copies:
        copy.wait()
    w_qkv, own_hat, slot_hat = held[:3]
    grads_in = held[3:] + outs
    d_query, d_own, d_slot = grads_in[0::3], grads_in[1::3], grads_in[2::3]
    rows_own, width = d_own_norm.shape
    step_rows = 4 * BLK

    def add(grads, hat, first):
        gain = jnp.sum(grads * hat.astype(f32), 0, keepdims=True)
        bias = jnp.sum(grads, 0, keepdims=True)
        if first:
            gain_part[...], bias_part[...] = gain, bias
        else:
            gain_part[...] += gain
            bias_part[...] += bias

    for r in range(0, rows_own, step_rows):
        rows = slice(r, r + step_rows)
        grads = dot_nt(jnp.concatenate([d[rows, :] for d in d_query], 1), w_qkv[:, :width])
        grads += dot_nt(joined(d_own, rows), w_qkv[:, width:])
        d_own_norm[rows, :] = grads
        add(grads, own_hat[rows, :], r == 0)

    half_rows = d_slot_norm.shape[0] // 2

    def back(step, _):
        rows = pl.ds(pl.multiple_of(step * half_rows, BLK), half_rows)
        grads = dot_nt(joined(d_slot, rows), w_qkv[:, width:])
        d_slot_norm[rows, :] = grads.astype(bf16)
        add(grads, slot_hat[rows, :], False)
        return 0

    lax.fori_loop(0, 2, back, 0)


def halves_to_dests(coords, grads, half, keep, send, slot, side):
    share = grads.shape[0] // 16
    for zr in range(4):
        for xr in range(2):
            for cr, target in ((0, keep), (1, send)):
                dest = (zr ^ coords[0]) * 4 + (xr ^ coords[1]) * 2 + (cr ^ coords[2])
                rows = pl.ds(pl.multiple_of(dest * share, 16), share)
                target[side, xr, zr, slot * share : (slot + 1) * share, :] = grads[
                    rows, half * 384 : (half + 1) * 384
                ]


def qkv_grad_kernel(
    num_out, coords, gain1, bias1, gain2, bias2, gain, bias, own_norm, slot_hat, *refs
):
    ins, outs, tmp, slot_norm = refs[: -2 - num_out], refs[-2 - num_out : -2], refs[-2], refs[-1]
    for r in range(0, slot_norm.shape[0], 2 * BLK):
        rows = slice(r, r + 2 * BLK)
        normed = slot_hat[rows, :].astype(f32)
        slot_norm[rows, :] = (normed * gain[...] + bias[...]).astype(bf16)
    d_query, d_own, d_slot = ins[0::3], ins[1::3], ins[2::3]
    width = own_norm.shape[1]
    whole = slice(None)
    for part in range(3):
        if part == 0:
            grads = dot_tn(own_norm[...], jnp.concatenate([d[...] for d in d_query], 1))
        else:
            cols = slice((part - 1) * QW, part * QW)
            grads = dot_tn(own_norm[...], jnp.concatenate([d[:, cols] for d in d_own], 1))
            grads += dot_tn(slot_norm[...], jnp.concatenate([d[:, cols] for d in d_slot], 1))
        if num_out == 1:
            outs[0][:, part * width : (part + 1) * width] = grads.astype(bf16)
        else:
            tmp[...] = grads.astype(bf16)
            for half in range(2):
                piece = part * 2 + half
                side = (piece // 3) ^ coords[3]
                halves_to_dests(coords, tmp, half, outs[0], outs[1], piece % 3, side)
    if num_out == 2:
        half = width // 2
        lines = [v[:, h * half : (h + 1) * half] for v in (gain1, bias1, gain2, bias2) for h in (0, 1)]
        block = jnp.concatenate(lines + [jnp.zeros((8, half), f32)], 0).astype(bf16)
        rows = slice(outs[0].shape[3] - 16, outs[0].shape[3])
        for out in outs:
            for side in range(2):
                for xr in range(2):
                    for zr in range(4):
                        out[side, xr, zr, rows, :] = block


def gelu_both(x):
    half_erf = 0.5 * lax.erf(x * 0.7071067811865476)
    cdf = 0.5 + half_erf
    density = jnp.exp(-0.5 * x * x) * 0.3989422804014327
    return x * cdf, cdf + x * density


def middle_kernel(
    num_grads, coords, tokens, context, grad_out, w_out, gain, bias, w_in, w_back,
    output, d_hidden, d_context, gain_part, bias_part, *refs,
):
    grad_refs, refs = refs[:num_grads], refs[num_grads:]
    hidden, norm_low, norm_t, out_sum, d_norm, act, slope, tmp = refs
    step, steps = pl.program_id(0), pl.num_programs(0)
    rows, width = hidden.shape
    tile = 256

    @pl.when(step == 0)
    def _():
        for r in range(0, rows, tile):
            t = slice(r, r + tile)
            value = tokens[t, :].astype(f32) + dot(context[t, :], w_out[...])
            hidden[t, :] = value
            normed, _ = norm_stats(value)
            norm_low[t, :] = (normed * gain[...] + bias[...]).astype(bf16)
        norm_t[...] = norm_low[...].T
        out_sum[...] = jnp.zeros_like(out_sum)
        d_norm[...] = jnp.zeros_like(d_norm)

    for r in range(0, rows, tile):
        t = slice(r, r + tile)
        value, grad = gelu_both(dot(norm_low[t, :], w_in[...]))
        low = value.astype(bf16)
        act[t, :] = low
        out_sum[t, :] += dot(low, w_back[...])
        d_low = (dot_nt(grad_out[t, :], w_back[...]) * grad).astype(bf16)
        slope[t, :] = d_low
        d_norm[t, :] += dot_nt(d_low, w_in[...])
    back_grads = dot_tn(act[...], grad_out[...]).astype(bf16)
    in_grads = dot(norm_t[...], slope[...]).astype(bf16)
    if num_grads == 3:
        grad_refs[0][...] = back_grads
        grad_refs[1][...] = in_grads
    else:
        tmp[...] = back_grads
        share = tmp.shape[0] // 8
        for yr in range(2):
            for xr in range(2):
                for cr in range(2):
                    place = (xr ^ coords[1]) * 4 + (cr ^ coords[2]) * 2 + (yr ^ coords[3])
                    rows_from = pl.ds(pl.multiple_of(place * share, 16), share)
                    for half in range(2):
                        grad_refs[cr][yr, xr, 0, half * share : (half + 1) * share, :] = tmp[
                            rows_from, half * width // 2 : (half + 1) * width // 2
                        ]
        tmp[...] = in_grads
        side = (step // 2) ^ coords[3]
        for odd in range(2):

            @pl.when(step % 2 == odd)
            def _():
                for half in range(2):
                    halves_to_dests(
                        coords, tmp, half, grad_refs[2], grad_refs[3], odd * 2 + half, side
                    )

    @pl.when(step == steps - 1)
    def _():
        for r in range(0, rows, tile):
            t = slice(r, r + tile)
            value = hidden[t, :]
            output[t, :] = (value + out_sum[t, :]).astype(bf16)
            normed, inv = norm_stats(value)
            grad = d_norm[t, :]
            part_gain = jnp.sum(grad * normed, 0, keepdims=True)
            part_bias = jnp.sum(grad, 0, keepdims=True)
            if r == 0:
                gain_part[...] = part_gain
                bias_part[...] = part_bias
            else:
                gain_part[...] += part_gain
                bias_part[...] += part_bias
            hat = grad * gain[...]
            mean_hat = jnp.mean(hat, -1, keepdims=True)
            mean_dot = jnp.mean(hat * normed, -1, keepdims=True)
            total = grad_out[t, :].astype(f32) + inv * (hat - mean_hat - normed * mean_dot)
            d_hidden[t, :] = total
            low = total.astype(bf16)
            norm_low[t, :] = low
            d_context[t, :] = dot_nt(low, w_out[...]).astype(bf16)
        out_grads = dot_tn(context[...], norm_low[...]).astype(bf16)
        if num_grads == 3:
            grad_refs[2][...] = out_grads
        else:
            tmp[...] = out_grads
            for half in range(2):
                halves_to_dests(
                    coords, tmp, half, grad_refs[2], grad_refs[3], 4, half ^ coords[3]
                )


def hop(values, route):
    return lax.ppermute(values, "seq", route)


def swap(bit):
    return [(i, i ^ bit) for i in range(16)]


CORE, ACROSS = swap(1), swap(2)
NEAR, FAR = swap(4), swap(8)
UP = [(i, i + 4) for i in range(12)]
DOWN = [(i + 4, i) for i in range(12)]
UP_LATE = [(i, i + 4) for i in range(4, 12) if i % 4 != 0]
DOWN_LATE = [(i + 4, i) for i in range(8) if i % 4 != 3]
UP_EARLY = [(i, i + 4) for i in range(8) if i % 4 != 3]
DOWN_EARLY = [(i + 4, i) for i in range(4, 12) if i % 4 != 0]
FAR_IN = [(i, i ^ 2) for i in range(16) if (i >= 8) == bool(i & 2)]
FAR_OUT = [(i, i ^ 2) for i in range(16) if (i >= 8) != bool(i & 2)]


def tie(*values):
    return lax.optimization_barrier(values)


def after(mark, *values):
    return tie(mark, *values)[1:]


def gather_pieces(tok, coords, plan, meanwhile):
    beside, below, above = hop(tok, ACROSS), hop(tok, UP), hop(tok, DOWN)
    s_tok = hop(tok, CORE)
    beside, below, above, s_tok, *plan = tie(beside, below, above, s_tok, *plan)
    below2, above2 = hop(below, UP_LATE), hop(above, DOWN_LATE)
    s_beside, s_below, s_above = [hop(v, CORE) for v in (beside, below, above)]
    below2, above2, s_beside, s_below, s_above, beside, *done = tie(
        below2, above2, s_beside, s_below, s_above, beside, *meanwhile(below, *plan)
    )
    far = jnp.where(coords[0] >= 2, below2, above2)
    below_x, above_x, far_x = hop(beside, UP), hop(beside, DOWN), hop(far, FAR_IN)
    s_far = hop(far, CORE)
    below_x, above_x, far_x, s_far = tie(below_x, above_x, far_x, s_far)
    s_below_x, s_above_x, s_far_x = [hop(v, CORE) for v in (below_x, above_x, far_x)]
    pieces = [
        below, s_below, below_x, s_below_x, tok, s_tok, beside, s_beside,
        above, s_above, above_x, s_above_x, far, s_far, far_x, s_far_x,
    ]
    return pieces, done


def slot_codes(slots, per_dev, coords):
    owner, block = slots // per_dev, slots % per_dev
    z, x, core = owner // 4, (owner // 2) % 2, owner % 2
    level = jnp.where(jnp.abs(z - coords[0]) == 2, 3, z - coords[0] + 1)
    piece = level * 4 + (x ^ coords[1]) * 2 + (core ^ coords[2])
    return (piece * per_dev + block).astype(jnp.int32)


def scatter_kernel(codes, sib_codes, own, sib, *refs):
    outs, acc = refs[:-1], refs[-1]
    per_dev = outs[0].shape[0]
    acc[...] = jnp.zeros_like(acc)

    def add(s, _):
        for which, source, cls in ((codes, own, 0), (sib_codes, sib, 1)):
            piece, block = which[s] // per_dev, which[s] % per_dev

            @pl.when(piece % 2 == cls)
            def _():
                acc[(piece // 2) * per_dev + block] += source[s].astype(f32)

        return 0

    lax.fori_loop(0, own.shape[0], add, 0)
    for k, out in enumerate(outs):

        def store(b, _):
            out[b] = acc[k * per_dev + b].astype(bf16)
            return 0

        lax.fori_loop(0, per_dev, store, 0)


def plus(*values):
    total = values[0].astype(f32)
    for value in values[1:]:
        total = total + value.astype(f32)
    return total.astype(bf16)


def over_y(values):
    return lax.ppermute(values, "grp", [(0, 1), (1, 0)])


def split(keep, got, axis=0):
    pick = lambda v, n: v[n] if axis == 0 else v[:, n]
    return plus(pick(keep, 1), pick(got, 1)), plus(pick(keep, 0), pick(got, 0))


def by_pairs(values):
    return values.reshape((2, 2) + values.shape[1:])


def both_halves(mine, other):
    first = lax.axis_index("grp") == 0
    return jnp.stack([jnp.where(first, mine, other), jnp.where(first, other, mine)]).astype(f32)


def call(kernel, out_shape, in_specs, scratch, name, cost=COST, room=32, out_specs=None):
    return pl.pallas_call(
        kernel,
        out_shape=out_shape,
        in_specs=in_specs,
        out_specs=out_specs or [vmem()] * len(out_shape),
        scratch_shapes=scratch,
        compiler_params=pltpu.CompilerParams(vmem_limit_bytes=room * 1024 * 1024),
        cost_estimate=cost,
        name=name,
    )


def body(
    tokens, w_qkv, w_out, w_in, w_back, ln1_gain, ln1_bias, ln2_gain, ln2_bias,
    doc_units, tail_pad, global_ids, rand_blocks, out_grad,
):
    tok = tokens[0]
    grad_out = out_grad[0]
    rows, width = tok.shape
    ff = w_in.shape[1]
    per_dev = rows // BLK
    shards = lax.axis_size("seq")
    placed = shards == 16 and lax.axis_size("grp") == 2
    me = lax.axis_index("seq")
    first_row = me * per_dev
    coords = jnp.stack([me // 4, (me // 2) % 2, me % 2, lax.axis_index("grp")]).astype(jnp.int32)
    live, slots = block_plan(doc_units[0], tail_pad[0], global_ids[0], rand_blocks[0], first_row)
    count = slots.shape[0]
    gain1, bias1 = ln1_gain[None], ln1_bias[None]
    gain2, bias2 = ln2_gain[None], ln2_bias[None]

    def own_rows(mark, codes, live):
        operands = after(mark, tok, codes, live)
        outs = call(
            own_kernel,
            [
                shape((rows, width), bf16), shape((rows, 2 * width), bf16),
                shape((rows, width), bf16), shape((rows, width), bf16),
            ],
            [vmem()] * 4,
            [],
            "own_rows", room=ROOM[0],
        )(operands[0], w_qkv, gain1, bias1)
        return list(outs) + list(operands[1:])

    if placed:
        codes = slot_codes(slots, per_dev, coords)
        pieces, done = gather_pieces(tok, coords, (codes, live), own_rows)
        pieces = [p.reshape(per_dev, BLK, width) for p in pieces]
    else:
        pieces = [lax.all_gather(tok, "seq").reshape(shards * per_dev, BLK, width)]
        done = own_rows(tok, slots, live)
    query, own_kv, own_norm, own_hat, codes, live = done

    quads = width // QW
    context, lse, slot_hat, slot_kv = call(
        functools.partial(forward_kernel, len(pieces)),
        [
            shape((rows, width), bf16),
            shape((per_dev, quads, QW), f32),
            shape((count * BLK, width), bf16),
            shape((count * BLK, 2 * width), bf16),
        ],
        [smem(), smem(), vmem(), vmem()] + [hbm()] * (len(pieces) + 3),
        [
            pltpu.VMEM((count, BLK, width), bf16),
            pltpu.VMEM((rows + 2 * BLK, 2 * width), bf16),
            pltpu.VMEM((rows, width), bf16),
            pltpu.VMEM((width, 2 * width), bf16),
            pltpu.VMEM((count * BLK, width), bf16),
            pltpu.VMEM((count * BLK, 2 * width), bf16),
            pltpu.SemaphoreType.DMA((count,)),
            pltpu.SemaphoreType.DMA((3,)),
            pltpu.SemaphoreType.DMA((count // 4, 2)),
        ],
        "attend_forward",
        room=ROOM[1],
        out_specs=[vmem(), vmem(), hbm(), hbm()],
    )(codes, live, gain1, bias1, *pieces, query, own_kv, w_qkv)

    chunk = width
    steps = ff // chunk
    const = lambda *dims: pl.BlockSpec(dims, lambda s, c: (0,) * len(dims))
    if placed:
        back_half = (2, 2, 4, ff // 16, width // 2)
        rest_half = (2, 2, 4, 5 * (width // 16), width // 2)
        back_spec = pl.BlockSpec((2, 2, 1, ff // 16, width // 2), lambda s, c: (0, 0, s ^ c[0], 0, 0))
        grad_specs = [back_spec, back_spec, const(*rest_half), const(*rest_half)]
        grad_shapes = [shape(back_half, bf16)] * 2 + [shape(rest_half, bf16)] * 2
    else:
        grad_specs = [
            pl.BlockSpec((chunk, width), lambda s, c: (s, 0)),
            pl.BlockSpec((width, chunk), lambda s, c: (0, s)),
            const(width, width),
        ]
        grad_shapes = [
            shape((ff, width), bf16), shape((width, ff), bf16), shape((width, width), bf16),
        ]
    output, d_hidden, d_context, gain_two, bias_two, *grads = pl.pallas_call(
        functools.partial(middle_kernel, len(grad_specs)),
        grid_spec=pltpu.PrefetchScalarGridSpec(
            num_scalar_prefetch=1,
            grid=(steps,),
            in_specs=[
                const(rows, width), const(rows, width), const(rows, width), const(width, width),
                const(1, width), const(1, width),
                pl.BlockSpec((width, chunk), lambda s, c: (0, s)),
                pl.BlockSpec((chunk, width), lambda s, c: (s, 0)),
            ],
            out_specs=[
                const(rows, width), const(rows, width), const(rows, width),
                const(1, width), const(1, width), *grad_specs,
            ],
            scratch_shapes=[
                pltpu.VMEM((rows, width), f32), pltpu.VMEM((rows, width), bf16),
                pltpu.VMEM((width, rows), bf16), pltpu.VMEM((rows, width), f32),
                pltpu.VMEM((rows, width), f32), pltpu.VMEM((rows, chunk), bf16),
                pltpu.VMEM((rows, chunk), bf16), pltpu.VMEM((chunk, width), bf16),
            ],
        ),
        out_shape=[
            shape((rows, width), bf16), shape((rows, width), f32), shape((rows, width), bf16),
            shape((1, width), f32), shape((1, width), f32), *grad_shapes,
        ],
        compiler_params=pltpu.CompilerParams(vmem_limit_bytes=ROOM[2] * 1024 * 1024),
        cost_estimate=COST,
        name="middle",
    )(coords, tok, context, grad_out, w_out, gain2, bias2, w_in, w_back)

    share = width // shards
    parts_in = (query, d_context, own_kv, own_kv, slot_kv, slot_kv)

    def attend_back(parts, live, early):
        column = lambda n, j: pl.BlockSpec((n, QW), lambda i: (0, j))
        whole = lambda s: pl.BlockSpec(s.shape, lambda i: (0,) * len(s.shape))
        specs, operands, outs, held = [], [], [], []
        for part in parts:
            specs += [column(rows, part), column(rows, part)]
            specs += [column(rows, part), column(rows, part + quads)]
            specs += [column(count * BLK, part), column(count * BLK, part + quads)]
            operands += [query, d_context, own_kv, own_kv, slot_kv, slot_kv]
            outs += [
                shape((rows, QW), bf16), shape((rows, 2 * QW), bf16),
                shape((count * BLK, 2 * QW), bf16),
            ]
        scratch = [
            pltpu.VMEM((2 * len(parts), rows + 2 * BLK, QW), bf16),
            pltpu.VMEM((2 * len(parts), rows + 2 * BLK, QW), f32),
            pltpu.VMEM((2 * len(parts), 2 * BLK, QW), f32),
        ]
        kernel = functools.partial(first_backward_kernel, parts)
        if early is not None:
            held = [w_qkv, own_hat, slot_hat, *early]
            kernel = functools.partial(last_backward_kernel, parts, len(early) // 3)
            outs += [
                shape((rows, width), f32), shape((count * BLK, width), bf16),
                shape((1, width), f32), shape((1, width), f32),
            ]
            scratch += [pltpu.VMEM(v.shape, v.dtype) for v in held]
            scratch += [pltpu.SemaphoreType.DMA((len(held),))]
        return list(
            pl.pallas_call(
                kernel,
                grid=(1,),
                out_shape=outs,
                in_specs=[smem(), whole(lse)] + [anym()] * len(held) + specs,
                out_specs=[whole(o) for o in outs],
                scratch_shapes=scratch,
                compiler_params=pltpu.CompilerParams(
                    vmem_limit_bytes=ROOM[3 if early is None else 4] * 1024 * 1024
                ),
                cost_estimate=COST,
                name="attend_backward",
            )(live, lse, *held, *operands)
        )

    first = attend_back((0,), live, None)
    if placed:
        keep_a, send_a, keep_b, send_b = grads
        got_a, got_b = hop(send_a, CORE), hop(send_b, CORE)
        got_a, got_b, *first = tie(got_a, got_b, *first)
        third = 3 * share
        pick = lambda v, low, high: v[:, :, :, low:high]
        total = lambda keep, got, low, high: plus(pick(keep, low, high), pick(got, low, high))
        in_z = lambda v: v.reshape(v.shape[:-3] + (2, 2) + v.shape[-2:])
        sum_y = in_z(total(keep_a, got_a, 0, third))
        sum_z = in_z(total(keep_b, got_b, 0, third))
        sum_x = in_z(
            jnp.concatenate(
                [
                    total(keep_a, got_a, third, 4 * share),
                    total(keep_b, got_b, third, 5 * share),
                ],
                3,
            )
        )
        out_y, mine_y = sum_y[1], sum_y[0]
        out_z, mine_z = sum_z[:, :, :, 1], sum_z[:, :, :, 0]
        out_x, mine_x = sum_x[:, 1], sum_x[:, 0]
        out_y, mine_y, out_z, mine_z, out_x, mine_x, live, *first = tie(
            out_y, mine_y, out_z, mine_z, out_x, mine_x, live, *first
        )
        got_y, got_z, got_x = over_y(out_y), hop(out_z, NEAR), hop(out_x, ACROSS)
    rest = attend_back((1, 2), live, first)
    d_parts = first + rest[:6]
    d_own_norm, d_slot_norm, gain_one, bias_one = rest[6:]

    def qkv_grads(d_parts):
        if placed:
            shapes = [shape((2, 2, 4, 3 * share + 16, width // 2), bf16)] * 2
        else:
            shapes = [shape((width, 3 * width), bf16)]
        return call(
            functools.partial(qkv_grad_kernel, len(shapes)),
            shapes,
            [smem()] + [vmem()] * (8 + 3 * quads),
            [pltpu.VMEM((width, width), bf16), pltpu.VMEM((count * BLK, width), bf16)],
            "qkv_grads",
            room=ROOM[5],
        )(
            coords, gain_one, bias_one, gain_two, bias_two, gain1, bias1, own_norm, slot_hat, *d_parts
        )

    def token_grads(d_norm1):
        normed_one, inv_one = norm_stats(tok.astype(f32))
        grad_hat = d_norm1 * ln1_gain
        d_first = inv_one * (
            grad_hat
            - jnp.mean(grad_hat, -1, keepdims=True)
            - normed_one * jnp.mean(grad_hat * normed_one, -1, keepdims=True)
        )
        return (d_hidden + d_first).astype(bf16)

    if placed:
        d_slot_norm = d_slot_norm.reshape(count, BLK, width)
        sib_codes = hop(codes, CORE)
        sib_norm = hop(d_slot_norm, CORE)
        got_y, got_z, got_x, d_slot_norm, *d_parts = tie(got_y, got_z, got_x, d_slot_norm, *d_parts)
        sum_y, sum_z, sum_x = plus(mine_y, got_y), plus(mine_z, got_z), plus(mine_x, got_x)
        out_y, mine_y = sum_y[:, :, 1], sum_y[:, :, 0]
        out_z, mine_z = sum_z[:, 1], sum_z[:, 0]
        out_x, mine_x = sum_x[1], sum_x[0]
        out_y, mine_y, out_z, mine_z, out_x, mine_x, *d_parts = tie(
            out_y, mine_y, out_z, mine_z, out_x, mine_x, *d_parts
        )
        got_y, got_z, got_x = hop(out_y, NEAR), hop(out_z, ACROSS), over_y(out_x)
        keep_c, send_c = qkv_grads(d_parts)
        keep_c, send_c, sib_norm, got_y, got_z, got_x = tie(
            keep_c, send_c, sib_norm, got_y, got_z, got_x
        )
        sum_y, sum_z, sum_x = plus(mine_y, got_y), plus(mine_z, got_z), plus(mine_x, got_x)
        out_y, mine_y = sum_y[1], sum_y[0]
        out_z, mine_z = sum_z[1], sum_z[0]
        out_x, mine_x = sum_x[:, 1], sum_x[:, 0]
        got_y, got_z, got_x = hop(out_y, ACROSS), over_y(out_z), hop(out_x, NEAR)
        mine_y, mine_z, mine_x, sib_norm = tie(mine_y, mine_z, mine_x, sib_norm)
        got_c = hop(send_c, CORE)
        piece_shape = shape((per_dev, BLK, width), bf16)
        sums = call(
            scatter_kernel,
            [piece_shape] * 8,
            [smem(), smem(), vmem(), vmem()],
            [pltpu.VMEM((8 * per_dev, BLK, width), f32)],
            "scatter_slots",
            room=ROOM[6],
        )(codes, sib_codes, d_slot_norm, sib_norm)
        below, below_x, own, beside, above, above_x, far, far_x = [
            p.reshape(rows, width) for p in sums
        ]
        from_above_x, from_below_x = hop(below_x, DOWN), hop(above_x, UP)
        in_far = hop(far_x, FAR_OUT)
        mine_y, mine_z, mine_x, got_y, got_z, got_x = after(
            own, mine_y, mine_z, mine_x, got_y, got_z, got_x
        )
        sum_y, sum_z, sum_x = plus(mine_y, got_y), plus(mine_z, got_z), plus(mine_x, got_x)
        sum_ab = jnp.concatenate([sum_y, sum_x[:, :share], sum_z, sum_x[:, share:]], 1)
        out_ab, mine_ab = sum_ab[1], sum_ab[0]
        got_ab = hop(out_ab, FAR)
        keep_c, got_c = after(mine_ab, keep_c, got_c)
        out_c, mine_c = split(keep_c, got_c)
        got_c = over_y(out_c)
        in_far, from_above_x, from_below_x = after(mine_c, in_far, from_above_x, from_below_x)
        far = plus(far, in_far)
        beside = plus(beside, from_above_x, from_below_x)
        from_above2, from_below2 = hop(far, DOWN_EARLY), hop(far, UP_EARLY)
        from_beside = hop(beside, ACROSS)
        mine_ab, got_ab = after(beside, mine_ab, got_ab)
        mine_ab = plus(mine_ab, got_ab)
        other_ab = over_y(mine_ab)
        mine_c, got_c = after(mine_ab, mine_c, got_c)
        out_c, mine_c = split(mine_c, got_c)
        got_c = hop(out_c, ACROSS)
        from_above2, from_below2 = after(mine_c, from_above2, from_below2)
        below, above = plus(below, from_above2), plus(above, from_below2)
        from_above, from_below = hop(below, DOWN), hop(above, UP)
        mine_c, got_c = after(above, mine_c, got_c)
        sum_c = by_pairs(plus(mine_c, got_c))
        out_c, mine_c = sum_c[:, 1], sum_c[:, 0]
        got_c = hop(out_c, NEAR)
        own, from_beside = after(mine_c, own, from_beside)
        own = own.astype(f32) + from_beside.astype(f32)
        mine_c, got_c = after(own, mine_c, got_c)
        mine_c = plus(mine_c, got_c)
        got_c = hop(mine_c[1], FAR)
        half = width // 2
        back_rows = ff // 16
        halves_ab = both_halves(*after(mine_c, mine_ab, other_ab))
        back_grad = halves_ab[:, :back_rows].reshape(2, 2, back_rows // 2, half)
        back_grad = back_grad.transpose(0, 2, 1, 3).reshape(back_rows, width)
        rest = halves_ab[:, back_rows:].reshape(2, 5, share, half)
        in_grad = rest[:, :4].reshape(8, share, half).transpose(1, 0, 2).reshape(share, ff)
        out_proj_grad = rest[:, 4].transpose(1, 0, 2).reshape(share, width)
        mine_c, got_c = after(back_grad, mine_c, got_c)
        mine_c = plus(mine_c[0], got_c)
        other_c = over_y(mine_c)
        from_above, from_below = after(mine_c, from_above, from_below)
        d_norm1 = d_own_norm + own + from_above.astype(f32) + from_below.astype(f32)
        tokens_grad = token_grads(d_norm1)
        mine_c, other_c = after(tokens_grad, mine_c, other_c)
        halves_c = both_halves(mine_c, other_c)
        qkv_grad = halves_c[:, : 3 * share].reshape(6, share, half).transpose(1, 0, 2)
        qkv_grad = qkv_grad.reshape(share, 3 * width)
        vectors = halves_c[0, 3 * share : 3 * share + 8].reshape(4, width)
        vectors = lax.dynamic_slice_in_dim(vectors, me * share, share, 1)
    else:
        spread_grads = jnp.zeros((shards * per_dev, BLK, width), f32)
        spread_grads = spread_grads.at[slots].add(
            d_slot_norm.reshape(count, BLK, width).astype(f32)
        )
        others = lax.psum_scatter(
            spread_grads.astype(bf16).reshape(shards * rows, width),
            "seq", scatter_dimension=0, tiled=True,
        )
        tokens_grad = token_grads(d_own_norm + others.astype(f32))

        def reduce(part):
            mine = lax.psum_scatter(part, "seq", scatter_dimension=0, tiled=True)
            return lax.psum(mine, "grp").astype(f32)

        back_grad, in_grad, out_proj_grad = [reduce(g) for g in grads]
        qkv_grad = reduce(qkv_grads(d_parts)[0])
        vectors = jnp.concatenate([gain_one, bias_one, gain_two, bias_two])
        vectors = lax.psum(vectors, ("seq", "grp"))
        vectors = lax.dynamic_slice_in_dim(vectors, me * share, share, 1)
    return (
        output[None],
        tokens_grad[None],
        qkv_grad,
        out_proj_grad,
        in_grad,
        back_grad,
        vectors[0],
        vectors[1],
        vectors[2],
        vectors[3],
    )


def solution(mesh):
    in_specs = (
        P("grp", "seq", None),
        P(),
        P(),
        P(),
        P(),
        P(),
        P(),
        P(),
        P(),
        P("grp", None),
        P("grp", None),
        P("grp", None, None),
        P("grp", "seq", None),
        P("grp", "seq", None),
    )
    out_specs = (
        P("grp", "seq", None),
        P("grp", "seq", None),
        P("seq", None),
        P("seq", None),
        P("seq", None),
        P("seq", None),
        P("seq"),
        P("seq"),
        P("seq"),
        P("seq"),
    )
    return jax.shard_map(body, mesh=mesh, in_specs=in_specs, out_specs=out_specs, check_vma=False)
```

```python
import functools

import jax
import jax.numpy as jnp
from jax import lax
from jax.experimental import pallas as pl
from jax.experimental.pallas import tpu as pltpu
from jax.sharding import PartitionSpec as P

HD = 64
BLK = 64
UNITB = 8
QUAD = 4
QW = QUAD * HD
ln_eps = 1e-12
bf16 = jnp.bfloat16
f32 = jnp.float32
ROOM = (12, 56, 40, 14, 30, 18, 20)
BRIEF = pl.CostEstimate(flops=1_000_000, bytes_accessed=1, transcendentals=0)
COST = pl.CostEstimate(flops=40_000_000_000, bytes_accessed=1, transcendentals=0)
vmem = functools.partial(pl.BlockSpec, memory_space=pltpu.VMEM)
smem = functools.partial(pl.BlockSpec, memory_space=pltpu.SMEM)
anym = functools.partial(pl.BlockSpec, memory_space=pl.ANY)
hbm = functools.partial(pl.BlockSpec, memory_space=pltpu.HBM)


def shape(dims, dtype):
    return jax.ShapeDtypeStruct(dims, dtype)


def dot(a, b):
    return lax.dot_general(a, b, (((1,), (0,)), ((), ())), preferred_element_type=f32)


def dot_nt(a, b):
    return lax.dot_general(a, b, (((1,), (1,)), ((), ())), preferred_element_type=f32)


def dot_tn(a, b):
    return lax.dot_general(a, b, (((0,), (0,)), ((), ())), preferred_element_type=f32)


def norm_stats(values):
    center = values - jnp.mean(values, -1, keepdims=True)
    inv_std = lax.rsqrt(jnp.mean(center * center, -1, keepdims=True) + ln_eps)
    return center * inv_std, inv_std


def block_plan(doc_len, tail_len, global_rel, rand_rows, first_row):
    per_dev = rand_rows.shape[0]
    doc_end = jnp.cumsum(doc_len) * UNITB
    starts = doc_end - doc_len * UNITB
    mine = ((first_row >= starts) & (first_row < doc_end)).astype(jnp.int32)
    begin = jnp.sum(mine * starts)
    finish = jnp.sum(mine * doc_end)
    padding = jnp.sum(mine * tail_len)
    glob_one = begin + jnp.sum(mine * global_rel[:, 0])
    glob_two = begin + jnp.sum(mine * global_rel[:, 1])
    rows = first_row + jnp.arange(per_dev, dtype=jnp.int32)
    before = jnp.where(rows - 1 >= begin, rows - 1, -1)
    follow = jnp.where(rows + 1 < finish, rows + 1, -1)
    whole = jnp.zeros_like(rows)
    candidates = jnp.concatenate(
        [jnp.stack([before, rows, follow, whole + glob_one, whole + glob_two], 1), rand_rows], 1
    )
    count = candidates.shape[1]
    equal = candidates[:, :, None] == candidates[:, None, :]
    earlier = jnp.arange(count)[:, None] > jnp.arange(count)[None, :]
    usable = (candidates >= 0) & jnp.logical_not(jnp.any(equal & earlier[None], 2))
    filled = jnp.where(candidates == finish - 1, BLK - padding, BLK)
    live = jnp.where(usable, filled, 0).astype(jnp.int32)
    halo = jnp.stack(
        [
            jnp.where(first_row - 1 >= begin, first_row - 1, first_row),
            jnp.where(first_row + per_dev < finish, first_row + per_dev, first_row),
            glob_one,
            glob_two,
        ]
    )
    slots = jnp.concatenate([halo, rand_rows.reshape(-1)]).astype(jnp.int32)
    return live.reshape(-1), slots


def head_masks(rows):
    lane = lax.broadcasted_iota(jnp.int32, (rows, QW), 1) // HD
    return [lane == h for h in range(QUAD)]


def spread(values, masks):
    zero = jnp.zeros_like(values)
    return jnp.concatenate([jnp.where(m, values, zero) for m in masks], 0)


def collect(values, masks):
    out = values[:BLK]
    for h in range(1, QUAD):
        out = jnp.where(masks[h], values[h * BLK : (h + 1) * BLK], out)
    return out


def at(row):
    return row if isinstance(row, int) else pl.multiple_of(row, BLK)


def key_rows(ext, slots, i, cols):
    return jnp.concatenate(
        [
            ext[pl.ds(at(i * BLK), 3 * BLK), cols],
            slots[2 * BLK : 4 * BLK, cols],
            slots[pl.ds(at((4 + 3 * i) * BLK), 3 * BLK), cols],
        ],
        0,
    )


def masked(scores, live, i, cand):
    row = lax.broadcasted_iota(jnp.int32, (BLK, QW), 0)
    return jnp.concatenate(
        [
            jnp.where(row < live[i * cand + c], scores[c * BLK : (c + 1) * BLK], -1e30)
            for c in range(cand)
        ],
        0,
    )


def fill_ext(ext, own, slots):
    rows = own.shape[0]
    ext[0:BLK, :] = slots[0:BLK, :]
    ext[BLK : BLK + rows, :] = own[...]
    ext[BLK + rows : 2 * BLK + rows, :] = slots[BLK : 2 * BLK, :]


def own_kernel(tokens, w_qkv, gain, bias, query, own_kv, own_norm, own_hat):
    rows, width = tokens.shape
    tile = 128
    for r in range(0, rows, tile):
        t = slice(r, r + tile)
        normed, _ = norm_stats(tokens[t, :].astype(f32))
        own_hat[t, :] = normed.astype(bf16)
        low = (normed * gain[...] + bias[...]).astype(bf16)
        own_norm[t, :] = low
        query[t, :] = (dot(low, w_qkv[:, :width]) * HD**-0.5).astype(bf16)
        own_kv[t, :] = dot(low, w_qkv[:, width:]).astype(bf16)


def forward_kernel(num_pieces, codes, live, gain, bias, *refs):
    pieces, refs = refs[:num_pieces], refs[num_pieces:]
    query_hbm, own_hbm, w_hbm, context, lse, hat_hbm, kv_hbm = refs[:7]
    slot_tok, ext, query, w_kv, slot_hat, slot_kv, sems, in_sems, out_sems = refs[7:]
    count = slot_tok.shape[0]
    per_piece = pieces[0].shape[0]
    rows_own, width = query.shape
    nblk = rows_own // BLK
    cand = live.shape[0] // nblk

    def fetch(s, piece, block):
        return pltpu.make_async_copy(piece.at[block], slot_tok.at[s], sems.at[s])

    def start(s, _):
        which, block = codes[s] // per_piece, codes[s] % per_piece
        for k, piece in enumerate(pieces):

            @pl.when(which == k)
            def _():
                fetch(s, piece, block).start()

        return 0

    ins = [
        pltpu.make_async_copy(w_hbm.at[:, pl.ds(width, 2 * width)], w_kv, in_sems.at[0]),
        pltpu.make_async_copy(own_hbm, ext.at[pl.ds(BLK, rows_own)], in_sems.at[1]),
        pltpu.make_async_copy(query_hbm, query, in_sems.at[2]),
    ]

    picks = (count - 4) // nblk
    cuts = [0, 4 + 4 * picks, 4 + 6 * picks, count]

    def outs(step):
        rows = pl.ds(cuts[step] * BLK, (cuts[step + 1] - cuts[step]) * BLK)
        return [
            pltpu.make_async_copy(slot_hat.at[rows], hat_hbm.at[rows], out_sems.at[step, 0]),
            pltpu.make_async_copy(slot_kv.at[rows], kv_hbm.at[rows], out_sems.at[step, 1]),
        ]

    ins[0].start()
    lax.fori_loop(0, count, start, 0)
    ins[1].start()
    ins[2].start()
    ins[0].wait()

    def project(low_slot, slots):
        for s in range(low_slot, low_slot + slots):
            fetch(s, pieces[0], 0).wait()
        rows = slice(low_slot * BLK, (low_slot + slots) * BLK)
        tok = slot_tok[low_slot : low_slot + slots].reshape(slots * BLK, width).astype(f32)
        normed, _ = norm_stats(tok)
        slot_hat[rows, :] = normed.astype(bf16)
        low = (normed * gain[...] + bias[...]).astype(bf16)
        slot_kv[rows, :] = dot(low, w_kv[...]).astype(bf16)

    project(0, 4 + 2 * picks)
    ins[1].wait()
    ins[2].wait()
    ext[0:BLK, :] = slot_kv[0:BLK, :]
    ext[BLK + rows_own :, :] = slot_kv[BLK : 2 * BLK, :]
    masks = head_masks(BLK)

    def attend(i, _):
        qrows = pl.ds(at(i * BLK), BLK)
        for quad in range(width // QW):
            cols = pl.ds(quad * QW, QW)
            vcols = pl.ds(width + quad * QW, QW)
            keys = key_rows(ext, slot_kv, i, cols)
            vals = key_rows(ext, slot_kv, i, vcols)
            scores = masked(dot_nt(keys, spread(query[qrows, cols], masks)), live, i, cand)
            top = jnp.max(scores, 0, keepdims=True)
            expo = jnp.exp(scores - top)
            total = jnp.sum(expo, 0, keepdims=True)
            probs = (expo * (1.0 / total)).astype(bf16)
            lse[i, pl.ds(quad, 1), :] = top + jnp.log(total)
            context[qrows, cols] = collect(dot_tn(probs, vals), masks).astype(bf16)
        return 0

    for i in range(nblk):
        if i % 2 == 0 and i + 2 < nblk:
            project(4 + (i + 2) * picks, 2 * picks)
        attend(i, 0)
        if i % 2 == 0 and i < 6:
            for copy in outs(i // 2):
                copy.start()
    for step in range(3):
        for copy in outs(step):
            copy.wait()


def attend_back_parts(parts, live, lse, ins, outs, ext, d_ext, d_glob):
    rows_own = ins[0].shape[0]
    nblk = rows_own // BLK
    cand = live.shape[0] // nblk
    d_ext[...] = jnp.zeros_like(d_ext)
    d_glob[...] = jnp.zeros_like(d_glob)
    masks = head_masks(BLK)
    for n in range(len(parts)):
        for kv in range(2):
            own, slots = ins[6 * n + 2 + kv], ins[6 * n + 4 + kv]
            fill_ext(ext.at[2 * n + kv], own, slots)

    def attend(i, _):
        qrows = pl.ds(pl.multiple_of(i * BLK, BLK), BLK)
        near = pl.ds(pl.multiple_of(i * BLK, BLK), 3 * BLK)
        far = pl.ds(pl.multiple_of((4 + 3 * i) * BLK, BLK), 3 * BLK)
        every = pl.ds(0, QW)
        for n, part in enumerate(parts):
            query, d_context, _, _, slot_k, slot_v = ins[6 * n : 6 * n + 6]
            d_query, _, d_slot = outs[3 * n : 3 * n + 3]
            keys = key_rows(ext.at[2 * n], slot_k, i, every)
            vals = key_rows(ext.at[2 * n + 1], slot_v, i, every)
            spread_q = spread(query[qrows, :], masks)
            spread_d = spread(d_context[qrows, :], masks)
            scores = masked(dot_nt(keys, spread_q), live, i, cand)
            probs = jnp.exp(scores - lse[i, pl.ds(part, 1), :])
            d_probs = dot_nt(vals, spread_d)
            delta = jnp.sum(d_probs * probs, 0, keepdims=True)
            d_scores = (probs * (d_probs - delta)).astype(bf16)
            d_keys = dot(d_scores, spread_q)
            d_vals = dot(probs.astype(bf16), spread_d)
            d_query[qrows, :] = (collect(dot_tn(d_scores, keys), masks) * HD**-0.5).astype(bf16)
            for kv, grads in enumerate((d_keys, d_vals)):
                d_ext[2 * n + kv, near, :] += grads[: 3 * BLK]
                d_glob[2 * n + kv] += grads[3 * BLK : 5 * BLK]
                d_slot[far, kv * QW : (kv + 1) * QW] = grads[5 * BLK :].astype(bf16)
        return 0

    lax.fori_loop(0, nblk, attend, 0, unroll=4 // len(parts))
    for n in range(len(parts)):
        _, d_own, d_slot = outs[3 * n : 3 * n + 3]
        for kv in range(2):
            cols = slice(kv * QW, (kv + 1) * QW)
            d_slot[0:BLK, cols] = d_ext[2 * n + kv, 0:BLK, :].astype(bf16)
            d_slot[BLK : 2 * BLK, cols] = d_ext[2 * n + kv, BLK + rows_own :, :].astype(bf16)
            d_slot[2 * BLK : 4 * BLK, cols] = d_glob[2 * n + kv].astype(bf16)
            d_own[:, cols] = d_ext[2 * n + kv, BLK : BLK + rows_own, :].astype(bf16)


def first_backward_kernel(parts, live, lse, *refs):
    count = len(parts)
    ins, outs, scratch = refs[: 6 * count], refs[6 * count : 9 * count], refs[9 * count :]
    attend_back_parts(parts, live, lse, ins, outs, *scratch)


def joined(refs, rows):
    return jnp.concatenate(
        [r[rows, kv * QW : (kv + 1) * QW] for kv in range(2) for r in refs], 1
    )


def last_backward_kernel(parts, early, live, lse, *refs):
    count = len(parts)
    late = 3 + 3 * early
    held_hbm, refs = refs[:late], refs[late:]
    ins, outs, refs = refs[: 6 * count], refs[6 * count : 9 * count], refs[9 * count :]
    (d_own_norm, d_slot_norm, gain_part, bias_part), refs = refs[:4], refs[4:]
    scratch, held, sems = refs[:3], refs[3:-1], refs[-1]
    copies = [
        pltpu.make_async_copy(src, dst, sems.at[n])
        for n, (src, dst) in enumerate(zip(held_hbm, held))
    ]
    for copy in copies:
        copy.start()
    attend_back_parts(parts, live, lse, ins, outs, *scratch)
    for copy in copies:
        copy.wait()
    w_qkv, own_hat, slot_hat = held[:3]
    grads_in = held[3:] + outs
    d_query, d_own, d_slot = grads_in[0::3], grads_in[1::3], grads_in[2::3]
    rows_own, width = d_own_norm.shape
    step_rows = 4 * BLK

    def add(grads, hat, first):
        gain = jnp.sum(grads * hat.astype(f32), 0, keepdims=True)
        bias = jnp.sum(grads, 0, keepdims=True)
        if first:
            gain_part[...], bias_part[...] = gain, bias
        else:
            gain_part[...] += gain
            bias_part[...] += bias

    for r in range(0, rows_own, step_rows):
        rows = slice(r, r + step_rows)
        grads = dot_nt(jnp.concatenate([d[rows, :] for d in d_query], 1), w_qkv[:, :width])
        grads += dot_nt(joined(d_own, rows), w_qkv[:, width:])
        d_own_norm[rows, :] = grads
        add(grads, own_hat[rows, :], r == 0)

    half_rows = d_slot_norm.shape[0] // 2

    def back(step, _):
        rows = pl.ds(pl.multiple_of(step * half_rows, BLK), half_rows)
        grads = dot_nt(joined(d_slot, rows), w_qkv[:, width:])
        d_slot_norm[rows, :] = grads.astype(bf16)
        add(grads, slot_hat[rows, :], False)
        return 0

    lax.fori_loop(0, 2, back, 0)


def halves_to_dests(coords, grads, half, keep, send, slot, side):
    share = grads.shape[0] // 16
    for zr in range(4):
        for xr in range(2):
            for cr, target in ((0, keep), (1, send)):
                dest = (zr ^ coords[0]) * 4 + (xr ^ coords[1]) * 2 + (cr ^ coords[2])
                rows = pl.ds(pl.multiple_of(dest * share, 16), share)
                target[side, xr, zr, slot * share : (slot + 1) * share, :] = grads[
                    rows, half * 384 : (half + 1) * 384
                ]


def qkv_grad_kernel(
    num_out, coords, gain1, bias1, gain2, bias2, gain, bias, own_norm, slot_hat, *refs
):
    ins, outs, tmp, slot_norm = refs[: -2 - num_out], refs[-2 - num_out : -2], refs[-2], refs[-1]
    for r in range(0, slot_norm.shape[0], 2 * BLK):
        rows = slice(r, r + 2 * BLK)
        normed = slot_hat[rows, :].astype(f32)
        slot_norm[rows, :] = (normed * gain[...] + bias[...]).astype(bf16)
    d_query, d_own, d_slot = ins[0::3], ins[1::3], ins[2::3]
    width = own_norm.shape[1]
    whole = slice(None)
    for part in range(3):
        if part == 0:
            grads = dot_tn(own_norm[...], jnp.concatenate([d[...] for d in d_query], 1))
        else:
            cols = slice((part - 1) * QW, part * QW)
            grads = dot_tn(own_norm[...], jnp.concatenate([d[:, cols] for d in d_own], 1))
            grads += dot_tn(slot_norm[...], jnp.concatenate([d[:, cols] for d in d_slot], 1))
        if num_out == 1:
            outs[0][:, part * width : (part + 1) * width] = grads.astype(bf16)
        else:
            tmp[...] = grads.astype(bf16)
            for half in range(2):
                piece = part * 2 + half
                side = (piece // 3) ^ coords[3]
                halves_to_dests(coords, tmp, half, outs[0], outs[1], piece % 3, side)
    if num_out == 2:
        half = width // 2
        lines = [v[:, h * half : (h + 1) * half] for v in (gain1, bias1, gain2, bias2) for h in (0, 1)]
        block = jnp.concatenate(lines + [jnp.zeros((8, half), f32)], 0).astype(bf16)
        rows = slice(outs[0].shape[3] - 16, outs[0].shape[3])
        for out in outs:
            for side in range(2):
                for xr in range(2):
                    for zr in range(4):
                        out[side, xr, zr, rows, :] = block


def gelu_both(x):
    half_erf = 0.5 * lax.erf(x * 0.7071067811865476)
    cdf = 0.5 + half_erf
    density = jnp.exp(-0.5 * x * x) * 0.3989422804014327
    return x * cdf, cdf + x * density


def middle_kernel(
    num_grads, coords, tokens, context, grad_out, w_out, gain, bias, w_in, w_back,
    output, d_hidden, d_context, gain_part, bias_part, *refs,
):
    grad_refs, refs = refs[:num_grads], refs[num_grads:]
    hidden, norm_low, norm_t, out_sum, d_norm, act, slope, tmp = refs
    step, steps = pl.program_id(0), pl.num_programs(0)
    rows, width = hidden.shape
    tile = 256

    @pl.when(step == 0)
    def _():
        for r in range(0, rows, tile):
            t = slice(r, r + tile)
            value = tokens[t, :].astype(f32) + dot(context[t, :], w_out[...])
            hidden[t, :] = value
            normed, _ = norm_stats(value)
            norm_low[t, :] = (normed * gain[...] + bias[...]).astype(bf16)
        norm_t[...] = norm_low[...].T
        out_sum[...] = jnp.zeros_like(out_sum)
        d_norm[...] = jnp.zeros_like(d_norm)

    for r in range(0, rows, tile):
        t = slice(r, r + tile)
        value, grad = gelu_both(dot(norm_low[t, :], w_in[...]))
        low = value.astype(bf16)
        act[t, :] = low
        out_sum[t, :] += dot(low, w_back[...])
        d_low = (dot_nt(grad_out[t, :], w_back[...]) * grad).astype(bf16)
        slope[t, :] = d_low
        d_norm[t, :] += dot_nt(d_low, w_in[...])
    back_grads = dot_tn(act[...], grad_out[...]).astype(bf16)
    in_grads = dot(norm_t[...], slope[...]).astype(bf16)
    if num_grads == 3:
        grad_refs[0][...] = back_grads
        grad_refs[1][...] = in_grads
    else:
        tmp[...] = back_grads
        share = tmp.shape[0] // 8
        for yr in range(2):
            for xr in range(2):
                for cr in range(2):
                    place = (xr ^ coords[1]) * 4 + (cr ^ coords[2]) * 2 + (yr ^ coords[3])
                    rows_from = pl.ds(pl.multiple_of(place * share, 16), share)
                    for half in range(2):
                        grad_refs[cr][yr, xr, 0, half * share : (half + 1) * share, :] = tmp[
                            rows_from, half * width // 2 : (half + 1) * width // 2
                        ]
        tmp[...] = in_grads
        side = (step // 2) ^ coords[3]
        for odd in range(2):

            @pl.when(step % 2 == odd)
            def _():
                for half in range(2):
                    halves_to_dests(
                        coords, tmp, half, grad_refs[2], grad_refs[3], odd * 2 + half, side
                    )

    @pl.when(step == steps - 1)
    def _():
        for r in range(0, rows, tile):
            t = slice(r, r + tile)
            value = hidden[t, :]
            output[t, :] = (value + out_sum[t, :]).astype(bf16)
            normed, inv = norm_stats(value)
            grad = d_norm[t, :]
            part_gain = jnp.sum(grad * normed, 0, keepdims=True)
            part_bias = jnp.sum(grad, 0, keepdims=True)
            if r == 0:
                gain_part[...] = part_gain
                bias_part[...] = part_bias
            else:
                gain_part[...] += part_gain
                bias_part[...] += part_bias
            hat = grad * gain[...]
            mean_hat = jnp.mean(hat, -1, keepdims=True)
            mean_dot = jnp.mean(hat * normed, -1, keepdims=True)
            total = grad_out[t, :].astype(f32) + inv * (hat - mean_hat - normed * mean_dot)
            d_hidden[t, :] = total
            low = total.astype(bf16)
            norm_low[t, :] = low
            d_context[t, :] = dot_nt(low, w_out[...]).astype(bf16)
        out_grads = dot_tn(context[...], norm_low[...]).astype(bf16)
        if num_grads == 3:
            grad_refs[2][...] = out_grads
        else:
            tmp[...] = out_grads
            for half in range(2):
                halves_to_dests(
                    coords, tmp, half, grad_refs[2], grad_refs[3], 4, half ^ coords[3]
                )


def hop(values, route):
    return lax.ppermute(values, "seq", route)


def swap(bit):
    return [(i, i ^ bit) for i in range(16)]


CORE, ACROSS = swap(1), swap(2)
NEAR, FAR = swap(4), swap(8)
UP = [(i, i + 4) for i in range(12)]
DOWN = [(i + 4, i) for i in range(12)]
UP_LATE = [(i, i + 4) for i in range(4, 12) if i % 4 != 0]
DOWN_LATE = [(i + 4, i) for i in range(8) if i % 4 != 3]
UP_EARLY = [(i, i + 4) for i in range(8) if i % 4 != 3]
DOWN_EARLY = [(i + 4, i) for i in range(4, 12) if i % 4 != 0]
FAR_IN = [(i, i ^ 2) for i in range(16) if (i >= 8) == bool(i & 2)]
FAR_OUT = [(i, i ^ 2) for i in range(16) if (i >= 8) != bool(i & 2)]


def tie(*values):
    return lax.optimization_barrier(values)


def after(mark, *values):
    return tie(mark, *values)[1:]


def gather_pieces(tok, coords, plan, meanwhile):
    beside, below, above = hop(tok, ACROSS), hop(tok, UP), hop(tok, DOWN)
    s_tok = hop(tok, CORE)
    beside, below, above, s_tok, *plan = tie(beside, below, above, s_tok, *plan)
    below2, above2 = hop(below, UP_LATE), hop(above, DOWN_LATE)
    s_beside, s_below, s_above = [hop(v, CORE) for v in (beside, below, above)]
    below2, above2, s_beside, s_below, s_above, beside, *done = tie(
        below2, above2, s_beside, s_below, s_above, beside, *meanwhile(below, *plan)
    )
    far = jnp.where(coords[0] >= 2, below2, above2)
    below_x, above_x, far_x = hop(beside, UP), hop(beside, DOWN), hop(far, FAR_IN)
    s_far = hop(far, CORE)
    below_x, above_x, far_x, s_far = tie(below_x, above_x, far_x, s_far)
    s_below_x, s_above_x, s_far_x = [hop(v, CORE) for v in (below_x, above_x, far_x)]
    pieces = [
        below, s_below, below_x, s_below_x, tok, s_tok, beside, s_beside,
        above, s_above, above_x, s_above_x, far, s_far, far_x, s_far_x,
    ]
    return pieces, done


def slot_codes(slots, per_dev, coords):
    owner, block = slots // per_dev, slots % per_dev
    z, x, core = owner // 4, (owner // 2) % 2, owner % 2
    level = jnp.where(jnp.abs(z - coords[0]) == 2, 3, z - coords[0] + 1)
    piece = level * 4 + (x ^ coords[1]) * 2 + (core ^ coords[2])
    return (piece * per_dev + block).astype(jnp.int32)


def scatter_kernel(codes, sib_codes, own, sib, *refs):
    outs, acc = refs[:-1], refs[-1]
    per_dev = outs[0].shape[0]
    acc[...] = jnp.zeros_like(acc)

    def add(s, _):
        for which, source, cls in ((codes, own, 0), (sib_codes, sib, 1)):
            piece, block = which[s] // per_dev, which[s] % per_dev

            @pl.when(piece % 2 == cls)
            def _():
                acc[(piece // 2) * per_dev + block] += source[s].astype(f32)

        return 0

    lax.fori_loop(0, own.shape[0], add, 0)
    for k, out in enumerate(outs):

        def store(b, _):
            out[b] = acc[k * per_dev + b].astype(bf16)
            return 0

        lax.fori_loop(0, per_dev, store, 0)


def plus(*values):
    total = values[0].astype(f32)
    for value in values[1:]:
        total = total + value.astype(f32)
    return total.astype(bf16)


def over_y(values):
    return lax.ppermute(values, "grp", [(0, 1), (1, 0)])


def split(keep, got, axis=0):
    pick = lambda v, n: v[n] if axis == 0 else v[:, n]
    return plus(pick(keep, 1), pick(got, 1)), plus(pick(keep, 0), pick(got, 0))


def by_pairs(values):
    return values.reshape((2, 2) + values.shape[1:])


def both_halves(mine, other):
    first = lax.axis_index("grp") == 0
    return jnp.stack([jnp.where(first, mine, other), jnp.where(first, other, mine)]).astype(f32)


def call(kernel, out_shape, in_specs, scratch, name, cost=COST, room=32, out_specs=None):
    return pl.pallas_call(
        kernel,
        out_shape=out_shape,
        in_specs=in_specs,
        out_specs=out_specs or [vmem()] * len(out_shape),
        scratch_shapes=scratch,
        compiler_params=pltpu.CompilerParams(vmem_limit_bytes=room * 1024 * 1024),
        cost_estimate=cost,
        name=name,
    )


def body(
    tokens, w_qkv, w_out, w_in, w_back, ln1_gain, ln1_bias, ln2_gain, ln2_bias,
    doc_units, tail_pad, global_ids, rand_blocks, out_grad,
):
    tok = tokens[0]
    grad_out = out_grad[0]
    rows, width = tok.shape
    ff = w_in.shape[1]
    per_dev = rows // BLK
    shards = lax.axis_size("seq")
    placed = shards == 16 and lax.axis_size("grp") == 2
    me = lax.axis_index("seq")
    first_row = me * per_dev
    coords = jnp.stack([me // 4, (me // 2) % 2, me % 2, lax.axis_index("grp")]).astype(jnp.int32)
    live, slots = block_plan(doc_units[0], tail_pad[0], global_ids[0], rand_blocks[0], first_row)
    count = slots.shape[0]
    gain1, bias1 = ln1_gain[None], ln1_bias[None]
    gain2, bias2 = ln2_gain[None], ln2_bias[None]

    def own_rows(mark, codes, live):
        operands = after(mark, tok, codes, live)
        outs = call(
            own_kernel,
            [
                shape((rows, width), bf16), shape((rows, 2 * width), bf16),
                shape((rows, width), bf16), shape((rows, width), bf16),
            ],
            [vmem()] * 4,
            [],
            "own_rows", room=ROOM[0],
        )(operands[0], w_qkv, gain1, bias1)
        return list(outs) + list(operands[1:])

    if placed:
        codes = slot_codes(slots, per_dev, coords)
        pieces, done = gather_pieces(tok, coords, (codes, live), own_rows)
        pieces = [p.reshape(per_dev, BLK, width) for p in pieces]
    else:
        pieces = [lax.all_gather(tok, "seq").reshape(shards * per_dev, BLK, width)]
        done = own_rows(tok, slots, live)
    query, own_kv, own_norm, own_hat, codes, live = done

    quads = width // QW
    context, lse, slot_hat, slot_kv = call(
        functools.partial(forward_kernel, len(pieces)),
        [
            shape((rows, width), bf16),
            shape((per_dev, quads, QW), f32),
            shape((count * BLK, width), bf16),
            shape((count * BLK, 2 * width), bf16),
        ],
        [smem(), smem(), vmem(), vmem()] + [hbm()] * (len(pieces) + 3),
        [
            pltpu.VMEM((count, BLK, width), bf16),
            pltpu.VMEM((rows + 2 * BLK, 2 * width), bf16),
            pltpu.VMEM((rows, width), bf16),
            pltpu.VMEM((width, 2 * width), bf16),
            pltpu.VMEM((count * BLK, width), bf16),
            pltpu.VMEM((count * BLK, 2 * width), bf16),
            pltpu.SemaphoreType.DMA((count,)),
            pltpu.SemaphoreType.DMA((3,)),
            pltpu.SemaphoreType.DMA((3, 2)),
        ],
        "attend_forward",
        room=ROOM[1],
        out_specs=[vmem(), vmem(), hbm(), hbm()],
    )(codes, live, gain1, bias1, *pieces, query, own_kv, w_qkv)

    chunk = width
    steps = ff // chunk
    const = lambda *dims: pl.BlockSpec(dims, lambda s, c: (0,) * len(dims))
    if placed:
        back_half = (2, 2, 4, ff // 16, width // 2)
        rest_half = (2, 2, 4, 5 * (width // 16), width // 2)
        back_spec = pl.BlockSpec((2, 2, 1, ff // 16, width // 2), lambda s, c: (0, 0, s ^ c[0], 0, 0))
        grad_specs = [back_spec, back_spec, const(*rest_half), const(*rest_half)]
        grad_shapes = [shape(back_half, bf16)] * 2 + [shape(rest_half, bf16)] * 2
    else:
        grad_specs = [
            pl.BlockSpec((chunk, width), lambda s, c: (s, 0)),
            pl.BlockSpec((width, chunk), lambda s, c: (0, s)),
            const(width, width),
        ]
        grad_shapes = [
            shape((ff, width), bf16), shape((width, ff), bf16), shape((width, width), bf16),
        ]
    output, d_hidden, d_context, gain_two, bias_two, *grads = pl.pallas_call(
        functools.partial(middle_kernel, len(grad_specs)),
        grid_spec=pltpu.PrefetchScalarGridSpec(
            num_scalar_prefetch=1,
            grid=(steps,),
            in_specs=[
                const(rows, width), const(rows, width), const(rows, width), const(width, width),
                const(1, width), const(1, width),
                pl.BlockSpec((width, chunk), lambda s, c: (0, s)),
                pl.BlockSpec((chunk, width), lambda s, c: (s, 0)),
            ],
            out_specs=[
                const(rows, width), const(rows, width), const(rows, width),
                const(1, width), const(1, width), *grad_specs,
            ],
            scratch_shapes=[
                pltpu.VMEM((rows, width), f32), pltpu.VMEM((rows, width), bf16),
                pltpu.VMEM((width, rows), bf16), pltpu.VMEM((rows, width), f32),
                pltpu.VMEM((rows, width), f32), pltpu.VMEM((rows, chunk), bf16),
                pltpu.VMEM((rows, chunk), bf16), pltpu.VMEM((chunk, width), bf16),
            ],
        ),
        out_shape=[
            shape((rows, width), bf16), shape((rows, width), f32), shape((rows, width), bf16),
            shape((1, width), f32), shape((1, width), f32), *grad_shapes,
        ],
        compiler_params=pltpu.CompilerParams(vmem_limit_bytes=ROOM[2] * 1024 * 1024),
        cost_estimate=COST,
        name="middle",
    )(coords, tok, context, grad_out, w_out, gain2, bias2, w_in, w_back)

    share = width // shards
    parts_in = (query, d_context, own_kv, own_kv, slot_kv, slot_kv)

    def attend_back(parts, live, early):
        column = lambda n, j: pl.BlockSpec((n, QW), lambda i: (0, j))
        whole = lambda s: pl.BlockSpec(s.shape, lambda i: (0,) * len(s.shape))
        specs, operands, outs, held = [], [], [], []
        for part in parts:
            specs += [column(rows, part), column(rows, part)]
            specs += [column(rows, part), column(rows, part + quads)]
            specs += [column(count * BLK, part), column(count * BLK, part + quads)]
            operands += [query, d_context, own_kv, own_kv, slot_kv, slot_kv]
            outs += [
                shape((rows, QW), bf16), shape((rows, 2 * QW), bf16),
                shape((count * BLK, 2 * QW), bf16),
            ]
        scratch = [
            pltpu.VMEM((2 * len(parts), rows + 2 * BLK, QW), bf16),
            pltpu.VMEM((2 * len(parts), rows + 2 * BLK, QW), f32),
            pltpu.VMEM((2 * len(parts), 2 * BLK, QW), f32),
        ]
        kernel = functools.partial(first_backward_kernel, parts)
        if early is not None:
            held = [w_qkv, own_hat, slot_hat, *early]
            kernel = functools.partial(last_backward_kernel, parts, len(early) // 3)
            outs += [
                shape((rows, width), f32), shape((count * BLK, width), bf16),
                shape((1, width), f32), shape((1, width), f32),
            ]
            scratch += [pltpu.VMEM(v.shape, v.dtype) for v in held]
            scratch += [pltpu.SemaphoreType.DMA((len(held),))]
        return list(
            pl.pallas_call(
                kernel,
                grid=(1,),
                out_shape=outs,
                in_specs=[smem(), whole(lse)] + [anym()] * len(held) + specs,
                out_specs=[whole(o) for o in outs],
                scratch_shapes=scratch,
                compiler_params=pltpu.CompilerParams(
                    vmem_limit_bytes=ROOM[3 if early is None else 4] * 1024 * 1024
                ),
                cost_estimate=COST,
                name="attend_backward",
            )(live, lse, *held, *operands)
        )

    first = attend_back((0,), live, None)
    if placed:
        keep_a, send_a, keep_b, send_b = grads
        got_a, got_b = hop(send_a, CORE), hop(send_b, CORE)
        got_a, got_b, *first = tie(got_a, got_b, *first)
        third = 3 * share
        pick = lambda v, low, high: v[:, :, :, low:high]
        total = lambda keep, got, low, high: plus(pick(keep, low, high), pick(got, low, high))
        in_z = lambda v: v.reshape(v.shape[:-3] + (2, 2) + v.shape[-2:])
        sum_y = in_z(total(keep_a, got_a, 0, third))
        sum_z = in_z(total(keep_b, got_b, 0, third))
        sum_x = in_z(
            jnp.concatenate(
                [
                    total(keep_a, got_a, third, 4 * share),
                    total(keep_b, got_b, third, 5 * share),
                ],
                3,
            )
        )
        out_y, mine_y = sum_y[1], sum_y[0]
        out_z, mine_z = sum_z[:, :, :, 1], sum_z[:, :, :, 0]
        out_x, mine_x = sum_x[:, 1], sum_x[:, 0]
        out_y, mine_y, out_z, mine_z, out_x, mine_x, live, *first = tie(
            out_y, mine_y, out_z, mine_z, out_x, mine_x, live, *first
        )
        got_y, got_z, got_x = over_y(out_y), hop(out_z, NEAR), hop(out_x, ACROSS)
    rest = attend_back((1, 2), live, first)
    d_parts = first + rest[:6]
    d_own_norm, d_slot_norm, gain_one, bias_one = rest[6:]

    def qkv_grads(d_parts):
        if placed:
            shapes = [shape((2, 2, 4, 3 * share + 16, width // 2), bf16)] * 2
        else:
            shapes = [shape((width, 3 * width), bf16)]
        return call(
            functools.partial(qkv_grad_kernel, len(shapes)),
            shapes,
            [smem()] + [vmem()] * (8 + 3 * quads),
            [pltpu.VMEM((width, width), bf16), pltpu.VMEM((count * BLK, width), bf16)],
            "qkv_grads",
            room=ROOM[5],
        )(
            coords, gain_one, bias_one, gain_two, bias_two, gain1, bias1, own_norm, slot_hat, *d_parts
        )

    def token_grads(d_norm1):
        normed_one, inv_one = norm_stats(tok.astype(f32))
        grad_hat = d_norm1 * ln1_gain
        d_first = inv_one * (
            grad_hat
            - jnp.mean(grad_hat, -1, keepdims=True)
            - normed_one * jnp.mean(grad_hat * normed_one, -1, keepdims=True)
        )
        return (d_hidden + d_first).astype(bf16)

    if placed:
        d_slot_norm = d_slot_norm.reshape(count, BLK, width)
        sib_codes = hop(codes, CORE)
        sib_norm = hop(d_slot_norm, CORE)
        got_y, got_z, got_x, d_slot_norm, *d_parts = tie(got_y, got_z, got_x, d_slot_norm, *d_parts)
        sum_y, sum_z, sum_x = plus(mine_y, got_y), plus(mine_z, got_z), plus(mine_x, got_x)
        out_y, mine_y = sum_y[:, :, 1], sum_y[:, :, 0]
        out_z, mine_z = sum_z[:, 1], sum_z[:, 0]
        out_x, mine_x = sum_x[1], sum_x[0]
        out_y, mine_y, out_z, mine_z, out_x, mine_x, *d_parts = tie(
            out_y, mine_y, out_z, mine_z, out_x, mine_x, *d_parts
        )
        got_y, got_z, got_x = hop(out_y, NEAR), hop(out_z, ACROSS), over_y(out_x)
        keep_c, send_c = qkv_grads(d_parts)
        keep_c, send_c, sib_norm, got_y, got_z, got_x = tie(
            keep_c, send_c, sib_norm, got_y, got_z, got_x
        )
        sum_y, sum_z, sum_x = plus(mine_y, got_y), plus(mine_z, got_z), plus(mine_x, got_x)
        out_y, mine_y = sum_y[1], sum_y[0]
        out_z, mine_z = sum_z[1], sum_z[0]
        out_x, mine_x = sum_x[:, 1], sum_x[:, 0]
        got_y, got_z, got_x = hop(out_y, ACROSS), over_y(out_z), hop(out_x, NEAR)
        mine_y, mine_z, mine_x, sib_norm = tie(mine_y, mine_z, mine_x, sib_norm)
        got_c = hop(send_c, CORE)
        piece_shape = shape((per_dev, BLK, width), bf16)
        sums = call(
            scatter_kernel,
            [piece_shape] * 8,
            [smem(), smem(), vmem(), vmem()],
            [pltpu.VMEM((8 * per_dev, BLK, width), f32)],
            "scatter_slots",
            room=ROOM[6],
        )(codes, sib_codes, d_slot_norm, sib_norm)
        below, below_x, own, beside, above, above_x, far, far_x = [
            p.reshape(rows, width) for p in sums
        ]
        from_above_x, from_below_x = hop(below_x, DOWN), hop(above_x, UP)
        in_far = hop(far_x, FAR_OUT)
        mine_y, mine_z, mine_x, got_y, got_z, got_x = after(
            own, mine_y, mine_z, mine_x, got_y, got_z, got_x
        )
        sum_y, sum_z, sum_x = plus(mine_y, got_y), plus(mine_z, got_z), plus(mine_x, got_x)
        sum_ab = jnp.concatenate([sum_y, sum_x[:, :share], sum_z, sum_x[:, share:]], 1)
        out_ab, mine_ab = sum_ab[1], sum_ab[0]
        got_ab = hop(out_ab, FAR)
        keep_c, got_c = after(mine_ab, keep_c, got_c)
        out_c, mine_c = split(keep_c, got_c)
        got_c = over_y(out_c)
        in_far, from_above_x, from_below_x = after(mine_c, in_far, from_above_x, from_below_x)
        far = plus(far, in_far)
        beside = plus(beside, from_above_x, from_below_x)
        from_above2, from_below2 = hop(far, DOWN_EARLY), hop(far, UP_EARLY)
        from_beside = hop(beside, ACROSS)
        mine_ab, got_ab = after(beside, mine_ab, got_ab)
        mine_ab = plus(mine_ab, got_ab)
        other_ab = over_y(mine_ab)
        mine_c, got_c = after(mine_ab, mine_c, got_c)
        out_c, mine_c = split(mine_c, got_c)
        got_c = hop(out_c, ACROSS)
        from_above2, from_below2 = after(mine_c, from_above2, from_below2)
        below, above = plus(below, from_above2), plus(above, from_below2)
        from_above, from_below = hop(below, DOWN), hop(above, UP)
        mine_c, got_c = after(above, mine_c, got_c)
        sum_c = by_pairs(plus(mine_c, got_c))
        out_c, mine_c = sum_c[:, 1], sum_c[:, 0]
        got_c = hop(out_c, NEAR)
        own, from_beside = after(mine_c, own, from_beside)
        own = own.astype(f32) + from_beside.astype(f32)
        mine_c, got_c = after(own, mine_c, got_c)
        mine_c = plus(mine_c, got_c)
        got_c = hop(mine_c[1], FAR)
        half = width // 2
        back_rows = ff // 16
        halves_ab = both_halves(*after(mine_c, mine_ab, other_ab))
        back_grad = halves_ab[:, :back_rows].reshape(2, 2, back_rows // 2, half)
        back_grad = back_grad.transpose(0, 2, 1, 3).reshape(back_rows, width)
        rest = halves_ab[:, back_rows:].reshape(2, 5, share, half)
        in_grad = rest[:, :4].reshape(8, share, half).transpose(1, 0, 2).reshape(share, ff)
        out_proj_grad = rest[:, 4].transpose(1, 0, 2).reshape(share, width)
        mine_c, got_c = after(back_grad, mine_c, got_c)
        mine_c = plus(mine_c[0], got_c)
        other_c = over_y(mine_c)
        from_above, from_below = after(mine_c, from_above, from_below)
        d_norm1 = d_own_norm + own + from_above.astype(f32) + from_below.astype(f32)
        tokens_grad = token_grads(d_norm1)
        mine_c, other_c = after(tokens_grad, mine_c, other_c)
        halves_c = both_halves(mine_c, other_c)
        qkv_grad = halves_c[:, : 3 * share].reshape(6, share, half).transpose(1, 0, 2)
        qkv_grad = qkv_grad.reshape(share, 3 * width)
        vectors = halves_c[0, 3 * share : 3 * share + 8].reshape(4, width)
        vectors = lax.dynamic_slice_in_dim(vectors, me * share, share, 1)
    else:
        spread_grads = jnp.zeros((shards * per_dev, BLK, width), f32)
        spread_grads = spread_grads.at[slots].add(
            d_slot_norm.reshape(count, BLK, width).astype(f32)
        )
        others = lax.psum_scatter(
            spread_grads.astype(bf16).reshape(shards * rows, width),
            "seq", scatter_dimension=0, tiled=True,
        )
        tokens_grad = token_grads(d_own_norm + others.astype(f32))

        def reduce(part):
            mine = lax.psum_scatter(part, "seq", scatter_dimension=0, tiled=True)
            return lax.psum(mine, "grp").astype(f32)

        back_grad, in_grad, out_proj_grad = [reduce(g) for g in grads]
        qkv_grad = reduce(qkv_grads(d_parts)[0])
        vectors = jnp.concatenate([gain_one, bias_one, gain_two, bias_two])
        vectors = lax.psum(vectors, ("seq", "grp"))
        vectors = lax.dynamic_slice_in_dim(vectors, me * share, share, 1)
    return (
        output[None],
        tokens_grad[None],
        qkv_grad,
        out_proj_grad,
        in_grad,
        back_grad,
        vectors[0],
        vectors[1],
        vectors[2],
        vectors[3],
    )


def solution(mesh):
    in_specs = (
        P("grp", "seq", None),
        P(),
        P(),
        P(),
        P(),
        P(),
        P(),
        P(),
        P(),
        P("grp", None),
        P("grp", None),
        P("grp", None, None),
        P("grp", "seq", None),
        P("grp", "seq", None),
    )
    out_specs = (
        P("grp", "seq", None),
        P("grp", "seq", None),
        P("seq", None),
        P("seq", None),
        P("seq", None),
        P("seq", None),
        P("seq"),
        P("seq"),
        P("seq"),
        P("seq"),
    )
    return jax.shard_map(body, mesh=mesh, in_specs=in_specs, out_specs=out_specs, check_vma=False)
```
